32 devices in a mesh: dp: 4 (over y, x), sp: 8 (over z, core).
Axes of the slice: x: 2, y: 2, z: 4, core: 2. Of those that a mesh axis runs over, the one named last changes fastest.
Arguments:
- q_pre: bfloat16 [4, 256, 8192], P('dp', 'sp'), may hold values from -6 to 6
- attn_out: bfloat16 [4, 256, 8192], P('dp', 'sp'), may hold values from -6 to 6
- d_attn: bfloat16 [4, 256, 8192], P('dp', 'sp'), may hold values from -24 to 24
- k_pre: bfloat16 [4, 1024, 512], P('dp', 'sp'), may hold values from -6 to 6
- values: bfloat16 [4, 1024, 512], P('dp', 'sp'), may hold values from -6 to 6
- q_gain: float32 [128], replicated, may hold values from 0.5 to 1.5
- k_gain: float32 [128], replicated, may hold values from 0.5 to 1.5
- offsets: int32 [4], P('dp'), may hold values from 1 to 768, 2304 in all
- moe_in: bfloat16 [4, 256, 4096], P('dp', 'sp'), may hold values from -2.59375 to 2.59375
- router: bfloat16 [4096, 128], replicated, may hold values from -0.0074768066 to 0.0074768066
- expert_ids: int32 [4, 256, 8], P('dp', 'sp'), may hold values from 0 to 127, all different within a row; in each aligned block of 32 rows (0 to 31, 32 to 63, ..., all dimensions but the last counted through in order) at most 3 rows name the same one
- d_moe: bfloat16 [4, 256, 4096], P('dp', 'sp'), may hold values from -6 to 6
- expert_out: bfloat16 [4, 128, 8, 3, 4096], P('dp', 'sp'), may hold values from -0.3125 to 0.3125
Outputs:
- dq_pre: bfloat16 [4, 256, 8192], P('dp', 'sp')
- dk_pre: bfloat16 [4, 1024, 512], P('dp', 'sp')
- dv_out: bfloat16 [4, 1024, 512], P('dp', 'sp')
- batch_grad: bfloat16 [4, 128, 8, 3, 4096], P('dp', 'sp')
- router_grad: float32 [4096, 128], P('sp')
The draws below stay inside these ranges and needn't reach their ends.
Inputs may be any that keep to these rules, and one draw needn't show every extreme that they name: `expert_ids`: within the rows of one device no expert is named more than 3 times; some expert is named exactly 3 times by the rows of some device. `offsets`: some group has its stretch at the end, offset 1024 - 256.
All inputs are finite; a program needn't handle non-finite values.
Results may differ from the reference program's by a relative error of at most 0.0075.
Values may be sent and summed in bfloat16 or wider, within the bound.
No kernel may reach another device: no remote copies, remote signals or barrier semaphores. Data moves between devices by JAX's collectives and lax.ppermute only.
A program may use at most 128 MiB of HBM per device.

```python
import math
import jax
import jax.numpy as jnp
import numpy as np
from jax import lax

D = 4096
QH = 64
KVH = 4
HD = 128
EXPERTS = 128
TOPK = 8
CAP = 3
TOK_DEV = 32
STRETCH = 256
KEYS = 1024
N_DP = 4
N_SP = 8


def block_levels(key, shape, cuts, least, top_value):
    level = 1.0
    for position, parts in cuts:
        draws = jax.random.uniform(jax.random.fold_in(jax.random.fold_in(key, 6), position), (parts,), jnp.float32, least / len(cuts), top_value / len(cuts))
        level = level * jnp.repeat(jnp.exp(draws), shape[position] // parts).reshape((-1,) + (1,) * (len(shape) - 1 - position))
    return level


def length_profile(amount, total, limit, slope):
    weights = [(1 << 20) // math.isqrt(standing ** slope) + 1 for standing in range(2, amount + 1)]
    spare, given = total - limit - (amount - 1), [1] * (amount - 1)
    while spare > 0:
        candidates = [i for i in range(amount - 1) if given[i] < limit]
        pool, left = sum([weights[i] for i in candidates]), spare
        for i in candidates:
            more = min(limit - given[i], max(1, left * weights[i] // pool), spare)
            given[i] = given[i] + more
            spare = spare - more
    return np.array([limit] + given)


def uneven(key, number_of, total, limit, slope):
    if number_of == 2:
        one = jax.random.randint(key, (), max(1, total - limit), min(limit, total - 1) + 1)
        return jnp.stack([one, total - one])
    lengths = jnp.asarray(length_profile(number_of, total, limit, slope), jnp.int32)
    twos = (number_of - 1) // 2
    donor, receiver = lengths[1:1 + 2 * twos:2], lengths[2:2 + 2 * twos:2]
    slack = jnp.minimum(donor - 1, limit - receiver)
    moved = jax.random.randint(jax.random.fold_in(key, 1), (twos,), 0, 1 << 20) % (slack + 1)
    lengths = lengths.at[1:1 + 2 * twos:2].set(donor - moved).at[2:2 + 2 * twos:2].set(receiver + moved)
    return lengths[jax.random.permutation(jax.random.fold_in(key, 2), number_of)]


def deal_out(rng, own, number, rows, count, top, limit, lean):
    order = jax.random.permutation(rng, count)
    crowded, ordinary = shares(count, rows * top, limit, lean, True), shares(count, rows * top, limit, lean, False)
    places = jnp.arange(count)

    def named(tallies, offset_by):
        used = int((tallies > 0).sum())
        fixed = max(1, used // 4)
        shifted = fixed + (places - fixed + offset_by * (used - fixed)) % max(1, count - fixed)
        return jnp.zeros((count,), jnp.int32).at[order[jnp.where(places < fixed, places, shifted)]].set(jnp.asarray(tallies, jnp.int32))

    tallies = jnp.where(number % 4 == 0, named(crowded, number // 4), named(ordinary, number - number // 4 - 1))
    mixed = jax.random.permutation(jax.random.fold_in(own, 3), count)
    giver, receiver = mixed[0:count // 2 * 2:2], mixed[1:count // 2 * 2:2]
    room = jnp.minimum(tallies[giver] - 1, limit - tallies[receiver]) // 2
    room = jnp.where((giver == order[0]) | (receiver == order[0]) | (tallies[receiver] == 0), 0, jnp.maximum(room, 0))
    shifted = jax.random.randint(jax.random.fold_in(own, 4), (count // 2,), 0, 1 << 20) % (room + 1)
    tallies = tallies.at[giver].add(-shifted).at[receiver].add(shifted)
    members = jnp.searchsorted(jnp.cumsum(tallies), jnp.arange(rows * top), side="right").astype(jnp.int32)
    listing = members.reshape(top, rows).T
    listing = listing[jax.random.permutation(jax.random.fold_in(own, 1), rows)]
    offset_by = jax.random.randint(jax.random.fold_in(own, 2), (rows, 1), 0, top)
    return jnp.take_along_axis(listing, (jnp.arange(top)[None, :] + offset_by) % top, axis=1)


def shares(number_of, total, most, slope, full):
    loads = [(1 << 20) // math.isqrt(rank ** slope) + 1 for rank in range(1, number_of + 1)]
    largest = most if full else min(most, max(-(-total // number_of), total * loads[0] // sum(loads)))
    least = 1 if total - largest >= number_of - 1 else 0
    counts, rest = [largest] + [least] * (number_of - 1), total - largest - least * (number_of - 1)
    while rest > 0:
        candidates = [i for i in range(1, number_of) if counts[i] < largest] or [i for i in range(1, number_of) if counts[i] < most]
        whole, left = sum([loads[i] for i in candidates]), rest
        for i in candidates:
            extra = min(most - counts[i], max(1, left * loads[i] // whole), rest)
            counts[i] = counts[i] + extra
            rest = rest - extra
    return np.array(counts)


def gaussian(rng, shape, deviation, most, cuts=(), kind=jnp.bfloat16):
    drawn = jax.random.normal(rng, shape, jnp.float32) * deviation
    if len(cuts) > 0:
        drawn = block_levels(rng, shape, cuts, -0.22, 0.18) * drawn
    return jnp.clip(drawn, min=-most, max=most).astype(kind)


def setup_inputs(seed: int = 0) -> dict:
    streams_of = jax.random.split(jax.random.key(seed), 14)
    q_pre = gaussian(streams_of[0], (N_DP, STRETCH, QH * HD), 1.0, 6.0, ((0, 4), (1, 8)))
    attn_out = gaussian(streams_of[1], (N_DP, STRETCH, QH * HD), 1.0, 6.0, ((0, 4), (1, 8)))
    d_attn = gaussian(streams_of[2], (N_DP, STRETCH, QH * HD), 4.0, 24.0, ((0, 4), (1, 8)))
    k_pre = gaussian(streams_of[3], (N_DP, KEYS, KVH * HD), 1.0, 6.0, ((0, 4), (1, 8)))
    values = gaussian(streams_of[4], (N_DP, KEYS, KVH * HD), 1.0, 6.0, ((0, 4), (1, 8)))
    q_gain = jnp.clip(1.0 + 0.1 * jax.random.normal(streams_of[5], (HD,), jnp.float32), 0.5, 1.5)
    k_gain = jnp.clip(1.0 + 0.1 * jax.random.normal(streams_of[6], (HD,), jnp.float32), 0.5, 1.5)
    offsets = uneven(streams_of[7], N_DP, N_DP * (KEYS - STRETCH) * 3 // 4, KEYS - STRETCH, 1).astype(jnp.int32)
    moe_in = gaussian(streams_of[8], (N_DP, STRETCH, D), 1.0, 2.59375, ((0, 4), (1, 8)))
    router = jnp.clip(jax.random.uniform(streams_of[9], (D, EXPERTS), jnp.float32, -0.0074768066, 0.0074768066), -0.0074768066, 0.0074768066).astype(jnp.bfloat16)
    expert_ids_keys = jax.random.split(jax.random.fold_in(streams_of[10], 1), N_DP * STRETCH // TOK_DEV)
    expert_ids_turns = jax.random.permutation(jax.random.fold_in(streams_of[10], 3), N_DP * STRETCH // TOK_DEV)
    expert_ids = jax.vmap(lambda own, number: deal_out(jax.random.fold_in(streams_of[10], 2), own, number, TOK_DEV, EXPERTS, TOPK, CAP, 2))(expert_ids_keys, expert_ids_turns).reshape((N_DP, STRETCH, TOPK))
    d_moe = gaussian(streams_of[11], (N_DP, STRETCH, D), 1.0, 6.0, ((0, 4), (1, 8)))
    expert_out = gaussian(streams_of[12], (N_DP, EXPERTS, N_SP, CAP, D), 0.05, 0.3125, ((0, 4), (1, 8)))
    return {"q_pre": q_pre, "attn_out": attn_out, "d_attn": d_attn, "k_pre": k_pre, "values": values, "q_gain": q_gain, "k_gain": k_gain, "offsets": offsets, "moe_in": moe_in, "router": router, "expert_ids": expert_ids, "d_moe": d_moe, "expert_out": expert_out}


norm_eps = 1e-06

def normed(inputs, gain):
    inverse = lax.rsqrt(lax.optimization_barrier(jnp.mean(inputs * inputs, axis=-1, keepdims=True)) + norm_eps)
    unit_vals = inputs * inverse
    return (unit_vals, inverse, unit_vals * gain)

def norm_back(grad_hat, unit_vals, inverse, gain):
    grad_unit = grad_hat * gain
    return inverse * (grad_unit - unit_vals * lax.optimization_barrier(jnp.mean(grad_unit * unit_vals, axis=-1, keepdims=True)))

def attention_group(q_group, out_group, dout_group, kpre_group, value_group, offset, q_gain, k_gain):
    score_scale = HD ** (-0.5)
    per_group = QH // KVH
    q_full = q_group.astype(jnp.float32).reshape(STRETCH, QH, HD)
    q_unit, q_inv, q_hat32 = normed(q_full, q_gain)
    q_hat = q_hat32.astype(jnp.bfloat16)
    k_full = kpre_group.astype(jnp.float32).reshape(KEYS, KVH, HD)
    k_unit, k_inv, k_hat32 = normed(k_full, k_gain)
    k_hat = k_hat32.astype(jnp.bfloat16)
    value_full = value_group.reshape(KEYS, KVH, HD)
    dout_full = dout_group.reshape(STRETCH, QH, HD)
    out_full = out_group.reshape(STRETCH, QH, HD)
    row_delta = lax.optimization_barrier(jnp.sum(dout_full.astype(jnp.float32) * out_full.astype(jnp.float32), axis=-1))
    visible = jnp.arange(KEYS, dtype=jnp.int32)[None, :] <= offset + jnp.arange(STRETCH, dtype=jnp.int32)[:, None]
    q_heads = jnp.transpose(q_hat.reshape(STRETCH, KVH, per_group, HD), (1, 2, 0, 3))
    dout_heads = jnp.transpose(dout_full.reshape(STRETCH, KVH, per_group, HD), (1, 2, 0, 3))
    delta_heads = jnp.transpose(row_delta.reshape(STRETCH, KVH, per_group), (1, 2, 0))
    key_heads = jnp.transpose(k_hat, (1, 0, 2))
    value_heads = jnp.transpose(value_full, (1, 0, 2))

    def one_group(pieces):
        q_set, dout_set, delta_set, key_one, value_one = pieces

        def one_head(totals, head_pieces):
            query_one, dout_one, delta_one = head_pieces
            scores = jnp.dot(query_one, key_one.T, preferred_element_type=jnp.float32) * score_scale
            lse = jnp.log(lax.optimization_barrier(jnp.sum(jnp.where(visible, jnp.exp(scores), 0.0), axis=-1)))
            probs = jnp.where(visible, jnp.exp(scores - lse[:, None]), 0.0)
            probs_b = probs.astype(jnp.bfloat16)
            dv_term = jnp.dot(probs_b.T, dout_one, preferred_element_type=jnp.float32)
            dprobs = jnp.dot(dout_one, value_one.T, preferred_element_type=jnp.float32)
            dscores = (probs * (dprobs - delta_one[:, None]) * score_scale).astype(jnp.bfloat16)
            dq_one = jnp.dot(dscores, key_one, preferred_element_type=jnp.float32)
            dk_term = jnp.dot(dscores.T, query_one, preferred_element_type=jnp.float32)
            return ((totals[0] + dk_term, totals[1] + dv_term), dq_one)
        zeros_kv = jnp.zeros((KEYS, HD), jnp.float32)
        (dk_sum, dv_sum), dq_set = lax.scan(one_head, (zeros_kv, zeros_kv), (q_set, dout_set, delta_set))
        return (dq_set, dk_sum, dv_sum)
    dq_sets, dk_hat, dv_sum = lax.map(one_group, (q_heads, dout_heads, delta_heads, key_heads, value_heads))
    dq_hat = jnp.transpose(dq_sets, (2, 0, 1, 3)).reshape(STRETCH, QH, HD)
    dq_pre = norm_back(dq_hat, q_unit, q_inv, q_gain).astype(jnp.bfloat16).reshape(STRETCH, QH * HD)
    dk_hat = jnp.transpose(dk_hat, (1, 0, 2))
    dk_pre = norm_back(dk_hat, k_unit, k_inv, k_gain).astype(jnp.bfloat16).reshape(KEYS, KVH * HD)
    dv_out = jnp.transpose(dv_sum, (1, 0, 2)).astype(jnp.bfloat16).reshape(KEYS, KVH * HD)
    return (dq_pre, dk_pre, dv_out)

def moe_group(input_group, router, id_group, dmoe_group, eout_group):
    logits_all = jnp.dot(input_group, router, preferred_element_type=jnp.float32)
    logits = jnp.take_along_axis(logits_all, id_group, axis=1)
    weights = jnp.exp(logits)
    gate_probs = weights / lax.optimization_barrier(jnp.sum(weights, axis=-1, keepdims=True))
    gate_b = gate_probs.astype(jnp.bfloat16)
    pair_ids = id_group.reshape(N_SP, TOK_DEV * TOPK)
    onehot = (pair_ids[:, :, None] == jnp.arange(EXPERTS, dtype=jnp.int32)[None, None, :]).astype(jnp.int32)
    before = jnp.cumsum(onehot, axis=1) - onehot
    slot_index = lax.optimization_barrier(jnp.sum(before * onehot, axis=-1)).astype(jnp.int32).reshape(STRETCH, TOPK)
    source = jnp.broadcast_to((jnp.arange(STRETCH, dtype=jnp.int32) // TOK_DEV)[:, None], (STRETCH, TOPK))
    grad_rows = (gate_b.astype(jnp.float32)[:, :, None] * dmoe_group.astype(jnp.float32)[:, None, :]).astype(jnp.bfloat16)
    batch_grad = jnp.zeros((EXPERTS, N_SP, CAP, D), jnp.bfloat16).at[id_group, source, slot_index].set(grad_rows)
    picked = eout_group[id_group, source, slot_index]
    dgate = lax.optimization_barrier(jnp.sum(picked.astype(jnp.float32) * dmoe_group.astype(jnp.float32)[:, None, :], axis=-1))
    dlogit = gate_probs * (dgate - lax.optimization_barrier(jnp.sum(gate_probs * dgate, axis=-1, keepdims=True)))
    token_rows = jnp.broadcast_to(jnp.arange(STRETCH, dtype=jnp.int32)[:, None], (STRETCH, TOPK))
    dense_grad = jnp.zeros((STRETCH, EXPERTS), jnp.float32).at[token_rows, id_group].add(dlogit)
    partial_value = jnp.dot(input_group.astype(jnp.float32).T, dense_grad, precision=lax.Precision.HIGHEST)
    return (batch_grad, partial_value)

def reference(q_pre, attn_out, d_attn, k_pre, values, q_gain, k_gain, offsets, moe_in, router, expert_ids, d_moe, expert_out):
    dq_list, dk_list, dv_list, batch_list = ([], [], [], [])
    router_grad = jnp.zeros((D, EXPERTS), jnp.float32)
    for group in range(N_DP):
        dq_one, dk_one, dv_one = attention_group(q_pre[group], attn_out[group], d_attn[group], k_pre[group], values[group], offsets[group], q_gain, k_gain)
        batch_one, partial_value = moe_group(moe_in[group], router, expert_ids[group], d_moe[group], expert_out[group])
        dq_list.append(dq_one)
        dk_list.append(dk_one)
        dv_list.append(dv_one)
        batch_list.append(batch_one)
        router_grad = router_grad + partial_value
    return (jnp.stack(dq_list), jnp.stack(dk_list), jnp.stack(dv_list), jnp.stack(batch_list), router_grad)
```

```python
import functools
import math

import jax
import jax.numpy as jnp
import numpy as np
from jax import lax
from jax.experimental import pallas as pl
from jax.experimental.pallas import tpu as pltpu
from jax.sharding import PartitionSpec as P

norm_eps = 1e-06
f32 = jnp.float32
bf16 = jnp.bfloat16
vmem_limit = 56 * 1024 * 1024


def dot_nt(a, b):
    return lax.dot_general(a, b, (((1,), (1,)), ((), ())), preferred_element_type=f32)


def dot_nn(a, b):
    return lax.dot_general(a, b, (((1,), (0,)), ((), ())), preferred_element_type=f32)


def dot_tn(a, b):
    return lax.dot_general(a, b, (((0,), (0,)), ((), ())), preferred_element_type=f32)


def whole(shape):
    return pl.BlockSpec(shape, lambda *_: (0,) * len(shape))


def keys_kernel(k_ref, v_ref, gain_ref, kv_ref):
    hd = gain_ref.shape[1]
    gain = gain_ref[...]
    for g in range(k_ref.shape[1] // hd):
        k = k_ref[:, g * hd : (g + 1) * hd].astype(f32)
        inv = lax.rsqrt(jnp.mean(k * k, axis=-1, keepdims=True) + norm_eps)
        kv_ref[:, 2 * g * hd : (2 * g + 1) * hd] = ((k * inv) * gain).astype(bf16)
        kv_ref[:, (2 * g + 1) * hd : (2 * g + 2) * hd] = v_ref[:, g * hd : (g + 1) * hd]


def pack_keys(k_pre, values, k_gain):
    rows, width = k_pre.shape
    return pl.pallas_call(
        keys_kernel,
        out_shape=jax.ShapeDtypeStruct((rows, 2 * width), bf16),
        name="pack_keys",
    )(k_pre, values, k_gain)


def gates_kernel(moe_ref, router_ref, ids_ref, dmoe_ref, pack_ref, info_ref):
    tok, width = moe_ref.shape
    experts = router_ref.shape[1]
    logits = dot_nn(moe_ref[...], router_ref[...])
    lane = lax.broadcasted_iota(jnp.int32, (tok, experts), 1)
    chosen = lane == ids_ref[:, 0:1]
    for k in range(1, ids_ref.shape[1]):
        chosen = jnp.logical_or(chosen, lane == ids_ref[:, k : k + 1])
    weights = jnp.where(chosen, jnp.exp(logits), 0.0)
    probs = weights / jnp.sum(weights, axis=-1, keepdims=True)
    high = probs.astype(bf16)
    low = (probs - high.astype(f32)).astype(bf16)
    coded = jnp.where(chosen, high.astype(f32), -1.0).astype(bf16)
    pack_ref[:, :width] = dmoe_ref[...]
    pack_ref[:, width:] = coded
    info_ref[:, :experts] = coded
    info_ref[:, experts:] = low


def gates(moe_in, router, ids, d_moe):
    tok, width = moe_in.shape
    experts = router.shape[1]
    return pl.pallas_call(
        gates_kernel,
        out_shape=(
            jax.ShapeDtypeStruct((tok, width + experts), bf16),
            jax.ShapeDtypeStruct((tok, 2 * experts), bf16),
        ),
        compiler_params=pltpu.CompilerParams(vmem_limit_bytes=vmem_limit),
        name="gates",
    )(moe_in, router, ids, d_moe)


def attend_kernel(blocks, meta_ref, q_ref, o_ref, do_ref, gain_ref, *refs):
    kv_refs = refs[:blocks]
    dq_ref = refs[blocks]
    part_refs = refs[blocks + 1 : 2 * blocks + 1]
    tok = q_ref.shape[0]
    hd = gain_ref.shape[1]
    heads = q_ref.shape[1] // hd
    kb = kv_refs[0].shape[0]
    keys = kb * blocks
    scale = hd ** (-0.5)
    offset = meta_ref[0]
    gain = gain_ref[...]
    key = jnp.concatenate([r[:, :hd] for r in kv_refs], axis=0)
    val = jnp.concatenate([r[:, hd:] for r in kv_refs], axis=0)
    pos = jnp.concatenate(
        [
            meta_ref[1 + b] * kb + lax.broadcasted_iota(jnp.int32, (kb, 1), 0)
            for b in range(blocks)
        ],
        axis=0,
    )
    step_heads = min(heads, max(128 // tok, heads * 1024 // keys))
    rows = step_heads * tok
    limit = offset + lax.rem(lax.broadcasted_iota(jnp.int32, (1, rows), 1), tok)
    visible = pos <= limit
    dk = dv = None
    for h0 in range(0, heads, step_heads):

        def stack(ref):
            return jnp.concatenate(
                [ref[:, h * hd : (h + 1) * hd] for h in range(h0, h0 + step_heads)], axis=0
            )

        q = stack(q_ref).astype(f32)
        do = stack(do_ref)
        prod = do.astype(f32) * stack(o_ref).astype(f32)
        delta = jnp.sum(prod.T, axis=0, keepdims=True)
        inv = lax.rsqrt(jnp.mean(q * q, axis=-1, keepdims=True) + norm_eps)
        unit = q * inv
        q_hat = (unit * gain).astype(bf16)
        scores = dot_nt(key, q_hat)
        ex = jnp.where(visible, jnp.exp2(scores * (scale * math.log2(math.e))), 0.0)
        probs = ex * (1.0 / jnp.sum(ex, axis=0, keepdims=True))
        dv_one = dot_nn(probs.astype(bf16), do)
        dprobs = dot_nt(val, do)
        ds = ((probs * scale) * (dprobs - delta)).astype(bf16)
        dk_one = dot_nn(ds, q_hat)
        dq = dot_tn(key, ds).T
        c = dq * gain
        dq_pre = (inv * (c - unit * jnp.mean(c * unit, axis=-1, keepdims=True))).astype(bf16)
        for i in range(step_heads):
            h = h0 + i
            dq_ref[:, h * hd : (h + 1) * hd] = dq_pre[i * tok : (i + 1) * tok, :]
        dk = dk_one if dk is None else dk + dk_one
        dv = dv_one if dv is None else dv + dv_one
    for b in range(blocks):
        part_refs[b][:, :hd] = dk[b * kb : (b + 1) * kb, :].astype(part_refs[b].dtype)
        part_refs[b][:, hd:] = dv[b * kb : (b + 1) * kb, :].astype(part_refs[b].dtype)


def attend(meta, q, o, do, gain, kv_blocks, part_types):
    tok, width = q.shape
    hd = gain.shape[1]
    kb, kv_width = kv_blocks[0].shape
    kv_heads = kv_width // (2 * hd)
    blocks = len(kv_blocks)
    step = width // kv_heads
    row_spec = pl.BlockSpec((tok, step), lambda g, m: (0, g))
    kv_spec = pl.BlockSpec((kb, 2 * hd), lambda g, m: (0, g))
    return pl.pallas_call(
        functools.partial(attend_kernel, blocks),
        grid_spec=pltpu.PrefetchScalarGridSpec(
            num_scalar_prefetch=1,
            grid=(kv_heads,),
            in_specs=[row_spec] * 3 + [whole((1, hd))] + [kv_spec] * blocks,
            out_specs=[row_spec] + [kv_spec] * blocks,
        ),
        out_shape=[jax.ShapeDtypeStruct((tok, width), bf16)]
        + [jax.ShapeDtypeStruct((kb, kv_width), t) for t in part_types],
        compiler_params=pltpu.CompilerParams(vmem_limit_bytes=vmem_limit),
        name="attend",
    )(meta, q, o, do, gain, *kv_blocks)


def finish_kernel(k_ref, gain_ref, *refs):
    dk_ref, dv_ref = refs[-2:]
    hd = gain_ref.shape[1]
    gain = gain_ref[...]
    total = refs[0][...].astype(f32)
    for r in refs[1:-2]:
        total = total + r[...].astype(f32)
    for g in range(k_ref.shape[1] // hd):
        k = k_ref[:, g * hd : (g + 1) * hd].astype(f32)
        inv = lax.rsqrt(jnp.mean(k * k, axis=-1, keepdims=True) + norm_eps)
        unit = k * inv
        c = total[:, 2 * g * hd : (2 * g + 1) * hd] * gain
        dk = inv * (c - unit * jnp.mean(c * unit, axis=-1, keepdims=True))
        dk_ref[:, g * hd : (g + 1) * hd] = dk.astype(bf16)
        dv_ref[:, g * hd : (g + 1) * hd] = total[
            :, (2 * g + 1) * hd : (2 * g + 2) * hd
        ].astype(bf16)


def finish_keys(k_pre, k_gain, parts):
    out = jax.ShapeDtypeStruct(k_pre.shape, bf16)
    return pl.pallas_call(finish_kernel, out_shape=(out, out), name="finish_keys")(
        k_pre, k_gain, *parts
    )


def earlier_same_block(rows, block):
    i = lax.broadcasted_iota(jnp.int32, (rows, rows), 0)
    j = lax.broadcasted_iota(jnp.int32, (rows, rows), 1)
    same = lax.div(i, block) == lax.div(j, block)
    return jnp.where(jnp.logical_and(same, j < i), 1.0, 0.0).astype(bf16)


def slots_kernel(
    blocks, sp, cap, meta_ref, table_ref, lanes_ref, *refs
):
    d_refs = refs[:blocks]
    g_refs = refs[blocks : 2 * blocks]
    eout_ref, batch_ref, terms_ref, dm, gated, hit_scr, acc = refs[2 * blocks :]
    tok = d_refs[0].shape[0]
    experts = g_refs[0].shape[1]
    rows = eout_ref.shape[0]
    tokens = tok * blocks
    step = pl.program_id(0)

    def pick():
        expert = meta_ref[0] + table_ref[:, 0:1]
        return lax.broadcasted_iota(jnp.int32, (rows, experts), 1) == expert

    @pl.when(step == 0)
    def _():
        coded = jnp.concatenate([r[...] for r in g_refs], axis=0)
        chosen = (coded >= 0).astype(bf16)
        rank = dot_nn(earlier_same_block(tokens, tok), chosen)
        sel = jnp.where(pick(), 1.0, 0.0).astype(bf16)
        gate = dot_nt(sel, coded)
        place = dot_nt(sel, rank.astype(bf16))
        lane_block = lax.div(lax.broadcasted_iota(jnp.int32, (1, tokens), 1), tok)
        source = jnp.zeros((1, tokens), jnp.int32)
        for b in range(blocks):
            source = jnp.where(lane_block == b, meta_ref[1 + b], source)
        hit = jnp.logical_and(
            jnp.logical_and(gate >= 0.0, place == table_ref[:, 1:2].astype(f32)),
            source == table_ref[:, 2:3],
        )
        gated[...] = jnp.where(hit, gate, 0.0).astype(bf16)
        hit_scr[...] = jnp.where(hit, 1.0, 0.0)
        acc[...] = jnp.zeros_like(acc)

    for b in range(blocks):
        dm[b * tok : (b + 1) * tok, :] = d_refs[b][...]
    d_all = dm[...]
    batch_ref[...] = dot_nn(gated[...], d_all).astype(bf16)
    acc[...] += dot_nt(eout_ref[...], d_all)

    @pl.when(step == pl.num_programs(0) - 1)
    def _():
        terms = jnp.sum(acc[...] * hit_scr[...], axis=-1, keepdims=True)
        placed = jnp.where(pick(), terms, 0.0)
        want = lax.broadcasted_iota(jnp.int32, (cap * sp, rows), 0)
        fold = jnp.where(want == lanes_ref[...], 1.0, 0.0)
        terms_ref[...] = lax.dot_general(
            fold,
            placed,
            (((1,), (0,)), ((), ())),
            precision=lax.Precision.HIGHEST,
            preferred_element_type=f32,
        )


def slots(meta, packs, eout, experts_here, cap, sp):
    rows, width = eout.shape
    tok, packed = packs[0].shape
    experts = packed - width
    blocks = len(packs)
    r = np.arange(rows)
    e, c, s = r // (cap * sp), (r // sp) % cap, r % sp
    table = jnp.asarray(np.stack([e, c, s], axis=1), jnp.int32)
    lanes = jnp.asarray((c * sp + s)[None, :], jnp.int32)
    col = min(width, 1024)
    d_spec = pl.BlockSpec((tok, col), lambda i, m: (0, i))
    g_spec = pl.BlockSpec((tok, experts), lambda i, m: (0, width // experts))
    e_spec = pl.BlockSpec((rows, col), lambda i, m: (0, i))
    return pl.pallas_call(
        functools.partial(slots_kernel, blocks, sp, cap),
        grid_spec=pltpu.PrefetchScalarGridSpec(
            num_scalar_prefetch=1,
            grid=(width // col,),
            in_specs=[whole((rows, 3)), whole((1, rows))]
            + [d_spec] * blocks
            + [g_spec] * blocks
            + [e_spec],
            out_specs=[e_spec, whole((cap * sp, experts))],
            scratch_shapes=[
                pltpu.VMEM((tok * blocks, col), bf16),
                pltpu.VMEM((rows, tok * blocks), bf16),
                pltpu.VMEM((rows, tok * blocks), f32),
                pltpu.VMEM((rows, tok * blocks), f32),
            ],
        ),
        out_shape=[
            jax.ShapeDtypeStruct((rows, width), bf16),
            jax.ShapeDtypeStruct((cap * sp, experts), f32),
        ],
        compiler_params=pltpu.CompilerParams(vmem_limit_bytes=vmem_limit),
        name="slots",
    )(meta, table, lanes, *packs, *packs, eout)


def router_kernel(tok, sp, cap, info_ref, terms_ref, moe_ref, out_ref):
    tokens = moe_ref.shape[0]
    experts = out_ref.shape[1]

    @pl.when(pl.program_id(0) == 0)
    def _():
        out_ref[...] = jnp.zeros_like(out_ref)

    high = info_ref[:, :experts]
    chosen = high >= 0
    prob = jnp.where(chosen, high.astype(f32) + info_ref[:, experts:].astype(f32), 0.0)
    rank = dot_nn(earlier_same_block(tokens, tok), chosen.astype(bf16))
    terms = jnp.sum(terms_ref[...], axis=0)
    pieces = []
    for s in range(sp):
        place = rank[s * tok : (s + 1) * tok, :]
        one = jnp.zeros((tok, experts), f32)
        for c in range(cap):
            one = jnp.where(place == c, terms[c * sp + s : c * sp + s + 1, :], one)
        pieces.append(one)
    dgate = jnp.where(chosen, jnp.concatenate(pieces, axis=0), 0.0)
    dlogit = prob * (dgate - jnp.sum(prob * dgate, axis=-1, keepdims=True))
    a = dlogit.astype(bf16)
    rest = dlogit - a.astype(f32)
    b = rest.astype(bf16)
    c = (rest - b.astype(f32)).astype(bf16)
    wide = dot_tn(moe_ref[...], jnp.concatenate([a, b, c], axis=1))
    out_ref[...] += (
        wide[:, :experts] + wide[:, experts : 2 * experts] + wide[:, 2 * experts :]
    )


def router_grad(info, terms, moe, tok, dp, sp, cap):
    tokens = info.shape[0] // dp
    experts = info.shape[1] // 2
    share = moe.shape[1]
    return pl.pallas_call(
        functools.partial(router_kernel, tok, sp, cap),
        grid=(dp,),
        in_specs=[
            pl.BlockSpec((tokens, 2 * experts), lambda g: (g, 0)),
            pl.BlockSpec((sp, cap * sp, experts), lambda g: (g, 0, 0)),
            pl.BlockSpec((tokens, share), lambda g: (g, 0)),
        ],
        out_specs=whole((share, experts)),
        out_shape=jax.ShapeDtypeStruct((share, experts), f32),
        compiler_params=pltpu.CompilerParams(vmem_limit_bytes=vmem_limit),
        name="router_grad",
    )(info, terms, moe)


def on_device(
    q_pre,
    attn_out,
    d_attn,
    k_pre,
    values,
    q_gain,
    k_gain,
    offsets,
    moe_in,
    router,
    expert_ids,
    d_moe,
    expert_out,
):
    dp = lax.axis_size("dp")
    sp = lax.axis_size("sp")
    me = lax.axis_index("sp").astype(jnp.int32)
    other = jnp.bitwise_xor(me, 1)
    chips = sp // 2
    swap = [(i, i ^ 1) for i in range(sp)]

    def exchange(x):
        return lax.ppermute(x, "sp", swap)

    def ahead(x, k):
        return lax.ppermute(x, "sp", [(i, (i + 2 * k) % sp) for i in range(sp)])

    def back(x, k):
        return lax.ppermute(x, "sp", [(i, (i - 2 * k) % sp) for i in range(sp)])

    def gathered(x):
        mine = [x] + [ahead(x, k) for k in range(1, chips)]
        return mine + [exchange(m) for m in mine]

    steps = 2 * jnp.arange(chips, dtype=jnp.int32)
    owners = jnp.concatenate([lax.rem(me - steps + sp, sp), lax.rem(other - steps + sp, sp)])
    qg, kg = q_gain[None, :], k_gain[None, :]

    kv = pack_keys(k_pre[0], values[0], kg)
    kv_blocks = gathered(kv)
    pack, info = gates(moe_in[0], router, expert_ids[0], d_moe[0])
    packs = gathered(pack)

    moe_share = lax.all_to_all(moe_in[0], "sp", split_axis=1, concat_axis=0, tiled=True)
    moe_all = lax.all_gather(moe_share, "dp", axis=0, tiled=True)
    info_all = lax.all_gather(info, ("dp", "sp"), axis=0, tiled=True)

    meta = jnp.concatenate([offsets + me * q_pre.shape[1], owners])
    dq, *parts = attend(
        meta,
        q_pre[0],
        attn_out[0],
        d_attn[0],
        qg,
        kv_blocks,
        [f32] * chips + [bf16] * chips,
    )
    pairs = [keep + exchange(send).astype(f32) for keep, send in zip(parts[:chips], parts[chips:])]
    arrived = [back(pairs[k].astype(bf16), k) for k in range(1, chips)]
    dk, dv = finish_keys(k_pre[0], kg, [pairs[0]] + arrived)

    experts_here, _, cap, width = expert_out.shape[1:]
    eout = jnp.transpose(expert_out[0], (0, 2, 1, 3)).reshape(experts_here * cap * sp, width)
    slot_meta = jnp.concatenate([(me * experts_here)[None], owners])
    batch, terms = slots(slot_meta, packs, eout, experts_here, cap, sp)
    batch = jnp.transpose(batch.reshape(experts_here, cap, sp, width), (0, 2, 1, 3))
    terms_all = lax.all_to_all(
        jnp.broadcast_to(terms[None], (dp * sp,) + terms.shape),
        ("dp", "sp"),
        split_axis=0,
        concat_axis=0,
        tiled=True,
    )
    router_local = router_grad(info_all, terms_all, moe_all, moe_in.shape[1], dp, sp, cap)
    return (dq[None], dk[None], dv[None], batch[None], router_local)


def solution(mesh):
    in_specs = (
        P("dp", "sp", None),
        P("dp", "sp", None),
        P("dp", "sp", None),
        P("dp", "sp", None),
        P("dp", "sp", None),
        P(),
        P(),
        P("dp"),
        P("dp", "sp", None),
        P(),
        P("dp", "sp", None),
        P("dp", "sp", None),
        P("dp", "sp", None, None, None),
    )
    out_specs = (
        P("dp", "sp", None),
        P("dp", "sp", None),
        P("dp", "sp", None),
        P("dp", "sp", None, None, None),
        P("sp", None),
    )
    return jax.shard_map(
        on_device, mesh=mesh, in_specs=in_specs, out_specs=out_specs, check_vma=False
    )
```

```python
import functools
import math

import jax
import jax.numpy as jnp
import numpy as np
from jax import lax
from jax.experimental import pallas as pl
from jax.experimental.pallas import tpu as pltpu
from jax.sharding import PartitionSpec as P

norm_eps = 1e-06
f32 = jnp.float32
bf16 = jnp.bfloat16
vmem_limit = 56 * 1024 * 1024


def dot_nt(a, b):
    return lax.dot_general(a, b, (((1,), (1,)), ((), ())), preferred_element_type=f32)


def dot_nn(a, b):
    return lax.dot_general(a, b, (((1,), (0,)), ((), ())), preferred_element_type=f32)


def dot_tn(a, b):
    return lax.dot_general(a, b, (((0,), (0,)), ((), ())), preferred_element_type=f32)


def whole(shape):
    return pl.BlockSpec(shape, lambda *_: (0,) * len(shape))


def keys_kernel(k_ref, v_ref, gain_ref, *kv_refs):
    hd = gain_ref.shape[1]
    gain = gain_ref[...]
    each = k_ref.shape[1] // hd // len(kv_refs)
    for g in range(k_ref.shape[1] // hd):
        kv_ref, i = kv_refs[g // each], g % each
        k = k_ref[:, g * hd : (g + 1) * hd].astype(f32)
        inv = lax.rsqrt(jnp.mean(k * k, axis=-1, keepdims=True) + norm_eps)
        kv_ref[:, 2 * i * hd : (2 * i + 1) * hd] = ((k * inv) * gain).astype(bf16)
        kv_ref[:, (2 * i + 1) * hd : (2 * i + 2) * hd] = v_ref[:, g * hd : (g + 1) * hd]


def pack_keys(k_pre, values, k_gain, parts):
    rows, width = k_pre.shape
    return pl.pallas_call(
        keys_kernel,
        out_shape=[jax.ShapeDtypeStruct((rows, 2 * width // parts), bf16)] * parts,
        name="pack_keys",
    )(k_pre, values, k_gain)


def gates_kernel(chips, meta_ref, moe_ref, router_ref, ids_ref, dmoe_ref, pack_ref, *share_refs):
    tok, width = moe_ref.shape
    experts = router_ref.shape[1]
    logits = dot_nn(moe_ref[...], router_ref[...])
    lane = lax.broadcasted_iota(jnp.int32, (tok, experts), 1)
    chosen = lane == ids_ref[:, 0:1]
    for k in range(1, ids_ref.shape[1]):
        chosen = jnp.logical_or(chosen, lane == ids_ref[:, k : k + 1])
    weights = jnp.where(chosen, jnp.exp(logits), 0.0)
    probs = weights / jnp.sum(weights, axis=-1, keepdims=True)
    high = probs.astype(bf16)
    low = (probs - high.astype(f32)).astype(bf16)
    pack_ref[:, :width] = dmoe_ref[...]
    pack_ref[:, width : width + experts] = jnp.where(chosen, high.astype(f32), -1.0).astype(bf16)
    pack_ref[:, width + experts :] = low
    share = width // (2 * chips)
    chip, core = meta_ref[0], meta_ref[1]
    for k in range(chips):
        to = lax.rem(chip + k, chips) * 2
        for i in range(2):
            at = pl.multiple_of((to + lax.rem(core + i, 2)) * share, 128)
            share_refs[k][:, i * share : (i + 1) * share] = moe_ref[:, pl.ds(at, share)]


def gates(meta, moe_in, router, ids, d_moe, chips):
    tok, width = moe_in.shape
    experts = router.shape[1]
    vm = pl.BlockSpec(memory_space=pltpu.VMEM)
    return pl.pallas_call(
        functools.partial(gates_kernel, chips),
        in_specs=[pl.BlockSpec(memory_space=pltpu.SMEM)] + [vm] * 4,
        out_shape=[jax.ShapeDtypeStruct((tok, width + 2 * experts), bf16)]
        + [jax.ShapeDtypeStruct((tok, width // chips), bf16)] * chips,
        compiler_params=pltpu.CompilerParams(vmem_limit_bytes=vmem_limit),
        name="gates",
    )(meta, moe_in, router, ids, d_moe)


def attend_kernel(blocks, first, meta_ref, q_ref, o_ref, do_ref, gain_ref, *refs):
    kv_refs = refs[:blocks]
    refs = refs[:blocks] + refs[blocks + (first > 0) :]
    dq_ref = refs[blocks]
    part_refs = refs[blocks + 1 : 2 * blocks + 1]
    tok = q_ref.shape[0]
    hd = gain_ref.shape[1]
    heads = q_ref.shape[1] // hd
    kb = kv_refs[0].shape[0]
    keys = kb * blocks
    scale = hd ** (-0.5)
    offset = meta_ref[0]
    gain = gain_ref[...]
    key = jnp.concatenate([r[:, :hd] for r in kv_refs], axis=0)
    val = jnp.concatenate([r[:, hd:] for r in kv_refs], axis=0)
    pos = jnp.concatenate(
        [
            meta_ref[1 + b] * kb + lax.broadcasted_iota(jnp.int32, (kb, 1), 0)
            for b in range(blocks)
        ],
        axis=0,
    )
    step_heads = min(heads, max(128 // tok, heads * 1024 // keys))
    rows = step_heads * tok
    limit = offset + lax.rem(lax.broadcasted_iota(jnp.int32, (1, rows), 1), tok)
    visible = pos <= limit
    dk = dv = None
    for h0 in range(0, heads, step_heads):

        def stack(ref):
            return jnp.concatenate(
                [ref[:, h * hd : (h + 1) * hd] for h in range(h0, h0 + step_heads)], axis=0
            )

        q = stack(q_ref).astype(f32)
        do = stack(do_ref)
        prod = do.astype(f32) * stack(o_ref).astype(f32)
        delta = jnp.sum(prod.T, axis=0, keepdims=True)
        inv = lax.rsqrt(jnp.mean(q * q, axis=-1, keepdims=True) + norm_eps)
        unit = q * inv
        q_hat = (unit * gain).astype(bf16)
        scores = dot_nt(key, q_hat)
        ex = jnp.where(visible, jnp.exp2(scores * (scale * math.log2(math.e))), 0.0)
        probs = ex * (1.0 / jnp.sum(ex, axis=0, keepdims=True))
        dv_one = dot_nn(probs.astype(bf16), do)
        dprobs = dot_nt(val, do)
        ds = ((probs * scale) * (dprobs - delta)).astype(bf16)
        dk_one = dot_nn(ds, q_hat)
        dq = dot_tn(key, ds).T
        c = dq * gain
        dq_pre = (inv * (c - unit * jnp.mean(c * unit, axis=-1, keepdims=True))).astype(bf16)
        for i in range(step_heads):
            h = h0 + i
            dq_ref[:, h * hd : (h + 1) * hd] = dq_pre[i * tok : (i + 1) * tok, :]
        dk = dk_one if dk is None else dk + dk_one
        dv = dv_one if dv is None else dv + dv_one
    for b in range(blocks):
        part_refs[b][:, :hd] = dk[b * kb : (b + 1) * kb, :].astype(part_refs[b].dtype)
        part_refs[b][:, hd:] = dv[b * kb : (b + 1) * kb, :].astype(part_refs[b].dtype)


def attend(meta, q, o, do, gain, kv_blocks, part_types, kv_heads, first, dq):
    tok, width = q.shape
    hd = gain.shape[1]
    kb, kv_width = kv_blocks[0].shape
    blocks = len(kv_blocks)
    step = width // kv_heads
    row_spec = pl.BlockSpec((tok, step), lambda g, m: (0, g + first))
    filled = [] if dq is None else [dq]
    kv_spec = pl.BlockSpec((kb, 2 * hd), lambda g, m: (0, g))
    return pl.pallas_call(
        functools.partial(attend_kernel, blocks, first),
        grid_spec=pltpu.PrefetchScalarGridSpec(
            num_scalar_prefetch=1,
            grid=(kv_width // (2 * hd),),
            in_specs=[row_spec] * 3
            + [whole((1, hd))]
            + [kv_spec] * blocks
            + [pl.BlockSpec(memory_space=pl.ANY)] * len(filled),
            out_specs=[row_spec] + [kv_spec] * blocks,
        ),
        out_shape=[jax.ShapeDtypeStruct((tok, width), bf16)]
        + [jax.ShapeDtypeStruct((kb, kv_width), t) for t in part_types],
        compiler_params=pltpu.CompilerParams(vmem_limit_bytes=vmem_limit),
        input_output_aliases={5 + blocks: 0} if filled else {},
        name="attend",
    )(meta, q, o, do, gain, *kv_blocks, *filled)


def finish_kernel(parts, k_ref, gain_ref, *refs):
    dk_ref, dv_ref = refs[-2:]
    hd = gain_ref.shape[1]
    gain = gain_ref[...]
    each = (len(refs) - 2) // parts
    heads = k_ref.shape[1] // hd
    for p in range(parts):
        total = refs[p * each][...].astype(f32)
        for r in refs[p * each + 1 : (p + 1) * each]:
            total = total + r[...].astype(f32)
        for i in range(heads // parts):
            g = p * (heads // parts) + i
            k = k_ref[:, g * hd : (g + 1) * hd].astype(f32)
            inv = lax.rsqrt(jnp.mean(k * k, axis=-1, keepdims=True) + norm_eps)
            unit = k * inv
            c = total[:, 2 * i * hd : (2 * i + 1) * hd] * gain
            dk = inv * (c - unit * jnp.mean(c * unit, axis=-1, keepdims=True))
            dk_ref[:, g * hd : (g + 1) * hd] = dk.astype(bf16)
            dv = total[:, (2 * i + 1) * hd : (2 * i + 2) * hd]
            dv_ref[:, g * hd : (g + 1) * hd] = dv.astype(bf16)


def finish_keys(k_pre, k_gain, sums):
    out = jax.ShapeDtypeStruct(k_pre.shape, bf16)
    return pl.pallas_call(
        functools.partial(finish_kernel, len(sums)),
        out_shape=(out, out),
        compiler_params=pltpu.CompilerParams(vmem_limit_bytes=vmem_limit),
        name="finish_keys",
    )(k_pre, k_gain, *[x for part in sums for x in part])


def earlier_same_block(rows, block):
    i = lax.broadcasted_iota(jnp.int32, (rows, rows), 0)
    j = lax.broadcasted_iota(jnp.int32, (rows, rows), 1)
    same = lax.div(i, block) == lax.div(j, block)
    return jnp.where(jnp.logical_and(same, j < i), 1.0, 0.0).astype(bf16)


def slots_kernel(
    blocks, sp, cap, meta_ref, table_ref, lanes_ref, *refs
):
    d_refs = refs[:blocks]
    g_refs = refs[blocks : 2 * blocks]
    eout_ref, batch_ref, terms_ref, dm, gated, hit_scr, acc = refs[2 * blocks :]
    tok = d_refs[0].shape[0]
    experts = g_refs[0].shape[1]
    rows = eout_ref.shape[0]
    tokens = tok * blocks
    step = pl.program_id(0)

    def pick():
        expert = meta_ref[0] + table_ref[:, 0:1]
        return lax.broadcasted_iota(jnp.int32, (rows, experts), 1) == expert

    @pl.when(step == 0)
    def _():
        coded = jnp.concatenate([r[...] for r in g_refs], axis=0)
        chosen = (coded >= 0).astype(bf16)
        rank = dot_nn(earlier_same_block(tokens, tok), chosen)
        sel = jnp.where(pick(), 1.0, 0.0).astype(bf16)
        gate = dot_nt(sel, coded)
        place = dot_nt(sel, rank.astype(bf16))
        lane_block = lax.div(lax.broadcasted_iota(jnp.int32, (1, tokens), 1), tok)
        source = jnp.zeros((1, tokens), jnp.int32)
        for b in range(blocks):
            source = jnp.where(lane_block == b, meta_ref[1 + b], source)
        hit = jnp.logical_and(
            jnp.logical_and(gate >= 0.0, place == table_ref[:, 1:2].astype(f32)),
            source == table_ref[:, 2:3],
        )
        gated[...] = jnp.where(hit, gate, 0.0).astype(bf16)
        hit_scr[...] = jnp.where(hit, 1.0, 0.0)
        acc[...] = jnp.zeros_like(acc)

    for b in range(blocks):
        dm[b * tok : (b + 1) * tok, :] = d_refs[b][...]
    d_all = dm[...]
    batch_ref[...] = dot_nn(gated[...], d_all).astype(bf16)
    acc[...] += dot_nt(eout_ref[...], d_all)

    @pl.when(step == pl.num_programs(0) - 1)
    def _():
        terms = jnp.sum(acc[...] * hit_scr[...], axis=-1, keepdims=True)
        placed = jnp.where(pick(), terms, 0.0)
        want = lax.broadcasted_iota(jnp.int32, (cap * sp, rows), 0)
        fold = jnp.where(want == lanes_ref[...], 1.0, 0.0)
        terms_ref[...] = lax.dot_general(
            fold,
            placed,
            (((1,), (0,)), ((), ())),
            precision=lax.Precision.HIGHEST,
            preferred_element_type=f32,
        )


def slots(meta, packs, eout, experts_here, cap, sp):
    rows, width = eout.shape
    tok, packed = packs[0].shape
    experts = (packed - width) // 2
    blocks = len(packs)
    r = np.arange(rows)
    e, c, s = r // (cap * sp), (r // sp) % cap, r % sp
    table = jnp.asarray(np.stack([e, c, s], axis=1), jnp.int32)
    lanes = jnp.asarray((c * sp + s)[None, :], jnp.int32)
    col = min(width, 1024)
    d_spec = pl.BlockSpec((tok, col), lambda i, m: (0, i))
    g_spec = pl.BlockSpec((tok, experts), lambda i, m: (0, width // experts))
    e_spec = pl.BlockSpec((rows, col), lambda i, m: (0, i))
    return pl.pallas_call(
        functools.partial(slots_kernel, blocks, sp, cap),
        grid_spec=pltpu.PrefetchScalarGridSpec(
            num_scalar_prefetch=1,
            grid=(width // col,),
            in_specs=[whole((rows, 3)), whole((1, rows))]
            + [d_spec] * blocks
            + [g_spec] * blocks
            + [e_spec],
            out_specs=[e_spec, whole((cap * sp, experts))],
            scratch_shapes=[
                pltpu.VMEM((tok * blocks, col), bf16),
                pltpu.VMEM((rows, tok * blocks), bf16),
                pltpu.VMEM((rows, tok * blocks), f32),
                pltpu.VMEM((rows, tok * blocks), f32),
            ],
        ),
        out_shape=[
            jax.ShapeDtypeStruct((rows, width), bf16),
            jax.ShapeDtypeStruct((cap * sp, experts), f32),
        ],
        compiler_params=pltpu.CompilerParams(vmem_limit_bytes=vmem_limit),
        name="slots",
    )(meta, table, lanes, *packs, *packs, eout)


def router_kernel(sp, cap, meta_ref, *refs):
    blocks = sp
    half = sp // 2
    info_refs = refs[:blocks]
    term_refs = refs[blocks : blocks + half]
    mine_refs = refs[blocks + half : blocks + 2 * half]
    sent_ref, out_ref, terms_scr = refs[blocks + 2 * half :]
    share, experts = out_ref.shape
    tok = info_refs[0].shape[0]
    info = jnp.concatenate([r[...] for r in info_refs], axis=0)
    moe = jnp.concatenate([r[:, :share] for r in mine_refs] + [sent_ref[...]], axis=0)
    terms = term_refs[0][...]
    for r in term_refs[1:]:
        terms = terms + r[...]
    terms_scr[...] = terms
    high = info[:, :experts]
    chosen = high >= 0
    prob = jnp.where(chosen, high.astype(f32) + info[:, experts:].astype(f32), 0.0)
    rank = dot_nn(earlier_same_block(tok * blocks, tok), chosen.astype(bf16))
    pieces = []
    for b in range(blocks):
        place = rank[b * tok : (b + 1) * tok, :]
        one = jnp.zeros((tok, experts), f32)
        for c in range(cap):
            row = terms_scr[pl.ds(c * sp + meta_ref[1 + b], 1), :]
            one = jnp.where(place == c, row, one)
        pieces.append(one)
    dgate = jnp.where(chosen, jnp.concatenate(pieces, axis=0), 0.0)
    dlogit = prob * (dgate - jnp.sum(prob * dgate, axis=-1, keepdims=True))
    a = dlogit.astype(bf16)
    rest = dlogit - a.astype(f32)
    b = rest.astype(bf16)
    c = (rest - b.astype(f32)).astype(bf16)
    wide = dot_tn(moe, jnp.concatenate([a, b, c], axis=1))
    out_ref[...] = wide[:, :experts] + wide[:, experts : 2 * experts] + wide[:, 2 * experts :]


def router_grad(meta, packs, terms, mine, sent, width, cap):
    sp = len(packs)
    tok, packed = packs[0].shape
    experts = (packed - width) // 2
    share = sent.shape[1]
    info_spec = pl.BlockSpec((tok, 2 * experts), lambda i, m: (0, width // (2 * experts)))
    return pl.pallas_call(
        functools.partial(router_kernel, sp, cap),
        grid_spec=pltpu.PrefetchScalarGridSpec(
            num_scalar_prefetch=1,
            grid=(1,),
            in_specs=[info_spec] * sp
            + [whole(terms[0].shape)] * len(terms)
            + [whole(mine[0].shape)] * len(mine)
            + [whole(sent.shape)],
            out_specs=whole((share, experts)),
            scratch_shapes=[pltpu.VMEM((cap * sp, experts), f32)],
        ),
        out_shape=jax.ShapeDtypeStruct((share, experts), f32),
        compiler_params=pltpu.CompilerParams(vmem_limit_bytes=vmem_limit),
        name="router_grad",
    )(meta, *packs, *terms, *mine, sent)


def on_device(
    q_pre,
    attn_out,
    d_attn,
    k_pre,
    values,
    q_gain,
    k_gain,
    offsets,
    moe_in,
    router,
    expert_ids,
    d_moe,
    expert_out,
):
    dp = lax.axis_size("dp")
    sp = lax.axis_size("sp")
    me = lax.axis_index("sp").astype(jnp.int32)
    other = jnp.bitwise_xor(me, 1)
    chips = sp // 2
    swap = [(i, i ^ 1) for i in range(sp)]

    def exchange(x):
        return lax.ppermute(x, "sp", swap)

    def ahead(x, k):
        return lax.ppermute(x, "sp", [(i, (i + 2 * k) % sp) for i in range(sp)])

    def back(x, k):
        return lax.ppermute(x, "sp", [(i, (i - 2 * k) % sp) for i in range(sp)])

    def gathered(x):
        mine = [x] + [ahead(x, k) for k in range(1, chips)]
        return mine + [exchange(m) for m in mine]

    steps = 2 * jnp.arange(chips, dtype=jnp.int32)
    owners = jnp.concatenate([lax.rem(me - steps + sp, sp), lax.rem(other - steps + sp, sp)])
    qg, kg = q_gain[None, :], k_gain[None, :]
    kv_heads = k_pre.shape[2] // q_gain.shape[0]
    parts = 2
    width = moe_in.shape[2]
    place = jnp.stack([me // 2, jnp.bitwise_and(me, 1)])

    pack, *shares = gates(place, moe_in[0], router, expert_ids[0], d_moe[0], chips)
    packs = gathered(pack)
    kv_parts = [gathered(kv) for kv in pack_keys(k_pre[0], values[0], kg, parts)]
    mine = [shares[0]] + [ahead(shares[k], k) for k in range(1, chips)]
    share = width // sp
    sent = exchange(jnp.concatenate([m[:, share:] for m in mine], axis=0))

    meta = jnp.concatenate([offsets + me * q_pre.shape[1], owners])
    dq, sums = None, []
    for p in range(parts):
        dq, *terms = attend(
            meta,
            q_pre[0],
            attn_out[0],
            d_attn[0],
            qg,
            kv_parts[p],
            [f32] * chips + [bf16] * chips,
            kv_heads,
            p * (kv_heads // parts),
            dq,
        )
        pairs = [
            keep + exchange(send).astype(f32) for keep, send in zip(terms[:chips], terms[chips:])
        ]
        sums.append([pairs[0]] + [back(pairs[k].astype(bf16), k) for k in range(1, chips)])
    dk, dv = finish_keys(k_pre[0], kg, sums)

    experts_here, _, cap, _ = expert_out.shape[1:]
    eout = jnp.transpose(expert_out[0], (0, 2, 1, 3)).reshape(experts_here * cap * sp, width)
    slot_meta = jnp.concatenate([(me * experts_here)[None], owners])
    batch, terms = slots(slot_meta, packs, eout, experts_here, cap, sp)
    batch = jnp.transpose(batch.reshape(experts_here, cap, sp, width), (0, 2, 1, 3))
    terms = terms + exchange(terms)
    terms = [terms] + [ahead(terms, k) for k in range(1, chips)]
    partial_sum = router_grad(slot_meta, packs, terms, mine, sent, width, cap)
    router_local = partial_sum
    for k in range(1, dp):
        if dp & (dp - 1):
            perm = [(i, (i + k) % dp) for i in range(dp)]
        else:
            perm = [(i, i ^ k) for i in range(dp)]
        router_local = router_local + lax.ppermute(partial_sum, "dp", perm)
    return (dq[None], dk[None], dv[None], batch[None], router_local)


def solution(mesh):
    in_specs = (
        P("dp", "sp", None),
        P("dp", "sp", None),
        P("dp", "sp", None),
        P("dp", "sp", None),
        P("dp", "sp", None),
        P(),
        P(),
        P("dp"),
        P("dp", "sp", None),
        P(),
        P("dp", "sp", None),
        P("dp", "sp", None),
        P("dp", "sp", None, None, None),
    )
    out_specs = (
        P("dp", "sp", None),
        P("dp", "sp", None),
        P("dp", "sp", None),
        P("dp", "sp", None, None, None),
        P("sp", None),
    )
    return jax.shard_map(
        on_device, mesh=mesh, in_specs=in_specs, out_specs=out_specs, check_vma=False
    )
```

```python
import functools
import math

import jax
import jax.numpy as jnp
import numpy as np
from jax import lax
from jax.experimental import pallas as pl
from jax.experimental.pallas import tpu as pltpu
from jax.sharding import PartitionSpec as P

norm_eps = 1e-06
f32 = jnp.float32
bf16 = jnp.bfloat16
vmem_limit = 56 * 1024 * 1024


def takes(us):
    flops = int(us * 1.15e9)
    return pl.CostEstimate(flops=flops, transcendentals=0, bytes_accessed=int(us * 3.6e6))


def dot_nt(a, b):
    return lax.dot_general(a, b, (((1,), (1,)), ((), ())), preferred_element_type=f32)


def dot_nn(a, b):
    return lax.dot_general(a, b, (((1,), (0,)), ((), ())), preferred_element_type=f32)


def dot_tn(a, b):
    return lax.dot_general(a, b, (((0,), (0,)), ((), ())), preferred_element_type=f32)


def whole(shape):
    return pl.BlockSpec(shape, lambda *_: (0,) * len(shape))


def keys_kernel(k_ref, v_ref, gain_ref, kv_ref):
    hd = gain_ref.shape[1]
    gain = gain_ref[...]
    for g in range(k_ref.shape[1] // hd):
        k = k_ref[:, g * hd : (g + 1) * hd].astype(f32)
        inv = lax.rsqrt(jnp.mean(k * k, axis=-1, keepdims=True) + norm_eps)
        kv_ref[:, 2 * g * hd : (2 * g + 1) * hd] = ((k * inv) * gain).astype(bf16)
        kv_ref[:, (2 * g + 1) * hd : (2 * g + 2) * hd] = v_ref[:, g * hd : (g + 1) * hd]


def pack_keys(k_pre, values, k_gain):
    rows, width = k_pre.shape
    return pl.pallas_call(
        keys_kernel,
        out_shape=jax.ShapeDtypeStruct((rows, 2 * width), bf16),
        cost_estimate=takes(1.8),
        name="pack_keys",
    )(k_pre, values, k_gain)


def gates_kernel(meta_ref, moe_ref, router_ref, ids_ref, dmoe_ref, *pack_refs):
    tok, width = moe_ref.shape
    experts = router_ref.shape[1]
    chips = len(pack_refs)
    logits = dot_nn(moe_ref[...], router_ref[...])
    lane = lax.broadcasted_iota(jnp.int32, (tok, experts), 1)
    chosen = lane == ids_ref[:, 0:1]
    for k in range(1, ids_ref.shape[1]):
        chosen = jnp.logical_or(chosen, lane == ids_ref[:, k : k + 1])
    weights = jnp.where(chosen, jnp.exp(logits), 0.0)
    probs = weights / jnp.sum(weights, axis=-1, keepdims=True)
    high = probs.astype(bf16)
    low = (probs - high.astype(f32)).astype(bf16)
    coded = jnp.where(chosen, high.astype(f32), -1.0).astype(bf16)
    share = width // (2 * chips)
    chip, core = meta_ref[0], meta_ref[1]
    d_all = dmoe_ref[...]
    for k in range(chips):
        to = lax.rem(chip + k, chips) * 2
        pack_refs[k][:, :width] = d_all
        for i in range(2):
            at = pl.multiple_of((to + lax.rem(core + i, 2)) * share, 128)
            pack_refs[k][:, width + i * share : width + (i + 1) * share] = moe_ref[
                :, pl.ds(at, share)
            ]
        pack_refs[k][:, width + 2 * share : width + 2 * share + experts] = coded
        pack_refs[k][:, width + 2 * share + experts :] = low


def gates(meta, moe_in, router, ids, d_moe, chips):
    tok, width = moe_in.shape
    experts = router.shape[1]
    vm = pl.BlockSpec(memory_space=pltpu.VMEM)
    packed = width + width // chips + 2 * experts
    return pl.pallas_call(
        gates_kernel,
        in_specs=[pl.BlockSpec(memory_space=pltpu.SMEM)] + [vm] * 4,
        out_shape=[jax.ShapeDtypeStruct((tok, packed), bf16)] * chips,
        compiler_params=pltpu.CompilerParams(vmem_limit_bytes=vmem_limit),
        cost_estimate=takes(2.8),
        name="gates",
    )(meta, moe_in, router, ids, d_moe)


def attend_kernel(blocks, meta_ref, q_ref, o_ref, do_ref, gain_ref, *refs):
    kv_refs = refs[:2]
    dq_ref = refs[-3]
    part_refs = refs[-2:]
    tok = q_ref.shape[0]
    hd = gain_ref.shape[1]
    heads = q_ref.shape[1] // hd
    kb = 2 * kv_refs[0].shape[0] // blocks
    keys = kb * blocks
    scale = hd ** (-0.5)
    offset = meta_ref[0]
    gain = gain_ref[...]
    key = jnp.concatenate([r[:, :hd] for r in kv_refs], axis=0)
    val = jnp.concatenate([r[:, hd:] for r in kv_refs], axis=0)
    pos = jnp.concatenate(
        [
            meta_ref[1 + b] * kb + lax.broadcasted_iota(jnp.int32, (kb, 1), 0)
            for b in range(blocks)
        ],
        axis=0,
    )
    step_heads = min(heads, max(128 // tok, heads * 1024 // keys))
    rows = step_heads * tok
    limit = offset + lax.rem(lax.broadcasted_iota(jnp.int32, (1, rows), 1), tok)
    visible = pos <= limit
    dk = dv = None
    for h0 in range(0, heads, step_heads):

        def stack(ref):
            return jnp.concatenate(
                [ref[:, h * hd : (h + 1) * hd] for h in range(h0, h0 + step_heads)], axis=0
            )

        q = stack(q_ref).astype(f32)
        do = stack(do_ref)
        prod = do.astype(f32) * stack(o_ref).astype(f32)
        delta = jnp.sum(prod.T, axis=0, keepdims=True)
        inv = lax.rsqrt(jnp.mean(q * q, axis=-1, keepdims=True) + norm_eps)
        unit = q * inv
        q_hat = (unit * gain).astype(bf16)
        scores = dot_nt(key, q_hat)
        ex = jnp.where(visible, jnp.exp2(scores * (scale * math.log2(math.e))), 0.0)
        probs = ex * (1.0 / jnp.sum(ex, axis=0, keepdims=True))
        dv_one = dot_nn(probs.astype(bf16), do)
        dprobs = dot_nt(val, do)
        ds = ((probs * scale) * (dprobs - delta)).astype(bf16)
        dk_one = dot_nn(ds, q_hat)
        dq = dot_tn(key, ds).T
        c = dq * gain
        dq_pre = (inv * (c - unit * jnp.mean(c * unit, axis=-1, keepdims=True))).astype(bf16)
        for i in range(step_heads):
            h = h0 + i
            dq_ref[:, h * hd : (h + 1) * hd] = dq_pre[i * tok : (i + 1) * tok, :]
        dk = dk_one if dk is None else dk + dk_one
        dv = dv_one if dv is None else dv + dv_one
    half = keys // 2
    for i, ref in enumerate(part_refs):
        ref[:, :hd] = dk[i * half : (i + 1) * half, :].astype(ref.dtype)
        ref[:, hd:] = dv[i * half : (i + 1) * half, :].astype(ref.dtype)


def attend(meta, q, o, do, gain, kv_halves, blocks, kv_heads):
    tok, width = q.shape
    hd = gain.shape[1]
    half, kv_width = kv_halves[0].shape
    step = width // kv_heads
    row_spec = pl.BlockSpec((tok, step), lambda g, m: (0, g))
    part_spec = pl.BlockSpec((half, 2 * hd), lambda g, m: (0, g))
    return pl.pallas_call(
        functools.partial(attend_kernel, blocks),
        grid_spec=pltpu.PrefetchScalarGridSpec(
            num_scalar_prefetch=1,
            grid=(kv_width // (2 * hd),),
            in_specs=[row_spec] * 3
            + [whole((1, hd))]
            + [part_spec] * 2,
            out_specs=[row_spec, part_spec, part_spec],
        ),
        out_shape=[
            jax.ShapeDtypeStruct((tok, width), bf16),
            jax.ShapeDtypeStruct((half, kv_width), f32),
            jax.ShapeDtypeStruct((half, kv_width), bf16),
        ],
        compiler_params=pltpu.CompilerParams(vmem_limit_bytes=vmem_limit),
        cost_estimate=takes(10),
        name="attend",
    )(meta, q, o, do, gain, *kv_halves)


def finish_kernel(k_ref, gain_ref, *refs):
    dk_ref, dv_ref = refs[-2:]
    hd = gain_ref.shape[1]
    gain = gain_ref[...]
    total = refs[0][...].astype(f32)
    for r in refs[1:-2]:
        total = total + r[...].astype(f32)
    for g in range(k_ref.shape[1] // hd):
        k = k_ref[:, g * hd : (g + 1) * hd].astype(f32)
        inv = lax.rsqrt(jnp.mean(k * k, axis=-1, keepdims=True) + norm_eps)
        unit = k * inv
        c = total[:, 2 * g * hd : (2 * g + 1) * hd] * gain
        dk = inv * (c - unit * jnp.mean(c * unit, axis=-1, keepdims=True))
        dk_ref[:, g * hd : (g + 1) * hd] = dk.astype(bf16)
        dv_ref[:, g * hd : (g + 1) * hd] = total[
            :, (2 * g + 1) * hd : (2 * g + 2) * hd
        ].astype(bf16)


def finish_keys(k_pre, k_gain, sums):
    out = jax.ShapeDtypeStruct(k_pre.shape, bf16)
    return pl.pallas_call(
        finish_kernel,
        out_shape=(out, out),
        compiler_params=pltpu.CompilerParams(vmem_limit_bytes=vmem_limit),
        cost_estimate=takes(2.2),
        name="finish_keys",
    )(k_pre, k_gain, *sums)


def earlier_same_block(rows, block):
    i = lax.broadcasted_iota(jnp.int32, (rows, rows), 0)
    j = lax.broadcasted_iota(jnp.int32, (rows, rows), 1)
    same = lax.div(i, block) == lax.div(j, block)
    return jnp.where(jnp.logical_and(same, j < i), 1.0, 0.0).astype(bf16)


def terms_kernel(blocks, sp, cap, meta_ref, table_ref, lanes_ref, *refs):
    d_refs = refs[:2]
    g_refs = refs[2:4]
    eout_ref, gated_ref, terms_ref, dm, hit_scr, acc = refs[4:]
    half = d_refs[0].shape[0]
    tokens = 2 * half
    tok = tokens // blocks
    experts = g_refs[0].shape[1]
    rows = eout_ref.shape[0]
    step = pl.program_id(0)

    def pick():
        expert = meta_ref[0] + table_ref[:, 0:1]
        return lax.broadcasted_iota(jnp.int32, (rows, experts), 1) == expert

    @pl.when(step == 0)
    def _():
        coded = jnp.concatenate([r[...] for r in g_refs], axis=0)
        chosen = (coded >= 0).astype(bf16)
        rank = dot_nn(earlier_same_block(tokens, tok), chosen)
        sel = jnp.where(pick(), 1.0, 0.0).astype(bf16)
        gate = dot_nt(sel, coded)
        place = dot_nt(sel, rank.astype(bf16))
        lane_block = lax.div(lax.broadcasted_iota(jnp.int32, (1, tokens), 1), tok)
        source = jnp.zeros((1, tokens), jnp.int32)
        for b in range(blocks):
            source = jnp.where(lane_block == b, meta_ref[1 + b], source)
        hit = jnp.logical_and(
            jnp.logical_and(gate >= 0.0, place == table_ref[:, 1:2].astype(f32)),
            source == table_ref[:, 2:3],
        )
        gated_ref[...] = jnp.where(hit, gate, 0.0).astype(bf16)
        hit_scr[...] = jnp.where(hit, 1.0, 0.0)
        acc[...] = jnp.zeros_like(acc)

    for i in range(2):
        dm[i * half : (i + 1) * half, :] = d_refs[i][...]
    acc[...] += dot_nt(eout_ref[...], dm[...])

    @pl.when(step == pl.num_programs(0) - 1)
    def _():
        terms = jnp.sum(acc[...] * hit_scr[...], axis=-1, keepdims=True)
        placed = jnp.where(pick(), terms, 0.0)
        want = lax.broadcasted_iota(jnp.int32, (cap * sp, rows), 0)
        fold = jnp.where(want == lanes_ref[...], 1.0, 0.0)
        terms_ref[...] = lax.dot_general(
            fold,
            placed,
            (((1,), (0,)), ((), ())),
            precision=lax.Precision.HIGHEST,
            preferred_element_type=f32,
        )


def slot_terms(meta, packs, eout, experts, cap, sp):
    rows, width = eout.shape
    half, packed = packs[0].shape
    blocks = sp
    r = np.arange(rows)
    e, c, s = r // (cap * sp), (r // sp) % cap, r % sp
    table = jnp.asarray(np.stack([e, c, s], axis=1), jnp.int32)
    lanes = jnp.asarray((c * sp + s)[None, :], jnp.int32)
    col = min(width, 1024)
    tokens = 2 * half
    gate_at = (packed - 2 * experts) // experts
    d_spec = pl.BlockSpec((half, col), lambda i, m: (0, i))
    g_spec = pl.BlockSpec((half, experts), lambda i, m: (0, gate_at))
    e_spec = pl.BlockSpec((rows, col), lambda i, m: (0, i))
    return pl.pallas_call(
        functools.partial(terms_kernel, blocks, sp, cap),
        grid_spec=pltpu.PrefetchScalarGridSpec(
            num_scalar_prefetch=1,
            grid=(width // col,),
            in_specs=[whole((rows, 3)), whole((1, rows))]
            + [d_spec] * 2
            + [g_spec] * 2
            + [e_spec],
            out_specs=[whole((rows, tokens)), whole((cap * sp, experts))],
            scratch_shapes=[
                pltpu.VMEM((tokens, col), bf16),
                pltpu.VMEM((rows, tokens), f32),
                pltpu.VMEM((rows, tokens), f32),
            ],
        ),
        out_shape=[
            jax.ShapeDtypeStruct((rows, tokens), bf16),
            jax.ShapeDtypeStruct((cap * sp, experts), f32),
        ],
        compiler_params=pltpu.CompilerParams(vmem_limit_bytes=vmem_limit),
        cost_estimate=takes(6.2),
        name="slot_terms",
    )(meta, table, lanes, *packs, *packs, eout)


def batch_kernel(gated_ref, *refs):
    batch_ref, dm = refs[-2:]
    tok = refs[0].shape[0]
    for b, r in enumerate(refs[:-2]):
        dm[b * tok : (b + 1) * tok, :] = r[...]
    batch_ref[...] = dot_nn(gated_ref[...], dm[...]).astype(bf16)


def batch_grad(gated, packs, width):
    rows, tokens = gated.shape
    tok = packs[0].shape[0]
    col = min(width, 1024)
    return pl.pallas_call(
        batch_kernel,
        grid=(width // col,),
        in_specs=[whole((rows, tokens))]
        + [pl.BlockSpec((tok, col), lambda i: (0, i))] * len(packs),
        out_specs=pl.BlockSpec((rows, col), lambda i: (0, i)),
        out_shape=jax.ShapeDtypeStruct((rows, width), bf16),
        scratch_shapes=[pltpu.VMEM((tokens, col), bf16)],
        compiler_params=pltpu.CompilerParams(vmem_limit_bytes=vmem_limit),
        cost_estimate=takes(4.6),
        name="batch_grad",
    )(gated, *packs)


def router_kernel(sp, cap, meta_ref, *refs):
    info_refs, moe_refs = refs[:2], refs[2:4]
    terms_in, out_ref, terms_ref = refs[4:]
    terms_ref[...] = jnp.sum(terms_in[...], axis=0)
    share, experts = out_ref.shape
    tok = 2 * info_refs[0].shape[0] // sp
    info = jnp.concatenate([r[...] for r in info_refs], axis=0)
    moe = jnp.concatenate([r[...] for r in moe_refs], axis=0)
    high = info[:, :experts]
    chosen = high >= 0
    prob = jnp.where(chosen, high.astype(f32) + info[:, experts:].astype(f32), 0.0)
    rank = dot_nn(earlier_same_block(tok * sp, tok), chosen.astype(bf16))
    pieces = []
    for b in range(sp):
        place = rank[b * tok : (b + 1) * tok, :]
        one = jnp.zeros((tok, experts), f32)
        for c in range(cap):
            row = terms_ref[pl.ds(c * sp + meta_ref[1 + b], 1), :]
            one = jnp.where(place == c, row, one)
        pieces.append(one)
    dgate = jnp.where(chosen, jnp.concatenate(pieces, axis=0), 0.0)
    dlogit = prob * (dgate - jnp.sum(prob * dgate, axis=-1, keepdims=True))
    a = dlogit.astype(bf16)
    rest = dlogit - a.astype(f32)
    b = rest.astype(bf16)
    c = (rest - b.astype(f32)).astype(bf16)
    wide = dot_tn(moe, jnp.concatenate([a, b, c], axis=1))
    total = wide[:, :experts] + wide[:, experts : 2 * experts] + wide[:, 2 * experts :]
    out_ref[...] = total.astype(bf16)


def router_grad(meta, packs, terms, width, experts, cap, sp):
    half, packed = packs[0].shape
    share = width // sp
    info_at = packed // (2 * experts) - 1
    info_spec = pl.BlockSpec((half, 2 * experts), lambda i, m: (0, info_at))
    moe_specs = [pl.BlockSpec((half, share), lambda i, m, c=c: (0, sp + c)) for c in range(2)]
    return pl.pallas_call(
        functools.partial(router_kernel, sp, cap),
        grid_spec=pltpu.PrefetchScalarGridSpec(
            num_scalar_prefetch=1,
            grid=(1,),
            in_specs=[info_spec] * 2 + moe_specs + [whole(terms.shape)],
            out_specs=whole((share, experts)),
            scratch_shapes=[pltpu.VMEM((cap * sp, experts), f32)],
        ),
        out_shape=jax.ShapeDtypeStruct((share, experts), bf16),
        compiler_params=pltpu.CompilerParams(vmem_limit_bytes=vmem_limit),
        cost_estimate=takes(3),
        name="router_grad",
    )(meta, *packs, *packs, terms)


def flipped(x, axis, size, k):
    return lax.ppermute(x, axis, [(i, i ^ k) for i in range(size)])


def sent_over(axis, size, x):
    if size & (size - 1):
        return [lax.psum(x.astype(f32), axis)]
    return [x] + [flipped(x, axis, size, k) for k in range(1, size)]


def tree_sum(terms):
    terms = [x.astype(f32) for x in terms]
    while len(terms) > 1:
        terms = [a + b for a, b in zip(terms[0::2], terms[1::2])]
    return terms[0]


def together(*arrays):
    return lax.optimization_barrier(arrays)


def on_device(
    q_pre,
    attn_out,
    d_attn,
    k_pre,
    values,
    q_gain,
    k_gain,
    offsets,
    moe_in,
    router,
    expert_ids,
    d_moe,
    expert_out,
):
    dp = lax.axis_size("dp")
    sp = lax.axis_size("sp")
    me = lax.axis_index("sp").astype(jnp.int32)
    other = jnp.bitwise_xor(me, 1)
    chips = sp // 2
    swap = [(i, i ^ 1) for i in range(sp)]

    def exchange(x):
        return lax.ppermute(x, "sp", swap)

    def ahead(x, k):
        return lax.ppermute(x, "sp", [(i, (i + 2 * k) % sp) for i in range(sp)])

    def back(x, k):
        return lax.ppermute(x, "sp", [(i, (i - 2 * k) % sp) for i in range(sp)])

    def both(mine):
        mine = jnp.concatenate(mine, axis=0)
        return [mine, exchange(mine)]

    steps = 2 * jnp.arange(chips, dtype=jnp.int32)
    owners = jnp.concatenate([lax.rem(me - steps + sp, sp), lax.rem(other - steps + sp, sp)])
    qg, kg = q_gain[None, :], k_gain[None, :]
    kv_heads = k_pre.shape[2] // q_gain.shape[0]
    width = moe_in.shape[2]
    experts = router.shape[1]
    place = jnp.stack([me // 2, jnp.bitwise_and(me, 1)])

    experts_here, _, cap, _ = expert_out.shape[1:]
    eout = jnp.transpose(expert_out[0], (0, 2, 1, 3)).reshape(experts_here * cap * sp, width)
    slot_meta = jnp.concatenate([(me * experts_here)[None], owners])
    meta = jnp.concatenate([offsets + me * q_pre.shape[1], owners])

    kv = pack_keys(k_pre[0], values[0], kg)
    kv = [kv] + [ahead(kv, k) for k in range(1, chips)]
    packs = gates(place, moe_in[0], router, expert_ids[0], d_moe[0], chips)
    kv, packs = together(kv, packs)

    packs = [packs[0]] + [ahead(packs[k], k) for k in range(1, chips)]
    dq, keep, send = attend(
        meta, q_pre[0], attn_out[0], d_attn[0], qg, both(kv), sp, kv_heads
    )
    packs, keep, send = together(packs, keep, send)

    rows = k_pre.shape[1]
    arrived = exchange(send)
    sums = [
        keep[k * rows : (k + 1) * rows] + arrived[k * rows : (k + 1) * rows].astype(f32)
        for k in range(chips)
    ]
    sums = [sums[0]] + [x.astype(bf16) for x in sums[1:]]
    packs, sums = together(packs, sums)

    sums = [sums[0]] + [back(sums[k], k) for k in range(1, chips)]
    packs = both(packs)
    gated, terms = slot_terms(slot_meta, packs, eout, experts, cap, sp)
    terms = lax.all_to_all(
        jnp.broadcast_to(terms[None], (sp,) + terms.shape),
        "sp",
        split_axis=0,
        concat_axis=0,
        tiled=True,
    )
    batch = batch_grad(gated, packs, width)
    sums, terms, batch = together(sums, terms, batch)

    routed = router_grad(slot_meta, packs, terms, width, experts, cap, sp)
    routed = sent_over("dp", dp, routed)
    dk, dv = finish_keys(k_pre[0], kg, sums)
    batch = jnp.transpose(batch.reshape(experts_here, cap, sp, width), (0, 2, 1, 3))
    return (dq[None], dk[None], dv[None], batch[None], tree_sum(routed))


def solution(mesh):
    in_specs = (
        P("dp", "sp", None),
        P("dp", "sp", None),
        P("dp", "sp", None),
        P("dp", "sp", None),
        P("dp", "sp", None),
        P(),
        P(),
        P("dp"),
        P("dp", "sp", None),
        P(),
        P("dp", "sp", None),
        P("dp", "sp", None),
        P("dp", "sp", None, None, None),
    )
    out_specs = (
        P("dp", "sp", None),
        P("dp", "sp", None),
        P("dp", "sp", None),
        P("dp", "sp", None, None, None),
        P("sp", None),
    )
    return jax.shard_map(
        on_device, mesh=mesh, in_specs=in_specs, out_specs=out_specs, check_vma=False
    )
```

```python
import functools
import math

import jax
import jax.numpy as jnp
import numpy as np
from jax import lax
from jax.experimental import pallas as pl
from jax.experimental.pallas import tpu as pltpu
from jax.sharding import PartitionSpec as P

norm_eps = 1e-06
f32 = jnp.float32
bf16 = jnp.bfloat16
vmem_limit = 56 * 1024 * 1024


def takes(us):
    flops = int(us * 1.15e9)
    return pl.CostEstimate(flops=flops, transcendentals=0, bytes_accessed=int(us * 3.6e6))


def dot_nt(a, b):
    return lax.dot_general(a, b, (((1,), (1,)), ((), ())), preferred_element_type=f32)


def dot_nn(a, b):
    return lax.dot_general(a, b, (((1,), (0,)), ((), ())), preferred_element_type=f32)


def dot_tn(a, b):
    return lax.dot_general(a, b, (((0,), (0,)), ((), ())), preferred_element_type=f32)


def whole(shape):
    return pl.BlockSpec(shape, lambda *_: (0,) * len(shape))


def keys_kernel(k_ref, v_ref, gain_ref, kv_ref):
    hd = gain_ref.shape[1]
    gain = gain_ref[...]
    for g in range(k_ref.shape[1] // hd):
        k = k_ref[:, g * hd : (g + 1) * hd].astype(f32)
        inv = lax.rsqrt(jnp.mean(k * k, axis=-1, keepdims=True) + norm_eps)
        kv_ref[:, 2 * g * hd : (2 * g + 1) * hd] = ((k * inv) * gain).astype(bf16)
        kv_ref[:, (2 * g + 1) * hd : (2 * g + 2) * hd] = v_ref[:, g * hd : (g + 1) * hd]


def pack_keys(k_pre, values, k_gain):
    rows, width = k_pre.shape
    return pl.pallas_call(
        keys_kernel,
        out_shape=jax.ShapeDtypeStruct((rows, 2 * width), bf16),
        cost_estimate=takes(1.8),
        name="pack_keys",
    )(k_pre, values, k_gain)


def gates_kernel(chips, meta_ref, moe_ref, router_ref, ids_ref, dmoe_ref, *pack_refs):
    tok, width = moe_ref.shape
    experts = router_ref.shape[1]
    logits = dot_nn(moe_ref[...], router_ref[...])
    lane = lax.broadcasted_iota(jnp.int32, (tok, experts), 1)
    chosen = lane == ids_ref[:, 0:1]
    for k in range(1, ids_ref.shape[1]):
        chosen = jnp.logical_or(chosen, lane == ids_ref[:, k : k + 1])
    weights = jnp.where(chosen, jnp.exp(logits), 0.0)
    probs = weights / jnp.sum(weights, axis=-1, keepdims=True)
    high = probs.astype(bf16)
    low = (probs - high.astype(f32)).astype(bf16)
    coded = jnp.where(chosen, high.astype(f32), -1.0).astype(bf16)
    share = width // (2 * chips)
    chip, core = meta_ref[0], meta_ref[1]
    d_all = dmoe_ref[...]
    for k, ref in enumerate(pack_refs):
        ref[:, :width] = d_all
        ref[:, width + 2 * share : width + 2 * share + experts] = coded
        ref[:, width + 2 * share + experts : width + 2 * share + 2 * experts] = low
        to = jnp.bitwise_xor(chip, k) * 2
        for i in range(2):
            at = pl.multiple_of((to + jnp.bitwise_xor(core, i)) * share, 128)
            ref[:, width + i * share : width + (i + 1) * share] = moe_ref[:, pl.ds(at, share)]


def gates(meta, moe_in, router, ids, d_moe, chips):
    tok, width = moe_in.shape
    experts = router.shape[1]
    vm = pl.BlockSpec(memory_space=pltpu.VMEM)
    packed = width + width // chips + 2 * experts
    return pl.pallas_call(
        functools.partial(gates_kernel, chips),
        in_specs=[pl.BlockSpec(memory_space=pltpu.SMEM)] + [vm] * 4,
        out_shape=[jax.ShapeDtypeStruct((tok, packed), bf16)] * chips,
        compiler_params=pltpu.CompilerParams(vmem_limit_bytes=vmem_limit),
        cost_estimate=takes(2.8),
        name="gates",
    )(meta, moe_in, router, ids, d_moe)


def attend_kernel(blocks, meta_ref, q_ref, o_ref, do_ref, gain_ref, *refs):
    kv_refs = refs[:2]
    dq_ref = refs[-5]
    part_refs = refs[-4:]
    tok = q_ref.shape[0]
    hd = gain_ref.shape[1]
    heads = q_ref.shape[1] // hd
    kb = 2 * kv_refs[0].shape[0] // blocks
    keys = kb * blocks
    scale = hd ** (-0.5)
    offset = meta_ref[0]
    gain = gain_ref[...]
    key = jnp.concatenate([r[:, :hd] for r in kv_refs], axis=0)
    val = jnp.concatenate([r[:, hd:] for r in kv_refs], axis=0)
    pos = jnp.concatenate(
        [
            meta_ref[1 + b] * kb + lax.broadcasted_iota(jnp.int32, (kb, 1), 0)
            for b in range(blocks)
        ],
        axis=0,
    )
    step_heads = min(heads, max(128 // tok, heads * 1024 // keys))
    rows = step_heads * tok
    limit = offset + lax.rem(lax.broadcasted_iota(jnp.int32, (1, rows), 1), tok)
    visible = pos <= limit
    dk = dv = None
    for h0 in range(0, heads, step_heads):

        def stack(ref):
            return jnp.concatenate(
                [ref[:, h * hd : (h + 1) * hd] for h in range(h0, h0 + step_heads)], axis=0
            )

        q = stack(q_ref).astype(f32)
        do = stack(do_ref)
        prod = do.astype(f32) * stack(o_ref).astype(f32)
        delta = jnp.sum(prod.T, axis=0, keepdims=True)
        inv = lax.rsqrt(jnp.mean(q * q, axis=-1, keepdims=True) + norm_eps)
        unit = q * inv
        q_hat = (unit * gain).astype(bf16)
        scores = dot_nt(key, q_hat)
        ex = jnp.where(visible, jnp.exp2(scores * (scale * math.log2(math.e))), 0.0)
        probs = ex * (1.0 / jnp.sum(ex, axis=0, keepdims=True))
        dv_one = dot_nn(probs.astype(bf16), do)
        dprobs = dot_nt(val, do)
        ds = ((probs * scale) * (dprobs - delta)).astype(bf16)
        dk_one = dot_nn(ds, q_hat)
        dq = dot_tn(key, ds).T
        c = dq * gain
        dq_pre = (inv * (c - unit * jnp.mean(c * unit, axis=-1, keepdims=True))).astype(bf16)
        for i in range(step_heads):
            h = h0 + i
            dq_ref[:, h * hd : (h + 1) * hd] = dq_pre[i * tok : (i + 1) * tok, :]
        dk = dk_one if dk is None else dk + dk_one
        dv = dv_one if dv is None else dv + dv_one
    at = 0
    for ref in part_refs:
        size = ref.shape[0]
        ref[:, :hd] = dk[at : at + size, :].astype(ref.dtype)
        ref[:, hd:] = dv[at : at + size, :].astype(ref.dtype)
        at += size


def attend(meta, q, o, do, gain, kv_halves, blocks, kv_heads):
    tok, width = q.shape
    hd = gain.shape[1]
    half, kv_width = kv_halves[0].shape
    step = width // kv_heads
    row_spec = pl.BlockSpec((tok, step), lambda g, m: (0, g))
    part_spec = pl.BlockSpec((half, 2 * hd), lambda g, m: (0, g))
    own = 2 * half // blocks
    sizes = (own, half - own) * 2
    return pl.pallas_call(
        functools.partial(attend_kernel, blocks),
        grid_spec=pltpu.PrefetchScalarGridSpec(
            num_scalar_prefetch=1,
            grid=(kv_width // (2 * hd),),
            in_specs=[row_spec] * 3
            + [whole((1, hd))]
            + [part_spec] * 2,
            out_specs=[row_spec] + [pl.BlockSpec((n, 2 * hd), lambda g, m: (0, g)) for n in sizes],
        ),
        out_shape=[
            jax.ShapeDtypeStruct((tok, width), bf16),
            jax.ShapeDtypeStruct((sizes[0], kv_width), f32),
            jax.ShapeDtypeStruct((sizes[1], kv_width), f32),
            jax.ShapeDtypeStruct((sizes[2], kv_width), bf16),
            jax.ShapeDtypeStruct((sizes[3], kv_width), bf16),
        ],
        compiler_params=pltpu.CompilerParams(vmem_limit_bytes=vmem_limit),
        cost_estimate=takes(10),
        name="attend",
    )(meta, q, o, do, gain, *kv_halves)


def finish_kernel(k_ref, gain_ref, *refs):
    dk_ref, dv_ref = refs[-2:]
    hd = gain_ref.shape[1]
    gain = gain_ref[...]
    total = refs[0][...].astype(f32)
    for r in refs[1:-2]:
        total = total + r[...].astype(f32)
    for g in range(k_ref.shape[1] // hd):
        k = k_ref[:, g * hd : (g + 1) * hd].astype(f32)
        inv = lax.rsqrt(jnp.mean(k * k, axis=-1, keepdims=True) + norm_eps)
        unit = k * inv
        c = total[:, 2 * g * hd : (2 * g + 1) * hd] * gain
        dk = inv * (c - unit * jnp.mean(c * unit, axis=-1, keepdims=True))
        dk_ref[:, g * hd : (g + 1) * hd] = dk.astype(bf16)
        dv_ref[:, g * hd : (g + 1) * hd] = total[
            :, (2 * g + 1) * hd : (2 * g + 2) * hd
        ].astype(bf16)


def finish_keys(k_pre, k_gain, sums):
    out = jax.ShapeDtypeStruct(k_pre.shape, bf16)
    return pl.pallas_call(
        finish_kernel,
        out_shape=(out, out),
        compiler_params=pltpu.CompilerParams(vmem_limit_bytes=vmem_limit),
        cost_estimate=takes(2.2),
        name="finish_keys",
    )(k_pre, k_gain, *sums)


def earlier_same_block(rows, block):
    i = lax.broadcasted_iota(jnp.int32, (rows, rows), 0)
    j = lax.broadcasted_iota(jnp.int32, (rows, rows), 1)
    same = lax.div(i, block) == lax.div(j, block)
    return jnp.where(jnp.logical_and(same, j < i), 1.0, 0.0).astype(bf16)


def terms_kernel(blocks, sp, cap, meta_ref, table_ref, lanes_ref, *refs):
    d_refs = refs[:2]
    g_refs = refs[2:4]
    eout_ref, gated_ref, terms_ref, dm, hit_scr, acc = refs[4:]
    half = d_refs[0].shape[0]
    tokens = 2 * half
    tok = tokens // blocks
    experts = g_refs[0].shape[1]
    rows = eout_ref.shape[0]
    step = pl.program_id(0)

    def pick():
        expert = meta_ref[0] + table_ref[:, 0:1]
        return lax.broadcasted_iota(jnp.int32, (rows, experts), 1) == expert

    @pl.when(step == 0)
    def _():
        coded = jnp.concatenate([r[...] for r in g_refs], axis=0)
        chosen = (coded >= 0).astype(bf16)
        rank = dot_nn(earlier_same_block(tokens, tok), chosen)
        sel = jnp.where(pick(), 1.0, 0.0).astype(bf16)
        gate = dot_nt(sel, coded)
        place = dot_nt(sel, rank.astype(bf16))
        lane_block = lax.div(lax.broadcasted_iota(jnp.int32, (1, tokens), 1), tok)
        source = jnp.zeros((1, tokens), jnp.int32)
        for b in range(blocks):
            source = jnp.where(lane_block == b, meta_ref[1 + b], source)
        hit = jnp.logical_and(
            jnp.logical_and(gate >= 0.0, place == table_ref[:, 1:2].astype(f32)),
            source == table_ref[:, 2:3],
        )
        gated_ref[...] = jnp.where(hit, gate, 0.0).astype(bf16)
        hit_scr[...] = jnp.where(hit, 1.0, 0.0)
        acc[...] = jnp.zeros_like(acc)

    for i in range(2):
        dm[i * half : (i + 1) * half, :] = d_refs[i][...]
    acc[...] += dot_nt(eout_ref[...], dm[...])

    @pl.when(step == pl.num_programs(0) - 1)
    def _():
        terms = jnp.sum(acc[...] * hit_scr[...], axis=-1, keepdims=True)
        placed = jnp.where(pick(), terms, 0.0)
        want = lax.broadcasted_iota(jnp.int32, (cap * sp, rows), 0)
        fold = jnp.where(want == lanes_ref[...], 1.0, 0.0)
        folded = lax.dot_general(
            fold,
            placed,
            (((1,), (0,)), ((), ())),
            precision=lax.Precision.HIGHEST,
            preferred_element_type=f32,
        )
        for to in range(terms_ref.shape[0]):
            terms_ref[to] = folded


def slot_terms(meta, packs, eout, experts, cap, sp):
    rows, width = eout.shape
    half, packed = packs[0].shape
    blocks = sp
    r = np.arange(rows)
    e, c, s = r // (cap * sp), (r // sp) % cap, r % sp
    table = jnp.asarray(np.stack([e, c, s], axis=1), jnp.int32)
    lanes = jnp.asarray((c * sp + s)[None, :], jnp.int32)
    col = min(width, 1024)
    tokens = 2 * half
    gate_at = (packed - 2 * experts) // experts
    d_spec = pl.BlockSpec((half, col), lambda i, m: (0, i))
    g_spec = pl.BlockSpec((half, experts), lambda i, m: (0, gate_at))
    e_spec = pl.BlockSpec((rows, col), lambda i, m: (0, i))
    return pl.pallas_call(
        functools.partial(terms_kernel, blocks, sp, cap),
        grid_spec=pltpu.PrefetchScalarGridSpec(
            num_scalar_prefetch=1,
            grid=(width // col,),
            in_specs=[whole((rows, 3)), whole((1, rows))]
            + [d_spec] * 2
            + [g_spec] * 2
            + [e_spec],
            out_specs=[whole((rows, tokens)), whole((sp, cap * sp, experts))],
            scratch_shapes=[
                pltpu.VMEM((tokens, col), bf16),
                pltpu.VMEM((rows, tokens), f32),
                pltpu.VMEM((rows, tokens), f32),
            ],
        ),
        out_shape=[
            jax.ShapeDtypeStruct((rows, tokens), bf16),
            jax.ShapeDtypeStruct((sp, cap * sp, experts), f32),
        ],
        compiler_params=pltpu.CompilerParams(vmem_limit_bytes=vmem_limit),
        cost_estimate=takes(6.2),
        name="slot_terms",
    )(meta, table, lanes, *packs, *packs, eout)


def batch_kernel(gated_ref, *refs):
    batch_ref, dm = refs[-2:]
    tok = refs[0].shape[0]
    for b, r in enumerate(refs[:-2]):
        dm[b * tok : (b + 1) * tok, :] = r[...]
    batch_ref[...] = dot_nn(gated_ref[...], dm[...]).astype(bf16)


def batch_grad(gated, packs, width):
    rows, tokens = gated.shape
    tok = packs[0].shape[0]
    col = min(width, 1024)
    return pl.pallas_call(
        batch_kernel,
        grid=(width // col,),
        in_specs=[whole((rows, tokens))]
        + [pl.BlockSpec((tok, col), lambda i: (0, i))] * len(packs),
        out_specs=pl.BlockSpec((rows, col), lambda i: (0, i)),
        out_shape=jax.ShapeDtypeStruct((rows, width), bf16),
        scratch_shapes=[pltpu.VMEM((tokens, col), bf16)],
        compiler_params=pltpu.CompilerParams(vmem_limit_bytes=vmem_limit),
        cost_estimate=takes(4.6),
        name="batch_grad",
    )(gated, *packs)


def router_kernel(sp, cap, meta_ref, *refs):
    info_refs, moe_refs = refs[:2], refs[2:4]
    terms_in, out_ref, terms_ref = refs[4:]
    terms_ref[...] = jnp.sum(terms_in[...], axis=0)
    share, experts = out_ref.shape
    tok = 2 * info_refs[0].shape[0] // sp
    info = jnp.concatenate([r[...] for r in info_refs], axis=0)
    moe = jnp.concatenate([r[...] for r in moe_refs], axis=0)
    high = info[:, :experts]
    chosen = high >= 0
    prob = jnp.where(chosen, high.astype(f32) + info[:, experts:].astype(f32), 0.0)
    rank = dot_nn(earlier_same_block(tok * sp, tok), chosen.astype(bf16))
    pieces = []
    for b in range(sp):
        place = rank[b * tok : (b + 1) * tok, :]
        one = jnp.zeros((tok, experts), f32)
        for c in range(cap):
            row = terms_ref[pl.ds(c * sp + meta_ref[1 + b], 1), :]
            one = jnp.where(place == c, row, one)
        pieces.append(one)
    dgate = jnp.where(chosen, jnp.concatenate(pieces, axis=0), 0.0)
    dlogit = prob * (dgate - jnp.sum(prob * dgate, axis=-1, keepdims=True))
    a = dlogit.astype(bf16)
    rest = dlogit - a.astype(f32)
    b = rest.astype(bf16)
    c = (rest - b.astype(f32)).astype(bf16)
    wide = dot_tn(moe, jnp.concatenate([a, b, c], axis=1))
    total = wide[:, :experts] + wide[:, experts : 2 * experts] + wide[:, 2 * experts :]
    out_ref[...] = total.astype(bf16)


def router_grad(meta, packs, terms, width, experts, cap, sp):
    half, packed = packs[0].shape
    share = width // sp
    info_at = packed // (2 * experts) - 1
    info_spec = pl.BlockSpec((half, 2 * experts), lambda i, m: (0, info_at))
    moe_specs = [pl.BlockSpec((half, share), lambda i, m, c=c: (0, sp + c)) for c in range(2)]
    return pl.pallas_call(
        functools.partial(router_kernel, sp, cap),
        grid_spec=pltpu.PrefetchScalarGridSpec(
            num_scalar_prefetch=1,
            grid=(1,),
            in_specs=[info_spec] * 2 + moe_specs + [whole(terms.shape)],
            out_specs=whole((share, experts)),
            scratch_shapes=[pltpu.VMEM((cap * sp, experts), f32)],
        ),
        out_shape=jax.ShapeDtypeStruct((share, experts), bf16),
        compiler_params=pltpu.CompilerParams(vmem_limit_bytes=vmem_limit),
        cost_estimate=takes(3),
        name="router_grad",
    )(meta, *packs, *packs, terms)


def flipped(x, axis, size, k):
    return lax.ppermute(x, axis, [(i, i ^ k) for i in range(size)])


def sent_over(axis, size, x):
    if size & (size - 1):
        return [lax.psum(x.astype(f32), axis)]
    return [x] + [flipped(x, axis, size, k) for k in range(1, size)]


def tree_sum(terms):
    terms = [x.astype(f32) for x in terms]
    while len(terms) > 1:
        terms = [a + b for a, b in zip(terms[0::2], terms[1::2])]
    return terms[0]


def together(*arrays):
    return lax.optimization_barrier(arrays)


def on_device(
    q_pre,
    attn_out,
    d_attn,
    k_pre,
    values,
    q_gain,
    k_gain,
    offsets,
    moe_in,
    router,
    expert_ids,
    d_moe,
    expert_out,
):
    dp = lax.axis_size("dp")
    sp = lax.axis_size("sp")
    me = lax.axis_index("sp").astype(jnp.int32)
    other = jnp.bitwise_xor(me, 1)
    chips = sp // 2
    swap = [(i, i ^ 1) for i in range(sp)]

    def exchange(x):
        return lax.ppermute(x, "sp", swap)

    def to_chip(x, k):
        return flipped(x, "sp", sp, 2 * k)

    def both(mine):
        mine = jnp.concatenate(mine, axis=0)
        return [mine, exchange(mine)]

    steps = 2 * jnp.arange(chips, dtype=jnp.int32)
    owners = jnp.concatenate([jnp.bitwise_xor(me, steps), jnp.bitwise_xor(other, steps)])
    qg, kg = q_gain[None, :], k_gain[None, :]
    kv_heads = k_pre.shape[2] // q_gain.shape[0]
    width = moe_in.shape[2]
    experts = router.shape[1]
    place = jnp.stack([me // 2, jnp.bitwise_and(me, 1)])

    experts_here, _, cap, _ = expert_out.shape[1:]
    eout = jnp.transpose(expert_out[0], (0, 2, 1, 3)).reshape(experts_here * cap * sp, width)
    slot_meta = jnp.concatenate([(me * experts_here)[None], owners])
    meta = jnp.concatenate([offsets + me * q_pre.shape[1], owners])

    kv = pack_keys(k_pre[0], values[0], kg)
    if chips == 4:
        far = to_chip(kv, 2)
        kv = [kv, to_chip(kv, 1), far, to_chip(far, 1)]
    else:
        kv = [kv] + [to_chip(kv, k) for k in range(1, chips)]
    packs = gates(place, moe_in[0], router, expert_ids[0], d_moe[0], chips)
    kv, packs = together(kv, packs)

    packs = [packs[0]] + [to_chip(packs[k], k) for k in range(1, chips)]
    dq, own, keep, own_send, send = attend(
        meta, q_pre[0], attn_out[0], d_attn[0], qg, both(kv), sp, kv_heads
    )
    packs, own, keep, own_send, send = together(packs, own, keep, own_send, send)

    rows = k_pre.shape[1]
    arrived = exchange(send)
    sums = [
        (keep[k * rows : (k + 1) * rows] + arrived[k * rows : (k + 1) * rows].astype(f32)).astype(bf16)
        for k in range(chips - 1)
    ]
    packs, sums, own_send = together(packs, sums, own_send)

    sums = [to_chip(sums[k - 1], k) for k in range(1, chips)]
    sums = [own, exchange(own_send)] + sums
    packs = both(packs)
    gated, terms = slot_terms(slot_meta, packs, eout, experts, cap, sp)
    terms = lax.all_to_all(terms, "sp", split_axis=0, concat_axis=0, tiled=True)
    batch = batch_grad(gated, packs, width)
    routed = router_grad(slot_meta, packs, terms, width, experts, cap, sp)
    sums, routed, batch = together(sums, routed, batch)

    routed = sent_over("dp", dp, routed)
    dk, dv = finish_keys(k_pre[0], kg, sums)
    batch = jnp.transpose(batch.reshape(experts_here, cap, sp, width), (0, 2, 1, 3))
    return (dq[None], dk[None], dv[None], batch[None], tree_sum(routed))


def solution(mesh):
    in_specs = (
        P("dp", "sp", None),
        P("dp", "sp", None),
        P("dp", "sp", None),
        P("dp", "sp", None),
        P("dp", "sp", None),
        P(),
        P(),
        P("dp"),
        P("dp", "sp", None),
        P(),
        P("dp", "sp", None),
        P("dp", "sp", None),
        P("dp", "sp", None, None, None),
    )
    out_specs = (
        P("dp", "sp", None),
        P("dp", "sp", None),
        P("dp", "sp", None),
        P("dp", "sp", None, None, None),
        P("sp", None),
    )
    return jax.shard_map(
        on_device, mesh=mesh, in_specs=in_specs, out_specs=out_specs, check_vma=False
    )
```

```python
import functools
import math

import jax
import jax.numpy as jnp
import numpy as np
from jax import lax
from jax.experimental import pallas as pl
from jax.experimental.pallas import tpu as pltpu
from jax.sharding import PartitionSpec as P

norm_eps = 1e-06
f32 = jnp.float32
bf16 = jnp.bfloat16
vmem_limit = 56 * 1024 * 1024


def takes(us):
    flops = int(us * 1.15e9)
    return pl.CostEstimate(flops=flops, transcendentals=0, bytes_accessed=int(us * 3.6e6))


def dot_nt(a, b):
    return lax.dot_general(a, b, (((1,), (1,)), ((), ())), preferred_element_type=f32)


def dot_nn(a, b):
    return lax.dot_general(a, b, (((1,), (0,)), ((), ())), preferred_element_type=f32)


def dot_tn(a, b):
    return lax.dot_general(a, b, (((0,), (0,)), ((), ())), preferred_element_type=f32)


def whole(shape):
    return pl.BlockSpec(shape, lambda *_: (0,) * len(shape))


def keys_kernel(k_ref, v_ref, gain_ref, kv_ref):
    hd = gain_ref.shape[1]
    gain = gain_ref[...]
    for g in range(k_ref.shape[1] // hd):
        k = k_ref[:, g * hd : (g + 1) * hd].astype(f32)
        inv = lax.rsqrt(jnp.mean(k * k, axis=-1, keepdims=True) + norm_eps)
        kv_ref[:, 2 * g * hd : (2 * g + 1) * hd] = ((k * inv) * gain).astype(bf16)
        kv_ref[:, (2 * g + 1) * hd : (2 * g + 2) * hd] = v_ref[:, g * hd : (g + 1) * hd]


def pack_keys(k_pre, values, k_gain):
    rows, width = k_pre.shape
    return pl.pallas_call(
        keys_kernel,
        out_shape=jax.ShapeDtypeStruct((rows, 2 * width), bf16),
        cost_estimate=takes(1.8),
        name="pack_keys",
    )(k_pre, values, k_gain)


def gates_kernel(chips, meta_ref, moe_ref, router_ref, ids_ref, dmoe_ref, *pack_refs):
    tok, width = moe_ref.shape
    experts = router_ref.shape[1]
    logits = dot_nn(moe_ref[...], router_ref[...])
    lane = lax.broadcasted_iota(jnp.int32, (tok, experts), 1)
    chosen = lane == ids_ref[:, 0:1]
    for k in range(1, ids_ref.shape[1]):
        chosen = jnp.logical_or(chosen, lane == ids_ref[:, k : k + 1])
    weights = jnp.where(chosen, jnp.exp(logits), 0.0)
    probs = weights / jnp.sum(weights, axis=-1, keepdims=True)
    high = probs.astype(bf16)
    low = (probs - high.astype(f32)).astype(bf16)
    coded = jnp.where(chosen, high.astype(f32), -1.0).astype(bf16)
    share = width // (2 * chips)
    chip, core = meta_ref[0], meta_ref[1]
    d_all = dmoe_ref[...]
    for k, ref in enumerate(pack_refs):
        ref[:, :width] = d_all
        ref[:, width + 2 * share : width + 2 * share + experts] = coded
        ref[:, width + 2 * share + experts : width + 2 * share + 2 * experts] = low
        to = jnp.bitwise_xor(chip, k) * 2
        for i in range(2):
            at = pl.multiple_of((to + jnp.bitwise_xor(core, i)) * share, 128)
            ref[:, width + i * share : width + (i + 1) * share] = moe_ref[:, pl.ds(at, share)]


def gates(meta, moe_in, router, ids, d_moe, chips):
    tok, width = moe_in.shape
    experts = router.shape[1]
    vm = pl.BlockSpec(memory_space=pltpu.VMEM)
    packed = width + width // chips + 2 * experts
    return pl.pallas_call(
        functools.partial(gates_kernel, chips),
        in_specs=[pl.BlockSpec(memory_space=pltpu.SMEM)] + [vm] * 4,
        out_shape=[jax.ShapeDtypeStruct((tok, packed), bf16)] * chips,
        compiler_params=pltpu.CompilerParams(vmem_limit_bytes=vmem_limit),
        cost_estimate=takes(2.8),
        name="gates",
    )(meta, moe_in, router, ids, d_moe)


def attend_kernel(blocks, meta_ref, q_ref, o_ref, do_ref, gain_ref, *refs):
    kv_refs = refs[:2]
    dq_ref = refs[-5]
    part_refs = refs[-4:]
    tok = q_ref.shape[0]
    hd = gain_ref.shape[1]
    heads = q_ref.shape[1] // hd
    kb = 2 * kv_refs[0].shape[0] // blocks
    keys = kb * blocks
    scale = hd ** (-0.5)
    offset = meta_ref[0]
    gain = gain_ref[...]
    key = jnp.concatenate([r[:, :hd] for r in kv_refs], axis=0)
    val = jnp.concatenate([r[:, hd:] for r in kv_refs], axis=0)
    pos = jnp.concatenate(
        [
            meta_ref[1 + b] * kb + lax.broadcasted_iota(jnp.int32, (kb, 1), 0)
            for b in range(blocks)
        ],
        axis=0,
    )
    step_heads = min(heads, max(128 // tok, heads * 1024 // keys))
    rows = step_heads * tok
    limit = offset + lax.rem(lax.broadcasted_iota(jnp.int32, (1, rows), 1), tok)
    visible = pos <= limit
    dk = dv = None
    for h0 in range(0, heads, step_heads):

        def stack(ref):
            return jnp.concatenate(
                [ref[:, h * hd : (h + 1) * hd] for h in range(h0, h0 + step_heads)], axis=0
            )

        q = stack(q_ref).astype(f32)
        do = stack(do_ref)
        prod = do.astype(f32) * stack(o_ref).astype(f32)
        delta = jnp.sum(prod.T, axis=0, keepdims=True)
        inv = lax.rsqrt(jnp.mean(q * q, axis=-1, keepdims=True) + norm_eps)
        unit = q * inv
        q_hat = (unit * gain).astype(bf16)
        scores = dot_nt(key, q_hat)
        ex = jnp.where(visible, jnp.exp2(scores * (scale * math.log2(math.e))), 0.0)
        probs = ex * (1.0 / jnp.sum(ex, axis=0, keepdims=True))
        dv_one = dot_nn(probs.astype(bf16), do)
        dprobs = dot_nt(val, do)
        ds = ((probs * scale) * (dprobs - delta)).astype(bf16)
        dk_one = dot_nn(ds, q_hat)
        dq = dot_tn(key, ds).T
        c = dq * gain
        dq_pre = (inv * (c - unit * jnp.mean(c * unit, axis=-1, keepdims=True))).astype(bf16)
        for i in range(step_heads):
            h = h0 + i
            dq_ref[:, h * hd : (h + 1) * hd] = dq_pre[i * tok : (i + 1) * tok, :]
        dk = dk_one if dk is None else dk + dk_one
        dv = dv_one if dv is None else dv + dv_one
    at = 0
    for ref in part_refs:
        size = ref.shape[0]
        ref[:, :hd] = dk[at : at + size, :].astype(ref.dtype)
        ref[:, hd:] = dv[at : at + size, :].astype(ref.dtype)
        at += size


def attend(meta, q, o, do, gain, kv_halves, blocks, kv_heads):
    tok, width = q.shape
    hd = gain.shape[1]
    half, kv_width = kv_halves[0].shape
    step = width // kv_heads
    row_spec = pl.BlockSpec((tok, step), lambda g, m: (0, g))
    part_spec = pl.BlockSpec((half, 2 * hd), lambda g, m: (0, g))
    own = 2 * half // blocks
    sizes = (own, half - own) * 2
    return pl.pallas_call(
        functools.partial(attend_kernel, blocks),
        grid_spec=pltpu.PrefetchScalarGridSpec(
            num_scalar_prefetch=1,
            grid=(kv_width // (2 * hd),),
            in_specs=[row_spec] * 3
            + [whole((1, hd))]
            + [part_spec] * 2,
            out_specs=[row_spec] + [pl.BlockSpec((n, 2 * hd), lambda g, m: (0, g)) for n in sizes],
        ),
        out_shape=[
            jax.ShapeDtypeStruct((tok, width), bf16),
            jax.ShapeDtypeStruct((sizes[0], kv_width), f32),
            jax.ShapeDtypeStruct((sizes[1], kv_width), f32),
            jax.ShapeDtypeStruct((sizes[2], kv_width), bf16),
            jax.ShapeDtypeStruct((sizes[3], kv_width), bf16),
        ],
        compiler_params=pltpu.CompilerParams(vmem_limit_bytes=vmem_limit),
        cost_estimate=takes(10),
        name="attend",
    )(meta, q, o, do, gain, *kv_halves)


def finish_kernel(chips, k_ref, gain_ref, own_ref, other_ref, *refs):
    first, rest = refs[: chips - 1], refs[chips - 1 : -2]
    dk_ref, dv_ref = refs[-2:]
    hd = gain_ref.shape[1]
    gain = gain_ref[...]
    cut = first[0].shape[1]
    for g in range(k_ref.shape[1] // hd):
        at = 2 * g * hd
        total = own_ref[:, at : at + 2 * hd] + other_ref[:, at : at + 2 * hd].astype(f32)
        parts, start = (first, at) if at < cut else (rest, at - cut)
        for r in parts:
            total = total + r[:, start : start + 2 * hd].astype(f32)
        k = k_ref[:, g * hd : (g + 1) * hd].astype(f32)
        inv = lax.rsqrt(jnp.mean(k * k, axis=-1, keepdims=True) + norm_eps)
        unit = k * inv
        c = total[:, :hd] * gain
        dk = inv * (c - unit * jnp.mean(c * unit, axis=-1, keepdims=True))
        dk_ref[:, g * hd : (g + 1) * hd] = dk.astype(bf16)
        dv_ref[:, g * hd : (g + 1) * hd] = total[:, hd:].astype(bf16)


def finish_keys(k_pre, k_gain, own, first, rest):
    out = jax.ShapeDtypeStruct(k_pre.shape, bf16)
    return pl.pallas_call(
        functools.partial(finish_kernel, len(first) + 1),
        out_shape=(out, out),
        compiler_params=pltpu.CompilerParams(vmem_limit_bytes=vmem_limit),
        cost_estimate=takes(2.2),
        name="finish_keys",
    )(k_pre, k_gain, *own, *first, *rest)


def earlier_same_block(rows, block):
    i = lax.broadcasted_iota(jnp.int32, (rows, rows), 0)
    j = lax.broadcasted_iota(jnp.int32, (rows, rows), 1)
    same = lax.div(i, block) == lax.div(j, block)
    return jnp.where(jnp.logical_and(same, j < i), 1.0, 0.0).astype(bf16)


def terms_kernel(blocks, sp, cap, meta_ref, table_ref, lanes_ref, *refs):
    d_refs = refs[:2]
    g_refs = refs[2:4]
    eout_ref, gated_ref, terms_ref, dm, hit_scr, acc = refs[4:]
    half = d_refs[0].shape[0]
    tokens = 2 * half
    tok = tokens // blocks
    experts = g_refs[0].shape[1]
    rows = eout_ref.shape[0]
    step = pl.program_id(0)

    def pick():
        expert = meta_ref[0] + table_ref[:, 0:1]
        return lax.broadcasted_iota(jnp.int32, (rows, experts), 1) == expert

    @pl.when(step == 0)
    def _():
        coded = jnp.concatenate([r[...] for r in g_refs], axis=0)
        chosen = (coded >= 0).astype(bf16)
        rank = dot_nn(earlier_same_block(tokens, tok), chosen)
        sel = jnp.where(pick(), 1.0, 0.0).astype(bf16)
        gate = dot_nt(sel, coded)
        place = dot_nt(sel, rank.astype(bf16))
        lane_block = lax.div(lax.broadcasted_iota(jnp.int32, (1, tokens), 1), tok)
        source = jnp.zeros((1, tokens), jnp.int32)
        for b in range(blocks):
            source = jnp.where(lane_block == b, meta_ref[1 + b], source)
        hit = jnp.logical_and(
            jnp.logical_and(gate >= 0.0, place == table_ref[:, 1:2].astype(f32)),
            source == table_ref[:, 2:3],
        )
        gated_ref[...] = jnp.where(hit, gate, 0.0).astype(bf16)
        hit_scr[...] = jnp.where(hit, 1.0, 0.0)
        acc[...] = jnp.zeros_like(acc)

    for i in range(2):
        dm[i * half : (i + 1) * half, :] = d_refs[i][...]
    acc[...] += dot_nt(eout_ref[...], dm[...])

    @pl.when(step == pl.num_programs(0) - 1)
    def _():
        terms = jnp.sum(acc[...] * hit_scr[...], axis=-1, keepdims=True)
        placed = jnp.where(pick(), terms, 0.0)
        want = lax.broadcasted_iota(jnp.int32, (cap * sp, rows), 0)
        fold = jnp.where(want == lanes_ref[...], 1.0, 0.0)
        folded = lax.dot_general(
            fold,
            placed,
            (((1,), (0,)), ((), ())),
            precision=lax.Precision.HIGHEST,
            preferred_element_type=f32,
        )
        for to in range(terms_ref.shape[0]):
            terms_ref[to] = folded


def slot_terms(meta, packs, eout, experts, cap, sp):
    rows, width = eout.shape
    half, packed = packs[0].shape
    blocks = sp
    r = np.arange(rows)
    e, c, s = r // (cap * sp), (r // sp) % cap, r % sp
    table = jnp.asarray(np.stack([e, c, s], axis=1), jnp.int32)
    lanes = jnp.asarray((c * sp + s)[None, :], jnp.int32)
    col = min(width, 2048)
    tokens = 2 * half
    gate_at = (packed - 2 * experts) // experts
    d_spec = pl.BlockSpec((half, col), lambda i, m: (0, i))
    g_spec = pl.BlockSpec((half, experts), lambda i, m: (0, gate_at))
    e_spec = pl.BlockSpec((rows, col), lambda i, m: (0, i))
    return pl.pallas_call(
        functools.partial(terms_kernel, blocks, sp, cap),
        grid_spec=pltpu.PrefetchScalarGridSpec(
            num_scalar_prefetch=1,
            grid=(width // col,),
            in_specs=[whole((rows, 3)), whole((1, rows))]
            + [d_spec] * 2
            + [g_spec] * 2
            + [e_spec],
            out_specs=[whole((rows, tokens)), whole((sp, cap * sp, experts))],
            scratch_shapes=[
                pltpu.VMEM((tokens, col), bf16),
                pltpu.VMEM((rows, tokens), f32),
                pltpu.VMEM((rows, tokens), f32),
            ],
        ),
        out_shape=[
            jax.ShapeDtypeStruct((rows, tokens), bf16),
            jax.ShapeDtypeStruct((sp, cap * sp, experts), f32),
        ],
        compiler_params=pltpu.CompilerParams(vmem_limit_bytes=vmem_limit),
        cost_estimate=takes(6.2),
        name="slot_terms",
    )(meta, table, lanes, *packs, *packs, eout)


def batch_kernel(gated_ref, *refs):
    batch_ref, dm = refs[-2:]
    tok = refs[0].shape[0]
    for b, r in enumerate(refs[:-2]):
        dm[b * tok : (b + 1) * tok, :] = r[...]
    batch_ref[...] = dot_nn(gated_ref[...], dm[...]).astype(bf16)


def batch_grad(gated, packs, width):
    rows, tokens = gated.shape
    tok = packs[0].shape[0]
    col = min(width, 2048)
    return pl.pallas_call(
        batch_kernel,
        grid=(width // col,),
        in_specs=[whole((rows, tokens))]
        + [pl.BlockSpec((tok, col), lambda i: (0, i))] * len(packs),
        out_specs=pl.BlockSpec((rows, col), lambda i: (0, i)),
        out_shape=jax.ShapeDtypeStruct((rows, width), bf16),
        scratch_shapes=[pltpu.VMEM((tokens, col), bf16)],
        compiler_params=pltpu.CompilerParams(vmem_limit_bytes=vmem_limit),
        cost_estimate=takes(4.6),
        name="batch_grad",
    )(gated, *packs)


def router_kernel(sp, cap, meta_ref, *refs):
    info_refs, moe_refs = refs[:2], refs[2:4]
    terms_in, out_ref, terms_ref = refs[4:]
    terms_ref[...] = jnp.sum(terms_in[...], axis=0)
    share, experts = out_ref.shape
    tok = 2 * info_refs[0].shape[0] // sp
    info = jnp.concatenate([r[...] for r in info_refs], axis=0)
    moe = jnp.concatenate([r[...] for r in moe_refs], axis=0)
    high = info[:, :experts]
    chosen = high >= 0
    prob = jnp.where(chosen, high.astype(f32) + info[:, experts:].astype(f32), 0.0)
    rank = dot_nn(earlier_same_block(tok * sp, tok), chosen.astype(bf16))
    pieces = []
    for b in range(sp):
        place = rank[b * tok : (b + 1) * tok, :]
        one = jnp.zeros((tok, experts), f32)
        for c in range(cap):
            row = terms_ref[pl.ds(c * sp + meta_ref[1 + b], 1), :]
            one = jnp.where(place == c, row, one)
        pieces.append(one)
    dgate = jnp.where(chosen, jnp.concatenate(pieces, axis=0), 0.0)
    dlogit = prob * (dgate - jnp.sum(prob * dgate, axis=-1, keepdims=True))
    a = dlogit.astype(bf16)
    rest = dlogit - a.astype(f32)
    b = rest.astype(bf16)
    c = (rest - b.astype(f32)).astype(bf16)
    wide = dot_tn(moe, jnp.concatenate([a, b, c], axis=1))
    total = wide[:, :experts] + wide[:, experts : 2 * experts] + wide[:, 2 * experts :]
    out_ref[...] = total.astype(bf16)


def router_grad(meta, packs, terms, width, experts, cap, sp):
    half, packed = packs[0].shape
    share = width // sp
    info_at = packed // (2 * experts) - 1
    info_spec = pl.BlockSpec((half, 2 * experts), lambda i, m: (0, info_at))
    moe_specs = [pl.BlockSpec((half, share), lambda i, m, c=c: (0, sp + c)) for c in range(2)]
    return pl.pallas_call(
        functools.partial(router_kernel, sp, cap),
        grid_spec=pltpu.PrefetchScalarGridSpec(
            num_scalar_prefetch=1,
            grid=(1,),
            in_specs=[info_spec] * 2 + moe_specs + [whole(terms.shape)],
            out_specs=whole((share, experts)),
            scratch_shapes=[pltpu.VMEM((cap * sp, experts), f32)],
        ),
        out_shape=jax.ShapeDtypeStruct((share, experts), bf16),
        compiler_params=pltpu.CompilerParams(vmem_limit_bytes=vmem_limit),
        cost_estimate=takes(3),
        name="router_grad",
    )(meta, *packs, *packs, terms)


def flipped(x, axis, size, k):
    return lax.ppermute(x, axis, [(i, i ^ k) for i in range(size)])


def sent_over(axis, size, x):
    if size & (size - 1):
        return [lax.psum(x.astype(f32), axis)]
    return [x] + [flipped(x, axis, size, k) for k in range(1, size)]


def tree_sum(terms):
    terms = [x.astype(f32) for x in terms]
    while len(terms) > 1:
        terms = [a + b for a, b in zip(terms[0::2], terms[1::2])]
    return terms[0]


def together(*arrays):
    return lax.optimization_barrier(arrays)


def on_device(
    q_pre,
    attn_out,
    d_attn,
    k_pre,
    values,
    q_gain,
    k_gain,
    offsets,
    moe_in,
    router,
    expert_ids,
    d_moe,
    expert_out,
):
    dp = lax.axis_size("dp")
    sp = lax.axis_size("sp")
    me = lax.axis_index("sp").astype(jnp.int32)
    other = jnp.bitwise_xor(me, 1)
    chips = sp // 2
    swap = [(i, i ^ 1) for i in range(sp)]

    def exchange(x):
        return lax.ppermute(x, "sp", swap)

    def to_chip(x, k):
        return flipped(x, "sp", sp, 2 * k)

    def both(mine):
        mine = jnp.concatenate(mine, axis=0)
        return [mine, exchange(mine)]

    steps = 2 * jnp.arange(chips, dtype=jnp.int32)
    owners = jnp.concatenate([jnp.bitwise_xor(me, steps), jnp.bitwise_xor(other, steps)])
    qg, kg = q_gain[None, :], k_gain[None, :]
    kv_heads = k_pre.shape[2] // q_gain.shape[0]
    width = moe_in.shape[2]
    experts = router.shape[1]
    place = jnp.stack([me // 2, jnp.bitwise_and(me, 1)])

    experts_here, _, cap, _ = expert_out.shape[1:]
    eout = jnp.transpose(expert_out[0], (0, 2, 1, 3)).reshape(experts_here * cap * sp, width)
    slot_meta = jnp.concatenate([(me * experts_here)[None], owners])
    meta = jnp.concatenate([offsets + me * q_pre.shape[1], owners])

    kv = pack_keys(k_pre[0], values[0], kg)
    if chips == 4:
        far = to_chip(kv, 2)
        kv = [kv, to_chip(kv, 1), far, to_chip(far, 1)]
    else:
        kv = [kv] + [to_chip(kv, k) for k in range(1, chips)]
    packs = gates(place, moe_in[0], router, expert_ids[0], d_moe[0], chips)
    kv, packs = together(kv, packs)

    packs = [packs[0]] + [to_chip(packs[k], k) for k in range(1, chips)]
    dq, own, keep, own_send, send = attend(
        meta, q_pre[0], attn_out[0], d_attn[0], qg, both(kv), sp, kv_heads
    )
    packs, own, keep, own_send, send = together(packs, own, keep, own_send, send)

    rows = k_pre.shape[1]
    arrived = exchange(send)
    sums = [
        (keep[k * rows : (k + 1) * rows] + arrived[k * rows : (k + 1) * rows].astype(f32)).astype(bf16)
        for k in range(chips - 1)
    ]
    cut = (kv_heads // 2) * 2 * q_gain.shape[0]
    first, rest = [x[:, :cut] for x in sums], [x[:, cut:] for x in sums]
    packs, first, rest, own_send = together(packs, first, rest, own_send)

    own_arrived = exchange(own_send)
    first = [to_chip(first[k - 1], k) for k in range(1, chips)]
    packs = both(packs)
    gated, terms = slot_terms(slot_meta, packs, eout, experts, cap, sp)
    terms = lax.all_to_all(terms, "sp", split_axis=0, concat_axis=0, tiled=True)
    batch = batch_grad(gated, packs, width)
    own_arrived, first, rest, terms, batch = together(own_arrived, first, rest, terms, batch)

    rest = [to_chip(rest[k - 1], k) for k in range(1, chips)]
    routed = router_grad(slot_meta, packs, terms, width, experts, cap, sp)
    routed = sent_over("dp", dp, routed)
    dk, dv = finish_keys(k_pre[0], kg, [own, own_arrived], first, rest)
    dk, dv, routed = together(dk, dv, routed)
    batch = jnp.transpose(batch.reshape(experts_here, cap, sp, width), (0, 2, 1, 3))
    return (dq[None], dk[None], dv[None], batch[None], tree_sum(routed))


def solution(mesh):
    in_specs = (
        P("dp", "sp", None),
        P("dp", "sp", None),
        P("dp", "sp", None),
        P("dp", "sp", None),
        P("dp", "sp", None),
        P(),
        P(),
        P("dp"),
        P("dp", "sp", None),
        P(),
        P("dp", "sp", None),
        P("dp", "sp", None),
        P("dp", "sp", None, None, None),
    )
    out_specs = (
        P("dp", "sp", None),
        P("dp", "sp", None),
        P("dp", "sp", None),
        P("dp", "sp", None, None, None),
        P("sp", None),
    )
    return jax.shard_map(
        on_device, mesh=mesh, in_specs=in_specs, out_specs=out_specs, check_vma=False
    )
```

```python
import functools
import math

import jax
import jax.numpy as jnp
import numpy as np
from jax import lax
from jax.experimental import pallas as pl
from jax.experimental.pallas import tpu as pltpu
from jax.sharding import PartitionSpec as P

norm_eps = 1e-06
f32 = jnp.float32
bf16 = jnp.bfloat16
mib = 1024 * 1024


def takes(us):
    flops = int(us * 1.15e9)
    return pl.CostEstimate(flops=flops, transcendentals=0, bytes_accessed=int(us * 3.6e6))


def dot_nt(a, b):
    return lax.dot_general(a, b, (((1,), (1,)), ((), ())), preferred_element_type=f32)


def dot_nn(a, b):
    return lax.dot_general(a, b, (((1,), (0,)), ((), ())), preferred_element_type=f32)


def dot_tn(a, b):
    return lax.dot_general(a, b, (((0,), (0,)), ((), ())), preferred_element_type=f32)


def whole(shape):
    return pl.BlockSpec(shape, lambda *_: (0,) * len(shape))


def keys_kernel(k_ref, v_ref, gain_ref, kv_ref):
    hd = gain_ref.shape[1]
    gain = gain_ref[...]
    for g in range(k_ref.shape[1] // hd):
        k = k_ref[:, g * hd : (g + 1) * hd].astype(f32)
        inv = lax.rsqrt(jnp.mean(k * k, axis=-1, keepdims=True) + norm_eps)
        kv_ref[:, 2 * g * hd : (2 * g + 1) * hd] = ((k * inv) * gain).astype(bf16)
        kv_ref[:, (2 * g + 1) * hd : (2 * g + 2) * hd] = v_ref[:, g * hd : (g + 1) * hd]


def pack_keys(k_pre, values, k_gain):
    rows, width = k_pre.shape
    return pl.pallas_call(
        keys_kernel,
        out_shape=jax.ShapeDtypeStruct((rows, 2 * width), bf16),
        cost_estimate=takes(1.8),
        name="pack_keys",
    )(k_pre, values, k_gain)


def gates_kernel(chips, meta_ref, moe_ref, router_ref, ids_ref, dmoe_ref, *pack_refs):
    tok, width = moe_ref.shape
    experts = router_ref.shape[1]
    logits = dot_nn(moe_ref[...], router_ref[...])
    lane = lax.broadcasted_iota(jnp.int32, (tok, experts), 1)
    chosen = lane == ids_ref[:, 0:1]
    for k in range(1, ids_ref.shape[1]):
        chosen = jnp.logical_or(chosen, lane == ids_ref[:, k : k + 1])
    weights = jnp.where(chosen, jnp.exp(logits), 0.0)
    probs = weights / jnp.sum(weights, axis=-1, keepdims=True)
    high = probs.astype(bf16)
    low = (probs - high.astype(f32)).astype(bf16)
    coded = jnp.where(chosen, high.astype(f32), -1.0).astype(bf16)
    share = width // (2 * chips)
    chip, core = meta_ref[0], meta_ref[1]
    d_all = dmoe_ref[...]
    for k, ref in enumerate(pack_refs):
        ref[:, :width] = d_all
        ref[:, width + 2 * share : width + 2 * share + experts] = coded
        ref[:, width + 2 * share + experts : width + 2 * share + 2 * experts] = low
        to = jnp.bitwise_xor(chip, k) * 2
        for i in range(2):
            at = pl.multiple_of((to + jnp.bitwise_xor(core, i)) * share, 128)
            ref[:, width + i * share : width + (i + 1) * share] = moe_ref[:, pl.ds(at, share)]


def gates(meta, moe_in, router, ids, d_moe, chips):
    tok, width = moe_in.shape
    experts = router.shape[1]
    vm = pl.BlockSpec(memory_space=pltpu.VMEM)
    packed = width + width // chips + 2 * experts
    return pl.pallas_call(
        functools.partial(gates_kernel, chips),
        in_specs=[pl.BlockSpec(memory_space=pltpu.SMEM)] + [vm] * 4,
        out_shape=[jax.ShapeDtypeStruct((tok, packed), bf16)] * chips,
        compiler_params=pltpu.CompilerParams(vmem_limit_bytes=8 * mib),
        cost_estimate=takes(2.8),
        name="gates",
    )(meta, moe_in, router, ids, d_moe)


def attend_kernel(blocks, meta_ref, q_ref, o_ref, do_ref, gain_ref, *refs):
    kv_refs = refs[:2]
    dq_ref = refs[-5]
    part_refs = refs[-4:]
    tok = q_ref.shape[0]
    hd = gain_ref.shape[1]
    heads = q_ref.shape[1] // hd
    kb = 2 * kv_refs[0].shape[0] // blocks
    keys = kb * blocks
    scale = hd ** (-0.5)
    offset = meta_ref[0]
    gain = gain_ref[...]
    key = jnp.concatenate([r[:, :hd] for r in kv_refs], axis=0)
    val = jnp.concatenate([r[:, hd:] for r in kv_refs], axis=0)
    pos = jnp.concatenate(
        [
            meta_ref[1 + b] * kb + lax.broadcasted_iota(jnp.int32, (kb, 1), 0)
            for b in range(blocks)
        ],
        axis=0,
    )
    step_heads = min(heads, max(128 // tok, heads * 1024 // keys))
    rows = step_heads * tok
    limit = offset + lax.rem(lax.broadcasted_iota(jnp.int32, (1, rows), 1), tok)
    visible = pos <= limit
    dk = dv = None
    for h0 in range(0, heads, step_heads):

        def stack(ref):
            return jnp.concatenate(
                [ref[:, h * hd : (h + 1) * hd] for h in range(h0, h0 + step_heads)], axis=0
            )

        q = stack(q_ref).astype(f32)
        do = stack(do_ref)
        prod = do.astype(f32) * stack(o_ref).astype(f32)
        delta = jnp.sum(prod.T, axis=0, keepdims=True)
        inv = lax.rsqrt(jnp.mean(q * q, axis=-1, keepdims=True) + norm_eps)
        unit = q * inv
        q_hat = (unit * gain).astype(bf16)
        scores = dot_nt(key, q_hat)
        ex = jnp.where(visible, jnp.exp2(scores * (scale * math.log2(math.e))), 0.0)
        probs = ex * (1.0 / jnp.sum(ex, axis=0, keepdims=True))
        dv_one = dot_nn(probs.astype(bf16), do)
        dprobs = dot_nt(val, do)
        ds = ((probs * scale) * (dprobs - delta)).astype(bf16)
        dk_one = dot_nn(ds, q_hat)
        dq = dot_tn(key, ds).T
        c = dq * gain
        dq_pre = (inv * (c - unit * jnp.mean(c * unit, axis=-1, keepdims=True))).astype(bf16)
        for i in range(step_heads):
            h = h0 + i
            dq_ref[:, h * hd : (h + 1) * hd] = dq_pre[i * tok : (i + 1) * tok, :]
        dk = dk_one if dk is None else dk + dk_one
        dv = dv_one if dv is None else dv + dv_one
    at = 0
    for ref in part_refs:
        size = ref.shape[0]
        ref[:, :hd] = dk[at : at + size, :].astype(ref.dtype)
        ref[:, hd:] = dv[at : at + size, :].astype(ref.dtype)
        at += size


def attend(meta, q, o, do, gain, kv_halves, blocks, kv_heads):
    tok, width = q.shape
    hd = gain.shape[1]
    half, kv_width = kv_halves[0].shape
    step = width // kv_heads
    row_spec = pl.BlockSpec((tok, step), lambda g, m: (0, g))
    part_spec = pl.BlockSpec((half, 2 * hd), lambda g, m: (0, g))
    own = 2 * half // blocks
    sizes = (own, half - own) * 2
    return pl.pallas_call(
        functools.partial(attend_kernel, blocks),
        grid_spec=pltpu.PrefetchScalarGridSpec(
            num_scalar_prefetch=1,
            grid=(kv_width // (2 * hd),),
            in_specs=[row_spec] * 3
            + [whole((1, hd))]
            + [part_spec] * 2,
            out_specs=[row_spec] + [pl.BlockSpec((n, 2 * hd), lambda g, m: (0, g)) for n in sizes],
        ),
        out_shape=[
            jax.ShapeDtypeStruct((tok, width), bf16),
            jax.ShapeDtypeStruct((sizes[0], kv_width), f32),
            jax.ShapeDtypeStruct((sizes[1], kv_width), f32),
            jax.ShapeDtypeStruct((sizes[2], kv_width), bf16),
            jax.ShapeDtypeStruct((sizes[3], kv_width), bf16),
        ],
        compiler_params=pltpu.CompilerParams(vmem_limit_bytes=32 * mib),
        cost_estimate=takes(10),
        name="attend",
    )(meta, q, o, do, gain, *kv_halves)


def pair_kernel(keep_ref, other_ref, *out_refs):
    rows, cut = out_refs[0].shape
    blocks = len(out_refs) // 2
    for k in range(blocks):
        at = k * rows
        total = keep_ref[at : at + rows, :] + other_ref[at : at + rows, :].astype(f32)
        out_refs[k][...] = total[:, :cut].astype(bf16)
        out_refs[blocks + k][...] = total[:, cut:].astype(bf16)


def pair_sums(keep, other, rows, kv_heads):
    blocks = keep.shape[0] // rows
    width = keep.shape[1]
    cut = (kv_heads // 2) * (width // kv_heads)
    sums = pl.pallas_call(
        pair_kernel,
        out_shape=[jax.ShapeDtypeStruct((rows, cut), bf16)] * blocks
        + [jax.ShapeDtypeStruct((rows, width - cut), bf16)] * blocks,
        compiler_params=pltpu.CompilerParams(vmem_limit_bytes=32 * mib),
        cost_estimate=takes(1),
        name="pair_sums",
    )(keep, other)
    return sums[:blocks], sums[blocks:]


def finish_kernel(chips, k_ref, gain_ref, own_ref, other_ref, *refs):
    first, rest = refs[: chips - 1], refs[chips - 1 : -2]
    dk_ref, dv_ref = refs[-2:]
    hd = gain_ref.shape[1]
    gain = gain_ref[...]
    cut = first[0].shape[1]
    for g in range(k_ref.shape[1] // hd):
        at = 2 * g * hd
        total = own_ref[:, at : at + 2 * hd] + other_ref[:, at : at + 2 * hd].astype(f32)
        parts, start = (first, at) if at < cut else (rest, at - cut)
        for r in parts:
            total = total + r[:, start : start + 2 * hd].astype(f32)
        k = k_ref[:, g * hd : (g + 1) * hd].astype(f32)
        inv = lax.rsqrt(jnp.mean(k * k, axis=-1, keepdims=True) + norm_eps)
        unit = k * inv
        c = total[:, :hd] * gain
        dk = inv * (c - unit * jnp.mean(c * unit, axis=-1, keepdims=True))
        dk_ref[:, g * hd : (g + 1) * hd] = dk.astype(bf16)
        dv_ref[:, g * hd : (g + 1) * hd] = total[:, hd:].astype(bf16)


def finish_keys(k_pre, k_gain, own, first, rest):
    out = jax.ShapeDtypeStruct(k_pre.shape, bf16)
    return pl.pallas_call(
        functools.partial(finish_kernel, len(first) + 1),
        out_shape=(out, out),
        compiler_params=pltpu.CompilerParams(vmem_limit_bytes=8 * mib),
        cost_estimate=takes(2.2),
        name="finish_keys",
    )(k_pre, k_gain, *own, *first, *rest)


def earlier_same_block(rows, block):
    i = lax.broadcasted_iota(jnp.int32, (rows, rows), 0)
    j = lax.broadcasted_iota(jnp.int32, (rows, rows), 1)
    same = lax.div(i, block) == lax.div(j, block)
    return jnp.where(jnp.logical_and(same, j < i), 1.0, 0.0).astype(bf16)


def terms_kernel(blocks, sp, cap, meta_ref, table_ref, lanes_ref, *refs):
    d_refs = refs[:2]
    g_refs = refs[2:4]
    eout_ref, gated_ref, terms_ref, dm, hit_scr, acc = refs[4:]
    half = d_refs[0].shape[0]
    tokens = 2 * half
    tok = tokens // blocks
    experts = g_refs[0].shape[1]
    rows = eout_ref.shape[0]
    step = pl.program_id(0)

    def pick():
        expert = meta_ref[0] + table_ref[:, 0:1]
        return lax.broadcasted_iota(jnp.int32, (rows, experts), 1) == expert

    @pl.when(step == 0)
    def _():
        coded = jnp.concatenate([r[...] for r in g_refs], axis=0)
        chosen = (coded >= 0).astype(bf16)
        rank = dot_nn(earlier_same_block(tokens, tok), chosen)
        sel = jnp.where(pick(), 1.0, 0.0).astype(bf16)
        gate = dot_nt(sel, coded)
        place = dot_nt(sel, rank.astype(bf16))
        lane_block = lax.div(lax.broadcasted_iota(jnp.int32, (1, tokens), 1), tok)
        source = jnp.zeros((1, tokens), jnp.int32)
        for b in range(blocks):
            source = jnp.where(lane_block == b, meta_ref[1 + b], source)
        hit = jnp.logical_and(
            jnp.logical_and(gate >= 0.0, place == table_ref[:, 1:2].astype(f32)),
            source == table_ref[:, 2:3],
        )
        gated_ref[...] = jnp.where(hit, gate, 0.0).astype(bf16)
        hit_scr[...] = jnp.where(hit, 1.0, 0.0)
        acc[...] = jnp.zeros_like(acc)

    for i in range(2):
        dm[i * half : (i + 1) * half, :] = d_refs[i][...]
    acc[...] += dot_nt(eout_ref[...], dm[...])

    @pl.when(step == pl.num_programs(0) - 1)
    def _():
        terms = jnp.sum(acc[...] * hit_scr[...], axis=-1, keepdims=True)
        placed = jnp.where(pick(), terms, 0.0)
        want = lax.broadcasted_iota(jnp.int32, (cap * sp, rows), 0)
        fold = jnp.where(want == lanes_ref[...], 1.0, 0.0)
        folded = lax.dot_general(
            fold,
            placed,
            (((1,), (0,)), ((), ())),
            precision=lax.Precision.HIGHEST,
            preferred_element_type=f32,
        )
        for to in range(terms_ref.shape[0]):
            terms_ref[to] = folded


def slot_terms(meta, packs, eout, experts, cap, sp):
    rows, width = eout.shape
    half, packed = packs[0].shape
    blocks = sp
    r = np.arange(rows)
    e, c, s = r // (cap * sp), (r // sp) % cap, r % sp
    table = jnp.asarray(np.stack([e, c, s], axis=1), jnp.int32)
    lanes = jnp.asarray((c * sp + s)[None, :], jnp.int32)
    col = min(width, 2048)
    tokens = 2 * half
    gate_at = (packed - 2 * experts) // experts
    d_spec = pl.BlockSpec((half, col), lambda i, m: (0, i))
    g_spec = pl.BlockSpec((half, experts), lambda i, m: (0, gate_at))
    e_spec = pl.BlockSpec((rows, col), lambda i, m: (0, i))
    return pl.pallas_call(
        functools.partial(terms_kernel, blocks, sp, cap),
        grid_spec=pltpu.PrefetchScalarGridSpec(
            num_scalar_prefetch=1,
            grid=(width // col,),
            in_specs=[whole((rows, 3)), whole((1, rows))]
            + [d_spec] * 2
            + [g_spec] * 2
            + [e_spec],
            out_specs=[whole((rows, tokens)), whole((sp, cap * sp, experts))],
            scratch_shapes=[
                pltpu.VMEM((tokens, col), bf16),
                pltpu.VMEM((rows, tokens), f32),
                pltpu.VMEM((rows, tokens), f32),
            ],
        ),
        out_shape=[
            jax.ShapeDtypeStruct((rows, tokens), bf16),
            jax.ShapeDtypeStruct((sp, cap * sp, experts), f32),
        ],
        compiler_params=pltpu.CompilerParams(vmem_limit_bytes=24 * mib),
        cost_estimate=takes(6.2),
        name="slot_terms",
    )(meta, table, lanes, *packs, *packs, eout)


def batch_kernel(gated_ref, *refs):
    batch_ref, dm = refs[-2:]
    tok = refs[0].shape[0]
    for b, r in enumerate(refs[:-2]):
        dm[b * tok : (b + 1) * tok, :] = r[...]
    batch_ref[...] = dot_nn(gated_ref[...], dm[...]).astype(bf16)


def batch_grad(gated, packs, width):
    rows, tokens = gated.shape
    tok = packs[0].shape[0]
    col = min(width, 2048)
    return pl.pallas_call(
        batch_kernel,
        grid=(width // col,),
        in_specs=[whole((rows, tokens))]
        + [pl.BlockSpec((tok, col), lambda i: (0, i))] * len(packs),
        out_specs=pl.BlockSpec((rows, col), lambda i: (0, i)),
        out_shape=jax.ShapeDtypeStruct((rows, width), bf16),
        scratch_shapes=[pltpu.VMEM((tokens, col), bf16)],
        compiler_params=pltpu.CompilerParams(vmem_limit_bytes=16 * mib),
        cost_estimate=takes(4.6),
        name="batch_grad",
    )(gated, *packs)


def router_kernel(sp, cap, meta_ref, *refs):
    info_refs, moe_refs = refs[:2], refs[2:4]
    terms_in, out_ref, terms_ref = refs[4:]
    terms_ref[...] = jnp.sum(terms_in[...], axis=0)
    share, experts = out_ref.shape
    tok = 2 * info_refs[0].shape[0] // sp
    info = jnp.concatenate([r[...] for r in info_refs], axis=0)
    moe = jnp.concatenate([r[...] for r in moe_refs], axis=0)
    high = info[:, :experts]
    chosen = high >= 0
    prob = jnp.where(chosen, high.astype(f32) + info[:, experts:].astype(f32), 0.0)
    rank = dot_nn(earlier_same_block(tok * sp, tok), chosen.astype(bf16))
    pieces = []
    for b in range(sp):
        place = rank[b * tok : (b + 1) * tok, :]
        one = jnp.zeros((tok, experts), f32)
        for c in range(cap):
            row = terms_ref[pl.ds(c * sp + meta_ref[1 + b], 1), :]
            one = jnp.where(place == c, row, one)
        pieces.append(one)
    dgate = jnp.where(chosen, jnp.concatenate(pieces, axis=0), 0.0)
    dlogit = prob * (dgate - jnp.sum(prob * dgate, axis=-1, keepdims=True))
    a = dlogit.astype(bf16)
    rest = dlogit - a.astype(f32)
    b = rest.astype(bf16)
    c = (rest - b.astype(f32)).astype(bf16)
    wide = dot_tn(moe, jnp.concatenate([a, b, c], axis=1))
    total = wide[:, :experts] + wide[:, experts : 2 * experts] + wide[:, 2 * experts :]
    out_ref[...] = total.astype(bf16)


def router_grad(meta, packs, terms, width, experts, cap, sp):
    half, packed = packs[0].shape
    share = width // sp
    info_at = packed // (2 * experts) - 1
    info_spec = pl.BlockSpec((half, 2 * experts), lambda i, m: (0, info_at))
    moe_specs = [pl.BlockSpec((half, share), lambda i, m, c=c: (0, sp + c)) for c in range(2)]
    return pl.pallas_call(
        functools.partial(router_kernel, sp, cap),
        grid_spec=pltpu.PrefetchScalarGridSpec(
            num_scalar_prefetch=1,
            grid=(1,),
            in_specs=[info_spec] * 2 + moe_specs + [whole(terms.shape)],
            out_specs=whole((share, experts)),
            scratch_shapes=[pltpu.VMEM((cap * sp, experts), f32)],
        ),
        out_shape=jax.ShapeDtypeStruct((share, experts), bf16),
        compiler_params=pltpu.CompilerParams(vmem_limit_bytes=16 * mib),
        cost_estimate=takes(3),
        name="router_grad",
    )(meta, *packs, *packs, terms)


def flipped(x, axis, size, k):
    return lax.ppermute(x, axis, [(i, i ^ k) for i in range(size)])


def sent_over(axis, size, x):
    if size & (size - 1):
        return [lax.psum(x.astype(f32), axis)]
    return [x] + [flipped(x, axis, size, k) for k in range(1, size)]


def tree_sum(terms):
    terms = [x.astype(f32) for x in terms]
    while len(terms) > 1:
        terms = [a + b for a, b in zip(terms[0::2], terms[1::2])]
    return terms[0]


def together(*arrays):
    return lax.optimization_barrier(arrays)


def on_device(
    q_pre,
    attn_out,
    d_attn,
    k_pre,
    values,
    q_gain,
    k_gain,
    offsets,
    moe_in,
    router,
    expert_ids,
    d_moe,
    expert_out,
):
    dp = lax.axis_size("dp")
    sp = lax.axis_size("sp")
    me = lax.axis_index("sp").astype(jnp.int32)
    other = jnp.bitwise_xor(me, 1)
    chips = sp // 2
    swap = [(i, i ^ 1) for i in range(sp)]

    def exchange(x):
        return lax.ppermute(x, "sp", swap)

    def to_chip(x, k):
        return flipped(x, "sp", sp, 2 * k)

    def both(mine):
        mine = jnp.concatenate(mine, axis=0)
        return [mine, exchange(mine)]

    steps = 2 * jnp.arange(chips, dtype=jnp.int32)
    owners = jnp.concatenate([jnp.bitwise_xor(me, steps), jnp.bitwise_xor(other, steps)])
    qg, kg = q_gain[None, :], k_gain[None, :]
    kv_heads = k_pre.shape[2] // q_gain.shape[0]
    width = moe_in.shape[2]
    experts = router.shape[1]
    place = jnp.stack([me // 2, jnp.bitwise_and(me, 1)])

    experts_here, _, cap, _ = expert_out.shape[1:]
    eout = jnp.transpose(expert_out[0], (0, 2, 1, 3)).reshape(experts_here * cap * sp, width)
    slot_meta = jnp.concatenate([(me * experts_here)[None], owners])
    meta = jnp.concatenate([offsets + me * q_pre.shape[1], owners])

    kv = pack_keys(k_pre[0], values[0], kg)
    if chips == 4:
        far = to_chip(kv, 2)
        kv = [kv, to_chip(kv, 1), far, to_chip(far, 1)]
    else:
        kv = [kv] + [to_chip(kv, k) for k in range(1, chips)]
    packs = gates(place, moe_in[0], router, expert_ids[0], d_moe[0], chips)
    kv, packs = together(kv, packs)

    packs = [packs[0]] + [to_chip(packs[k], k) for k in range(1, chips)]
    dq, own, keep, own_send, send = attend(
        meta, q_pre[0], attn_out[0], d_attn[0], qg, both(kv), sp, kv_heads
    )
    packs, own, keep, own_send, send = together(packs, own, keep, own_send, send)

    rows = k_pre.shape[1]
    arrived = exchange(send)
    first, rest = pair_sums(keep, arrived, rows, kv_heads)
    packs, first, rest, own_send = together(packs, first, rest, own_send)

    own_arrived = exchange(own_send)
    first = [to_chip(first[k - 1], k) for k in range(1, chips)]
    packs = both(packs)
    gated, terms = slot_terms(slot_meta, packs, eout, experts, cap, sp)
    terms = lax.all_to_all(terms, "sp", split_axis=0, concat_axis=0, tiled=True)
    batch = batch_grad(gated, packs, width)
    own_arrived, first, rest, terms, batch = together(own_arrived, first, rest, terms, batch)

    rest = [to_chip(rest[k - 1], k) for k in range(1, chips)]
    routed = router_grad(slot_meta, packs, terms, width, experts, cap, sp)
    routed = sent_over("dp", dp, routed)
    dk, dv = finish_keys(k_pre[0], kg, [own, own_arrived], first, rest)
    dk, dv, routed = together(dk, dv, routed)
    batch = jnp.transpose(batch.reshape(experts_here, cap, sp, width), (0, 2, 1, 3))
    return (dq[None], dk[None], dv[None], batch[None], tree_sum(routed))


def solution(mesh):
    in_specs = (
        P("dp", "sp", None),
        P("dp", "sp", None),
        P("dp", "sp", None),
        P("dp", "sp", None),
        P("dp", "sp", None),
        P(),
        P(),
        P("dp"),
        P("dp", "sp", None),
        P(),
        P("dp", "sp", None),
        P("dp", "sp", None),
        P("dp", "sp", None, None, None),
    )
    out_specs = (
        P("dp", "sp", None),
        P("dp", "sp", None),
        P("dp", "sp", None),
        P("dp", "sp", None, None, None),
        P("sp", None),
    )
    return jax.shard_map(
        on_device, mesh=mesh, in_specs=in_specs, out_specs=out_specs, check_vma=False
    )
```

```python
import functools
import math

import jax
import jax.numpy as jnp
import numpy as np
from jax import lax
from jax.experimental import pallas as pl
from jax.experimental.pallas import tpu as pltpu
from jax.sharding import PartitionSpec as P

norm_eps = 1e-06
f32 = jnp.float32
bf16 = jnp.bfloat16
mib = 1024 * 1024


def takes(us):
    flops = int(us * 1.15e9)
    return pl.CostEstimate(flops=flops, transcendentals=0, bytes_accessed=int(us * 3.6e6))


def dot_nt(a, b):
    return lax.dot_general(a, b, (((1,), (1,)), ((), ())), preferred_element_type=f32)


def dot_nn(a, b):
    return lax.dot_general(a, b, (((1,), (0,)), ((), ())), preferred_element_type=f32)


def dot_tn(a, b):
    return lax.dot_general(a, b, (((0,), (0,)), ((), ())), preferred_element_type=f32)


def whole(shape):
    return pl.BlockSpec(shape, lambda *_: (0,) * len(shape))


def keys_kernel(k_ref, v_ref, gain_ref, kv_ref):
    hd = gain_ref.shape[1]
    gain = gain_ref[...]
    for g in range(k_ref.shape[1] // hd):
        k = k_ref[:, g * hd : (g + 1) * hd].astype(f32)
        inv = lax.rsqrt(jnp.mean(k * k, axis=-1, keepdims=True) + norm_eps)
        kv_ref[:, 2 * g * hd : (2 * g + 1) * hd] = ((k * inv) * gain).astype(bf16)
        kv_ref[:, (2 * g + 1) * hd : (2 * g + 2) * hd] = v_ref[:, g * hd : (g + 1) * hd]


def pack_keys(k_pre, values, k_gain):
    rows, width = k_pre.shape
    return pl.pallas_call(
        keys_kernel,
        out_shape=jax.ShapeDtypeStruct((rows, 2 * width), bf16),
        cost_estimate=takes(1.8),
        name="pack_keys",
    )(k_pre, values, k_gain)


def gates_kernel(meta_ref, moe_ref, router_ref, ids_ref, dmoe_ref, pack_ref, *share_refs):
    tok, width = moe_ref.shape
    experts = router_ref.shape[1]
    logits = dot_nn(moe_ref[...], router_ref[...])
    lane = lax.broadcasted_iota(jnp.int32, (tok, experts), 1)
    chosen = lane == ids_ref[:, 0:1]
    for k in range(1, ids_ref.shape[1]):
        chosen = jnp.logical_or(chosen, lane == ids_ref[:, k : k + 1])
    weights = jnp.where(chosen, jnp.exp(logits), 0.0)
    probs = weights / jnp.sum(weights, axis=-1, keepdims=True)
    high = probs.astype(bf16)
    pack_ref[:, :width] = dmoe_ref[...]
    pack_ref[:, width : width + experts] = jnp.where(chosen, high.astype(f32), -1.0).astype(bf16)
    pack_ref[:, width + experts :] = (probs - high.astype(f32)).astype(bf16)
    share = share_refs[0].shape[1] // 2
    chip, core = meta_ref[0], meta_ref[1]
    for k, ref in enumerate(share_refs):
        to = jnp.bitwise_xor(chip, k) * 2
        for i in range(2):
            at = pl.multiple_of((to + jnp.bitwise_xor(core, i)) * share, 128)
            ref[:, i * share : (i + 1) * share] = moe_ref[:, pl.ds(at, share)]


def gates(meta, moe_in, router, ids, d_moe, chips):
    tok, width = moe_in.shape
    experts = router.shape[1]
    vm = pl.BlockSpec(memory_space=pltpu.VMEM)
    return pl.pallas_call(
        gates_kernel,
        in_specs=[pl.BlockSpec(memory_space=pltpu.SMEM)] + [vm] * 4,
        out_shape=[jax.ShapeDtypeStruct((tok, width + 2 * experts), bf16)]
        + [jax.ShapeDtypeStruct((tok, width // chips), bf16)] * chips,
        compiler_params=pltpu.CompilerParams(vmem_limit_bytes=8 * mib),
        cost_estimate=takes(1),
        name="gates",
    )(meta, moe_in, router, ids, d_moe)


def attend_kernel(blocks, meta_ref, q_ref, o_ref, do_ref, gain_ref, *refs):
    kv_refs = refs[:2]
    dq_ref = refs[-5]
    part_refs = refs[-4:]
    tok = q_ref.shape[0]
    hd = gain_ref.shape[1]
    heads = q_ref.shape[1] // hd
    kb = 2 * kv_refs[0].shape[0] // blocks
    keys = kb * blocks
    scale = hd ** (-0.5)
    offset = meta_ref[0]
    gain = gain_ref[...]
    key = jnp.concatenate([r[:, :hd] for r in kv_refs], axis=0)
    val = jnp.concatenate([r[:, hd:] for r in kv_refs], axis=0)
    pos = jnp.concatenate(
        [
            meta_ref[1 + b] * kb + lax.broadcasted_iota(jnp.int32, (kb, 1), 0)
            for b in range(blocks)
        ],
        axis=0,
    )
    step_heads = min(heads, max(128 // tok, heads * 1024 // keys))
    rows = step_heads * tok
    limit = offset + lax.rem(lax.broadcasted_iota(jnp.int32, (1, rows), 1), tok)
    visible = pos <= limit
    dk = dv = None
    for h0 in range(0, heads, step_heads):

        def stack(ref):
            return jnp.concatenate(
                [ref[:, h * hd : (h + 1) * hd] for h in range(h0, h0 + step_heads)], axis=0
            )

        q = stack(q_ref).astype(f32)
        do = stack(do_ref)
        prod = do.astype(f32) * stack(o_ref).astype(f32)
        delta = jnp.sum(prod.T, axis=0, keepdims=True)
        inv = lax.rsqrt(jnp.mean(q * q, axis=-1, keepdims=True) + norm_eps)
        unit = q * inv
        q_hat = (unit * gain).astype(bf16)
        scores = dot_nt(key, q_hat)
        ex = jnp.where(visible, jnp.exp2(scores * (scale * math.log2(math.e))), 0.0)
        probs = ex * (1.0 / jnp.sum(ex, axis=0, keepdims=True))
        dv_one = dot_nn(probs.astype(bf16), do)
        dprobs = dot_nt(val, do)
        ds = ((probs * scale) * (dprobs - delta)).astype(bf16)
        dk_one = dot_nn(ds, q_hat)
        dq = dot_tn(key, ds).T
        c = dq * gain
        dq_pre = (inv * (c - unit * jnp.mean(c * unit, axis=-1, keepdims=True))).astype(bf16)
        for i in range(step_heads):
            h = h0 + i
            dq_ref[:, h * hd : (h + 1) * hd] = dq_pre[i * tok : (i + 1) * tok, :]
        dk = dk_one if dk is None else dk + dk_one
        dv = dv_one if dv is None else dv + dv_one
    at = 0
    for ref in part_refs:
        size = ref.shape[0]
        ref[:, :hd] = dk[at : at + size, :].astype(ref.dtype)
        ref[:, hd:] = dv[at : at + size, :].astype(ref.dtype)
        at += size


def attend(meta, q, o, do, gain, kv_halves, blocks, kv_heads):
    tok, width = q.shape
    hd = gain.shape[1]
    half, kv_width = kv_halves[0].shape
    step = width // kv_heads
    row_spec = pl.BlockSpec((tok, step), lambda g, m: (0, g))
    part_spec = pl.BlockSpec((half, 2 * hd), lambda g, m: (0, g))
    own = 2 * half // blocks
    sizes = (own, half - own) * 2
    return pl.pallas_call(
        functools.partial(attend_kernel, blocks),
        grid_spec=pltpu.PrefetchScalarGridSpec(
            num_scalar_prefetch=1,
            grid=(kv_width // (2 * hd),),
            in_specs=[row_spec] * 3
            + [whole((1, hd))]
            + [part_spec] * 2,
            out_specs=[row_spec] + [pl.BlockSpec((n, 2 * hd), lambda g, m: (0, g)) for n in sizes],
        ),
        out_shape=[
            jax.ShapeDtypeStruct((tok, width), bf16),
            jax.ShapeDtypeStruct((sizes[0], kv_width), f32),
            jax.ShapeDtypeStruct((sizes[1], kv_width), f32),
            jax.ShapeDtypeStruct((sizes[2], kv_width), bf16),
            jax.ShapeDtypeStruct((sizes[3], kv_width), bf16),
        ],
        compiler_params=pltpu.CompilerParams(vmem_limit_bytes=32 * mib),
        cost_estimate=takes(10),
        name="attend",
    )(meta, q, o, do, gain, *kv_halves)


def pair_kernel(keep_ref, other_ref, *out_refs):
    rows, cut = out_refs[0].shape
    blocks = len(out_refs) // 2
    for k in range(blocks):
        at = k * rows
        total = keep_ref[at : at + rows, :] + other_ref[at : at + rows, :].astype(f32)
        out_refs[k][...] = total[:, :cut].astype(bf16)
        out_refs[blocks + k][...] = total[:, cut:].astype(bf16)


def pair_sums(keep, other, rows, kv_heads):
    blocks = keep.shape[0] // rows
    width = keep.shape[1]
    cut = (kv_heads // 2) * (width // kv_heads)
    sums = pl.pallas_call(
        pair_kernel,
        out_shape=[jax.ShapeDtypeStruct((rows, cut), bf16)] * blocks
        + [jax.ShapeDtypeStruct((rows, width - cut), bf16)] * blocks,
        compiler_params=pltpu.CompilerParams(vmem_limit_bytes=32 * mib),
        cost_estimate=takes(1),
        name="pair_sums",
    )(keep, other)
    return sums[:blocks], sums[blocks:]


def finish_kernel(chips, k_ref, gain_ref, own_ref, other_ref, *refs):
    first, rest = refs[: chips - 1], refs[chips - 1 : -2]
    dk_ref, dv_ref = refs[-2:]
    hd = gain_ref.shape[1]
    gain = gain_ref[...]
    cut = first[0].shape[1]
    for g in range(k_ref.shape[1] // hd):
        at = 2 * g * hd
        total = own_ref[:, at : at + 2 * hd] + other_ref[:, at : at + 2 * hd].astype(f32)
        parts, start = (first, at) if at < cut else (rest, at - cut)
        for r in parts:
            total = total + r[:, start : start + 2 * hd].astype(f32)
        k = k_ref[:, g * hd : (g + 1) * hd].astype(f32)
        inv = lax.rsqrt(jnp.mean(k * k, axis=-1, keepdims=True) + norm_eps)
        unit = k * inv
        c = total[:, :hd] * gain
        dk = inv * (c - unit * jnp.mean(c * unit, axis=-1, keepdims=True))
        dk_ref[:, g * hd : (g + 1) * hd] = dk.astype(bf16)
        dv_ref[:, g * hd : (g + 1) * hd] = total[:, hd:].astype(bf16)


def finish_keys(k_pre, k_gain, own, first, rest):
    out = jax.ShapeDtypeStruct(k_pre.shape, bf16)
    return pl.pallas_call(
        functools.partial(finish_kernel, len(first) + 1),
        out_shape=(out, out),
        compiler_params=pltpu.CompilerParams(vmem_limit_bytes=8 * mib),
        cost_estimate=takes(2.2),
        name="finish_keys",
    )(k_pre, k_gain, *own, *first, *rest)


def earlier_same_block(rows, block):
    i = lax.broadcasted_iota(jnp.int32, (rows, rows), 0)
    j = lax.broadcasted_iota(jnp.int32, (rows, rows), 1)
    same = lax.div(i, block) == lax.div(j, block)
    return jnp.where(jnp.logical_and(same, j < i), 1.0, 0.0).astype(bf16)


def terms_kernel(blocks, sp, cap, meta_ref, table_ref, lanes_ref, *refs):
    d_refs = refs[:2]
    g_refs = refs[2:4]
    eout_ref, gated_ref, terms_ref, dm, hit_scr, acc = refs[4:]
    half = d_refs[0].shape[0]
    tokens = 2 * half
    tok = tokens // blocks
    experts = g_refs[0].shape[1]
    rows = eout_ref.shape[0]
    step = pl.program_id(0)

    def pick():
        expert = meta_ref[0] + table_ref[:, 0:1]
        return lax.broadcasted_iota(jnp.int32, (rows, experts), 1) == expert

    @pl.when(step == 0)
    def _():
        coded = jnp.concatenate([r[...] for r in g_refs], axis=0)
        chosen = (coded >= 0).astype(bf16)
        rank = dot_nn(earlier_same_block(tokens, tok), chosen)
        sel = jnp.where(pick(), 1.0, 0.0).astype(bf16)
        gate = dot_nt(sel, coded)
        place = dot_nt(sel, rank.astype(bf16))
        lane_block = lax.div(lax.broadcasted_iota(jnp.int32, (1, tokens), 1), tok)
        source = jnp.zeros((1, tokens), jnp.int32)
        for b in range(blocks):
            source = jnp.where(lane_block == b, meta_ref[1 + b], source)
        hit = jnp.logical_and(
            jnp.logical_and(gate >= 0.0, place == table_ref[:, 1:2].astype(f32)),
            source == table_ref[:, 2:3],
        )
        gated_ref[...] = jnp.where(hit, gate, 0.0).astype(bf16)
        hit_scr[...] = jnp.where(hit, 1.0, 0.0)
        acc[...] = jnp.zeros_like(acc)

    for i in range(2):
        dm[i * half : (i + 1) * half, :] = d_refs[i][...]
    acc[...] += dot_nt(eout_ref[...], dm[...])

    @pl.when(step == pl.num_programs(0) - 1)
    def _():
        terms = jnp.sum(acc[...] * hit_scr[...], axis=-1, keepdims=True)
        placed = jnp.where(pick(), terms, 0.0)
        want = lax.broadcasted_iota(jnp.int32, (cap * sp, rows), 0)
        fold = jnp.where(want == lanes_ref[...], 1.0, 0.0)
        folded = lax.dot_general(
            fold,
            placed,
            (((1,), (0,)), ((), ())),
            precision=lax.Precision.HIGHEST,
            preferred_element_type=f32,
        )
        for to in range(terms_ref.shape[0]):
            terms_ref[to] = folded


def slot_terms(meta, packs, eout, experts, cap, sp):
    rows, width = eout.shape
    half, packed = packs[0].shape
    blocks = sp
    r = np.arange(rows)
    e, c, s = r // (cap * sp), (r // sp) % cap, r % sp
    table = jnp.asarray(np.stack([e, c, s], axis=1), jnp.int32)
    lanes = jnp.asarray((c * sp + s)[None, :], jnp.int32)
    col = min(width, 2048)
    tokens = 2 * half
    gate_at = (packed - 2 * experts) // experts
    d_spec = pl.BlockSpec((half, col), lambda i, m: (0, i))
    g_spec = pl.BlockSpec((half, experts), lambda i, m: (0, gate_at))
    e_spec = pl.BlockSpec((rows, col), lambda i, m: (0, i))
    return pl.pallas_call(
        functools.partial(terms_kernel, blocks, sp, cap),
        grid_spec=pltpu.PrefetchScalarGridSpec(
            num_scalar_prefetch=1,
            grid=(width // col,),
            in_specs=[whole((rows, 3)), whole((1, rows))]
            + [d_spec] * 2
            + [g_spec] * 2
            + [e_spec],
            out_specs=[whole((rows, tokens)), whole((sp, cap * sp, experts))],
            scratch_shapes=[
                pltpu.VMEM((tokens, col), bf16),
                pltpu.VMEM((rows, tokens), f32),
                pltpu.VMEM((rows, tokens), f32),
            ],
        ),
        out_shape=[
            jax.ShapeDtypeStruct((rows, tokens), bf16),
            jax.ShapeDtypeStruct((sp, cap * sp, experts), f32),
        ],
        compiler_params=pltpu.CompilerParams(vmem_limit_bytes=24 * mib),
        cost_estimate=takes(6.2),
        name="slot_terms",
    )(meta, table, lanes, *packs, *packs, eout)


def batch_kernel(gated_ref, *refs):
    batch_ref, dm = refs[-2:]
    tok = refs[0].shape[0]
    for b, r in enumerate(refs[:-2]):
        dm[b * tok : (b + 1) * tok, :] = r[...]
    batch_ref[...] = dot_nn(gated_ref[...], dm[...]).astype(bf16)


def batch_grad(gated, packs, width):
    rows, tokens = gated.shape
    tok = packs[0].shape[0]
    col = min(width, 2048)
    return pl.pallas_call(
        batch_kernel,
        grid=(width // col,),
        in_specs=[whole((rows, tokens))]
        + [pl.BlockSpec((tok, col), lambda i: (0, i))] * len(packs),
        out_specs=pl.BlockSpec((rows, col), lambda i: (0, i)),
        out_shape=jax.ShapeDtypeStruct((rows, width), bf16),
        scratch_shapes=[pltpu.VMEM((tokens, col), bf16)],
        compiler_params=pltpu.CompilerParams(vmem_limit_bytes=16 * mib),
        cost_estimate=takes(4.6),
        name="batch_grad",
    )(gated, *packs)


def router_kernel(sp, cap, meta_ref, *refs):
    info_refs, moe_refs = refs[:2], refs[2:4]
    terms_in, out_ref, terms_ref = refs[4:]
    terms_ref[...] = jnp.sum(terms_in[...], axis=0)
    share, experts = out_ref.shape
    tok = 2 * info_refs[0].shape[0] // sp
    info = jnp.concatenate([r[...] for r in info_refs], axis=0)
    moe = jnp.concatenate([r[...] for r in moe_refs], axis=0)
    high = info[:, :experts]
    chosen = high >= 0
    prob = jnp.where(chosen, high.astype(f32) + info[:, experts:].astype(f32), 0.0)
    rank = dot_nn(earlier_same_block(tok * sp, tok), chosen.astype(bf16))
    pieces = []
    for b in range(sp):
        place = rank[b * tok : (b + 1) * tok, :]
        one = jnp.zeros((tok, experts), f32)
        for c in range(cap):
            row = terms_ref[pl.ds(c * sp + meta_ref[1 + b], 1), :]
            one = jnp.where(place == c, row, one)
        pieces.append(one)
    dgate = jnp.where(chosen, jnp.concatenate(pieces, axis=0), 0.0)
    dlogit = prob * (dgate - jnp.sum(prob * dgate, axis=-1, keepdims=True))
    a = dlogit.astype(bf16)
    rest = dlogit - a.astype(f32)
    b = rest.astype(bf16)
    c = (rest - b.astype(f32)).astype(bf16)
    wide = dot_tn(moe, jnp.concatenate([a, b, c], axis=1))
    total = wide[:, :experts] + wide[:, experts : 2 * experts] + wide[:, 2 * experts :]
    out_ref[...] = total.astype(bf16)


def router_grad(meta, packs, moe, terms, width, experts, cap, sp):
    half, packed = packs[0].shape
    share = width // sp
    info_at = packed // (2 * experts) - 1
    info_spec = pl.BlockSpec((half, 2 * experts), lambda i, m: (0, info_at))
    moe_specs = [whole((half, share))] * 2
    return pl.pallas_call(
        functools.partial(router_kernel, sp, cap),
        grid_spec=pltpu.PrefetchScalarGridSpec(
            num_scalar_prefetch=1,
            grid=(1,),
            in_specs=[info_spec] * 2 + moe_specs + [whole(terms.shape)],
            out_specs=whole((share, experts)),
            scratch_shapes=[pltpu.VMEM((cap * sp, experts), f32)],
        ),
        out_shape=jax.ShapeDtypeStruct((share, experts), bf16),
        compiler_params=pltpu.CompilerParams(vmem_limit_bytes=16 * mib),
        cost_estimate=takes(3),
        name="router_grad",
    )(meta, *packs, *moe, terms)


def flipped(x, axis, size, k):
    return lax.ppermute(x, axis, [(i, i ^ k) for i in range(size)])


def sent_over(axis, size, x):
    if size & (size - 1):
        return [lax.psum(x.astype(f32), axis)]
    return [x] + [flipped(x, axis, size, k) for k in range(1, size)]


def tree_sum(terms):
    terms = [x.astype(f32) for x in terms]
    while len(terms) > 1:
        terms = [a + b for a, b in zip(terms[0::2], terms[1::2])]
    return terms[0]


def together(*arrays):
    return lax.optimization_barrier(arrays)


def on_device(
    q_pre,
    attn_out,
    d_attn,
    k_pre,
    values,
    q_gain,
    k_gain,
    offsets,
    moe_in,
    router,
    expert_ids,
    d_moe,
    expert_out,
):
    dp = lax.axis_size("dp")
    sp = lax.axis_size("sp")
    me = lax.axis_index("sp").astype(jnp.int32)
    other = jnp.bitwise_xor(me, 1)
    chips = sp // 2
    swap = [(i, i ^ 1) for i in range(sp)]

    def exchange(x):
        return lax.ppermute(x, "sp", swap)

    def to_chip(x, k):
        return flipped(x, "sp", sp, 2 * k)

    def both(mine):
        mine = jnp.concatenate(mine, axis=0)
        return [mine, exchange(mine)]

    steps = 2 * jnp.arange(chips, dtype=jnp.int32)
    owners = jnp.concatenate([jnp.bitwise_xor(me, steps), jnp.bitwise_xor(other, steps)])
    qg, kg = q_gain[None, :], k_gain[None, :]
    kv_heads = k_pre.shape[2] // q_gain.shape[0]
    width = moe_in.shape[2]
    experts = router.shape[1]
    place = jnp.stack([me // 2, jnp.bitwise_and(me, 1)])

    experts_here, _, cap, _ = expert_out.shape[1:]
    eout = jnp.transpose(expert_out[0], (0, 2, 1, 3)).reshape(experts_here * cap * sp, width)
    slot_meta = jnp.concatenate([(me * experts_here)[None], owners])
    meta = jnp.concatenate([offsets + me * q_pre.shape[1], owners])

    kv = pack_keys(k_pre[0], values[0], kg)
    if chips == 4:
        far = to_chip(kv, 2)
        kv = [kv, to_chip(kv, 1), far, to_chip(far, 1)]
    else:
        kv = [kv] + [to_chip(kv, k) for k in range(1, chips)]
    pack, *shares = gates(place, moe_in[0], router, expert_ids[0], d_moe[0], chips)
    shares = [shares[0]] + [to_chip(shares[k], k) for k in range(1, chips)]
    kv, pack, shares = together(kv, pack, shares)

    packs = [pack] + [to_chip(pack, k) for k in range(1, chips)]
    share = width // sp
    mine = jnp.concatenate([x[:, :share] for x in shares], axis=0)
    theirs = exchange(jnp.concatenate([x[:, share:] for x in shares], axis=0))
    dq, own, keep, own_send, send = attend(
        meta, q_pre[0], attn_out[0], d_attn[0], qg, both(kv), sp, kv_heads
    )
    packs, mine, theirs, own, keep, own_send, send = together(
        packs, mine, theirs, own, keep, own_send, send
    )

    rows = k_pre.shape[1]
    arrived = exchange(send)
    first, rest = pair_sums(keep, arrived, rows, kv_heads)
    packs, first, rest, own_send = together(packs, first, rest, own_send)

    own_arrived = exchange(own_send)
    first = [to_chip(first[k - 1], k) for k in range(1, chips)]
    packs = both(packs)
    gated, terms = slot_terms(slot_meta, packs, eout, experts, cap, sp)
    terms = lax.all_to_all(terms, "sp", split_axis=0, concat_axis=0, tiled=True)
    batch = batch_grad(gated, packs, width)
    own_arrived, first, rest, batch = together(own_arrived, first, rest, batch)

    rest = [to_chip(rest[k - 1], k) for k in range(1, chips)]
    routed = router_grad(slot_meta, packs, (mine, theirs), terms, width, experts, cap, sp)
    routed = sent_over("dp", dp, routed)
    dk, dv = finish_keys(k_pre[0], kg, [own, own_arrived], first, rest)
    dk, dv, routed = together(dk, dv, routed)
    batch = jnp.transpose(batch.reshape(experts_here, cap, sp, width), (0, 2, 1, 3))
    return (dq[None], dk[None], dv[None], batch[None], tree_sum(routed))


def solution(mesh):
    in_specs = (
        P("dp", "sp", None),
        P("dp", "sp", None),
        P("dp", "sp", None),
        P("dp", "sp", None),
        P("dp", "sp", None),
        P(),
        P(),
        P("dp"),
        P("dp", "sp", None),
        P(),
        P("dp", "sp", None),
        P("dp", "sp", None),
        P("dp", "sp", None, None, None),
    )
    out_specs = (
        P("dp", "sp", None),
        P("dp", "sp", None),
        P("dp", "sp", None),
        P("dp", "sp", None, None, None),
        P("sp", None),
    )
    return jax.shard_map(
        on_device, mesh=mesh, in_specs=in_specs, out_specs=out_specs, check_vma=False
    )
```

```python
import functools
import math

import jax
import jax.numpy as jnp
import numpy as np
from jax import lax
from jax.experimental import pallas as pl
from jax.experimental.pallas import tpu as pltpu
from jax.sharding import PartitionSpec as P

norm_eps = 1e-06
f32 = jnp.float32
bf16 = jnp.bfloat16
mib = 1024 * 1024


def takes(us):
    flops = int(us * 1.15e9)
    return pl.CostEstimate(flops=flops, transcendentals=0, bytes_accessed=int(us * 3.6e6))


def dot_nt(a, b):
    return lax.dot_general(a, b, (((1,), (1,)), ((), ())), preferred_element_type=f32)


def dot_nn(a, b):
    return lax.dot_general(a, b, (((1,), (0,)), ((), ())), preferred_element_type=f32)


def dot_tn(a, b):
    return lax.dot_general(a, b, (((0,), (0,)), ((), ())), preferred_element_type=f32)


def whole(shape):
    return pl.BlockSpec(shape, lambda *_: (0,) * len(shape))


def keys_kernel(k_ref, v_ref, gain_ref, kv_ref):
    hd = gain_ref.shape[1]
    gain = gain_ref[...]
    for g in range(k_ref.shape[1] // hd):
        k = k_ref[:, g * hd : (g + 1) * hd].astype(f32)
        inv = lax.rsqrt(jnp.mean(k * k, axis=-1, keepdims=True) + norm_eps)
        kv_ref[:, 2 * g * hd : (2 * g + 1) * hd] = ((k * inv) * gain).astype(bf16)
        kv_ref[:, (2 * g + 1) * hd : (2 * g + 2) * hd] = v_ref[:, g * hd : (g + 1) * hd]


def pack_keys(k_pre, values, k_gain):
    rows, width = k_pre.shape
    return pl.pallas_call(
        keys_kernel,
        out_shape=jax.ShapeDtypeStruct((rows, 2 * width), bf16),
        cost_estimate=takes(1.8),
        name="pack_keys",
    )(k_pre, values, k_gain)


def gates_kernel(meta_ref, moe_ref, router_ref, ids_ref, dmoe_ref, pack_ref, *share_refs):
    tok, width = moe_ref.shape
    experts = router_ref.shape[1]
    logits = dot_nn(moe_ref[...], router_ref[...])
    lane = lax.broadcasted_iota(jnp.int32, (tok, experts), 1)
    chosen = lane == ids_ref[:, 0:1]
    for k in range(1, ids_ref.shape[1]):
        chosen = jnp.logical_or(chosen, lane == ids_ref[:, k : k + 1])
    weights = jnp.where(chosen, jnp.exp(logits), 0.0)
    probs = weights / jnp.sum(weights, axis=-1, keepdims=True)
    high = probs.astype(bf16)
    pack_ref[:, :width] = dmoe_ref[...]
    pack_ref[:, width : width + experts] = jnp.where(chosen, high.astype(f32), -1.0).astype(bf16)
    pack_ref[:, width + experts :] = (probs - high.astype(f32)).astype(bf16)
    share = share_refs[0].shape[1] // 2
    chip, core = meta_ref[0], meta_ref[1]
    for k, ref in enumerate(share_refs):
        to = jnp.bitwise_xor(chip, k) * 2
        for i in range(2):
            at = pl.multiple_of((to + jnp.bitwise_xor(core, i)) * share, 128)
            ref[:, i * share : (i + 1) * share] = moe_ref[:, pl.ds(at, share)]


def gates(meta, moe_in, router, ids, d_moe, chips):
    tok, width = moe_in.shape
    experts = router.shape[1]
    vm = pl.BlockSpec(memory_space=pltpu.VMEM)
    return pl.pallas_call(
        gates_kernel,
        in_specs=[pl.BlockSpec(memory_space=pltpu.SMEM)] + [vm] * 4,
        out_shape=[jax.ShapeDtypeStruct((tok, width + 2 * experts), bf16)]
        + [jax.ShapeDtypeStruct((tok, width // chips), bf16)] * chips,
        compiler_params=pltpu.CompilerParams(vmem_limit_bytes=8 * mib),
        cost_estimate=takes(1),
        name="gates",
    )(meta, moe_in, router, ids, d_moe)


def attend_kernel(blocks, meta_ref, q_ref, o_ref, do_ref, gain_ref, *refs):
    kv_refs = refs[:2]
    dq_ref = refs[-5]
    part_refs = refs[-4:]
    tok = q_ref.shape[0]
    hd = gain_ref.shape[1]
    heads = q_ref.shape[1] // hd
    kb = 2 * kv_refs[0].shape[0] // blocks
    keys = kb * blocks
    scale = hd ** (-0.5)
    offset = meta_ref[0]
    gain = gain_ref[...]
    key = jnp.concatenate([r[:, :hd] for r in kv_refs], axis=0)
    val = jnp.concatenate([r[:, hd:] for r in kv_refs], axis=0)
    pos = jnp.concatenate(
        [
            meta_ref[1 + b] * kb + lax.broadcasted_iota(jnp.int32, (kb, 1), 0)
            for b in range(blocks)
        ],
        axis=0,
    )
    step_heads = min(heads, max(128 // tok, heads * 1024 // keys))
    rows = step_heads * tok
    limit = offset + lax.rem(lax.broadcasted_iota(jnp.int32, (1, rows), 1), tok)
    visible = pos <= limit
    dk = dv = None
    for h0 in range(0, heads, step_heads):

        def stack(ref):
            return jnp.concatenate(
                [ref[:, h * hd : (h + 1) * hd] for h in range(h0, h0 + step_heads)], axis=0
            )

        q = stack(q_ref).astype(f32)
        do = stack(do_ref)
        prod = do.astype(f32) * stack(o_ref).astype(f32)
        delta = jnp.sum(prod.T, axis=0, keepdims=True)
        inv = lax.rsqrt(jnp.mean(q * q, axis=-1, keepdims=True) + norm_eps)
        unit = q * inv
        q_hat = (unit * gain).astype(bf16)
        scores = dot_nt(key, q_hat)
        ex = jnp.where(visible, jnp.exp2(scores * (scale * math.log2(math.e))), 0.0)
        probs = ex * (1.0 / jnp.sum(ex, axis=0, keepdims=True))
        dv_one = dot_nn(probs.astype(bf16), do)
        dprobs = dot_nt(val, do)
        ds = ((probs * scale) * (dprobs - delta)).astype(bf16)
        dk_one = dot_nn(ds, q_hat)
        dq = dot_tn(key, ds).T
        c = dq * gain
        dq_pre = (inv * (c - unit * jnp.mean(c * unit, axis=-1, keepdims=True))).astype(bf16)
        for i in range(step_heads):
            h = h0 + i
            dq_ref[:, h * hd : (h + 1) * hd] = dq_pre[i * tok : (i + 1) * tok, :]
        dk = dk_one if dk is None else dk + dk_one
        dv = dv_one if dv is None else dv + dv_one
    at = 0
    for ref in part_refs:
        size = ref.shape[0]
        ref[:, :hd] = dk[at : at + size, :].astype(ref.dtype)
        ref[:, hd:] = dv[at : at + size, :].astype(ref.dtype)
        at += size


def attend(meta, q, o, do, gain, kv_halves, blocks, kv_heads):
    tok, width = q.shape
    hd = gain.shape[1]
    half, kv_width = kv_halves[0].shape
    step = width // kv_heads
    row_spec = pl.BlockSpec((tok, step), lambda g, m: (0, g))
    part_spec = pl.BlockSpec((half, 2 * hd), lambda g, m: (0, g))
    own = 2 * half // blocks
    sizes = (own, half - own) * 2
    return pl.pallas_call(
        functools.partial(attend_kernel, blocks),
        grid_spec=pltpu.PrefetchScalarGridSpec(
            num_scalar_prefetch=1,
            grid=(kv_width // (2 * hd),),
            in_specs=[row_spec] * 3
            + [whole((1, hd))]
            + [part_spec] * 2,
            out_specs=[row_spec] + [pl.BlockSpec((n, 2 * hd), lambda g, m: (0, g)) for n in sizes],
        ),
        out_shape=[
            jax.ShapeDtypeStruct((tok, width), bf16),
            jax.ShapeDtypeStruct((sizes[0], kv_width), f32),
            jax.ShapeDtypeStruct((sizes[1], kv_width), f32),
            jax.ShapeDtypeStruct((sizes[2], kv_width), bf16),
            jax.ShapeDtypeStruct((sizes[3], kv_width), bf16),
        ],
        compiler_params=pltpu.CompilerParams(vmem_limit_bytes=32 * mib),
        cost_estimate=takes(10),
        name="attend",
    )(meta, q, o, do, gain, *kv_halves)


def pair_kernel(keep_ref, other_ref, *out_refs):
    rows, cut = out_refs[0].shape
    blocks = len(out_refs) // 2
    for k in range(blocks):
        at = k * rows
        total = keep_ref[at : at + rows, :] + other_ref[at : at + rows, :].astype(f32)
        out_refs[k][...] = total[:, :cut].astype(bf16)
        out_refs[blocks + k][...] = total[:, cut:].astype(bf16)


def pair_sums(keep, other, rows, kv_heads):
    blocks = keep.shape[0] // rows
    width = keep.shape[1]
    cut = (kv_heads // 2) * (width // kv_heads)
    sums = pl.pallas_call(
        pair_kernel,
        out_shape=[jax.ShapeDtypeStruct((rows, cut), bf16)] * blocks
        + [jax.ShapeDtypeStruct((rows, width - cut), bf16)] * blocks,
        compiler_params=pltpu.CompilerParams(vmem_limit_bytes=32 * mib),
        cost_estimate=takes(1),
        name="pair_sums",
    )(keep, other)
    return sums[:blocks], sums[blocks:]


def finish_kernel(parts, k_ref, gain_ref, own_ref, other_ref, *refs):
    dk_ref, dv_ref = refs[-2:]
    hd = gain_ref.shape[1]
    gain = gain_ref[...]
    total = own_ref[...] + other_ref[...].astype(f32)
    for r in refs[:parts]:
        total = total + r[...].astype(f32)
    for g in range(k_ref.shape[1] // hd):
        k = k_ref[:, g * hd : (g + 1) * hd].astype(f32)
        inv = lax.rsqrt(jnp.mean(k * k, axis=-1, keepdims=True) + norm_eps)
        unit = k * inv
        c = total[:, 2 * g * hd : (2 * g + 1) * hd] * gain
        dk = inv * (c - unit * jnp.mean(c * unit, axis=-1, keepdims=True))
        dk_ref[:, g * hd : (g + 1) * hd] = dk.astype(bf16)
        dv_ref[:, g * hd : (g + 1) * hd] = total[
            :, (2 * g + 1) * hd : (2 * g + 2) * hd
        ].astype(bf16)


def finish_keys(k_pre, k_gain, own, parts, half, filled):
    rows, width = k_pre.shape
    narrow = pl.BlockSpec((rows, width // 2), lambda i: (0, half))
    wide = pl.BlockSpec((rows, width), lambda i: (0, half))
    out = jax.ShapeDtypeStruct(k_pre.shape, bf16)
    before = 4 + len(parts)
    return pl.pallas_call(
        functools.partial(finish_kernel, len(parts)),
        grid=(1,),
        in_specs=[narrow, whole(k_gain.shape), wide, wide]
        + [whole(p.shape) for p in parts]
        + [pl.BlockSpec(memory_space=pl.ANY)] * len(filled),
        out_specs=[narrow, narrow],
        out_shape=[out, out],
        input_output_aliases={before + i: i for i in range(len(filled))},
        compiler_params=pltpu.CompilerParams(vmem_limit_bytes=8 * mib),
        cost_estimate=takes(1.2),
        name="finish_keys",
    )(k_pre, k_gain, *own, *parts, *filled)


def earlier_same_block(rows, block):
    i = lax.broadcasted_iota(jnp.int32, (rows, rows), 0)
    j = lax.broadcasted_iota(jnp.int32, (rows, rows), 1)
    same = lax.div(i, block) == lax.div(j, block)
    return jnp.where(jnp.logical_and(same, j < i), 1.0, 0.0).astype(bf16)


def terms_kernel(blocks, sp, cap, meta_ref, table_ref, lanes_ref, *refs):
    d_refs = refs[:2]
    g_refs = refs[2:4]
    eout_ref, gated_ref, terms_ref, dm, hit_scr, acc = refs[4:]
    half = d_refs[0].shape[0]
    tokens = 2 * half
    tok = tokens // blocks
    experts = g_refs[0].shape[1]
    rows = eout_ref.shape[0]
    step = pl.program_id(0)

    def pick():
        expert = meta_ref[0] + table_ref[:, 0:1]
        return lax.broadcasted_iota(jnp.int32, (rows, experts), 1) == expert

    @pl.when(step == 0)
    def _():
        coded = jnp.concatenate([r[...] for r in g_refs], axis=0)
        chosen = (coded >= 0).astype(bf16)
        rank = dot_nn(earlier_same_block(tokens, tok), chosen)
        sel = jnp.where(pick(), 1.0, 0.0).astype(bf16)
        gate = dot_nt(sel, coded)
        place = dot_nt(sel, rank.astype(bf16))
        lane_block = lax.div(lax.broadcasted_iota(jnp.int32, (1, tokens), 1), tok)
        source = jnp.zeros((1, tokens), jnp.int32)
        for b in range(blocks):
            source = jnp.where(lane_block == b, meta_ref[1 + b], source)
        hit = jnp.logical_and(
            jnp.logical_and(gate >= 0.0, place == table_ref[:, 1:2].astype(f32)),
            source == table_ref[:, 2:3],
        )
        gated_ref[...] = jnp.where(hit, gate, 0.0).astype(bf16)
        hit_scr[...] = jnp.where(hit, 1.0, 0.0)
        acc[...] = jnp.zeros_like(acc)

    for i in range(2):
        dm[i * half : (i + 1) * half, :] = d_refs[i][...]
    acc[...] += dot_nt(eout_ref[...], dm[...])

    @pl.when(step == pl.num_programs(0) - 1)
    def _():
        terms = jnp.sum(acc[...] * hit_scr[...], axis=-1, keepdims=True)
        placed = jnp.where(pick(), terms, 0.0)
        want = lax.broadcasted_iota(jnp.int32, (cap * sp, rows), 0)
        fold = jnp.where(want == lanes_ref[...], 1.0, 0.0)
        folded = lax.dot_general(
            fold,
            placed,
            (((1,), (0,)), ((), ())),
            precision=lax.Precision.HIGHEST,
            preferred_element_type=f32,
        )
        for to in range(terms_ref.shape[0]):
            terms_ref[to] = folded


def slot_terms(meta, packs, eout, experts, cap, sp):
    rows, width = eout.shape
    half, packed = packs[0].shape
    blocks = sp
    r = np.arange(rows)
    e, c, s = r // (cap * sp), (r // sp) % cap, r % sp
    table = jnp.asarray(np.stack([e, c, s], axis=1), jnp.int32)
    lanes = jnp.asarray((c * sp + s)[None, :], jnp.int32)
    col = min(width, 2048)
    tokens = 2 * half
    gate_at = (packed - 2 * experts) // experts
    d_spec = pl.BlockSpec((half, col), lambda i, m: (0, i))
    g_spec = pl.BlockSpec((half, experts), lambda i, m: (0, gate_at))
    e_spec = pl.BlockSpec((rows, col), lambda i, m: (0, i))
    return pl.pallas_call(
        functools.partial(terms_kernel, blocks, sp, cap),
        grid_spec=pltpu.PrefetchScalarGridSpec(
            num_scalar_prefetch=1,
            grid=(width // col,),
            in_specs=[whole((rows, 3)), whole((1, rows))]
            + [d_spec] * 2
            + [g_spec] * 2
            + [e_spec],
            out_specs=[whole((rows, tokens)), whole((sp, cap * sp, experts))],
            scratch_shapes=[
                pltpu.VMEM((tokens, col), bf16),
                pltpu.VMEM((rows, tokens), f32),
                pltpu.VMEM((rows, tokens), f32),
            ],
        ),
        out_shape=[
            jax.ShapeDtypeStruct((rows, tokens), bf16),
            jax.ShapeDtypeStruct((sp, cap * sp, experts), f32),
        ],
        compiler_params=pltpu.CompilerParams(vmem_limit_bytes=24 * mib),
        cost_estimate=takes(6.2),
        name="slot_terms",
    )(meta, table, lanes, *packs, *packs, eout)


def batch_kernel(gated_ref, *refs):
    batch_ref, dm = refs[-2:]
    tok = refs[0].shape[0]
    for b, r in enumerate(refs[:-2]):
        dm[b * tok : (b + 1) * tok, :] = r[...]
    batch_ref[...] = dot_nn(gated_ref[...], dm[...]).astype(bf16)


def batch_grad(gated, packs, width):
    rows, tokens = gated.shape
    tok = packs[0].shape[0]
    col = min(width, 2048)
    return pl.pallas_call(
        batch_kernel,
        grid=(width // col,),
        in_specs=[whole((rows, tokens))]
        + [pl.BlockSpec((tok, col), lambda i: (0, i))] * len(packs),
        out_specs=pl.BlockSpec((rows, col), lambda i: (0, i)),
        out_shape=jax.ShapeDtypeStruct((rows, width), bf16),
        scratch_shapes=[pltpu.VMEM((tokens, col), bf16)],
        compiler_params=pltpu.CompilerParams(vmem_limit_bytes=16 * mib),
        cost_estimate=takes(4.6),
        name="batch_grad",
    )(gated, *packs)


def router_kernel(sp, cap, meta_ref, *refs):
    info_refs, moe_refs = refs[:2], refs[2:4]
    terms_in, out_ref, terms_ref = refs[4:]
    terms_ref[...] = jnp.sum(terms_in[...], axis=0)
    share, experts = out_ref.shape
    tok = 2 * info_refs[0].shape[0] // sp
    info = jnp.concatenate([r[...] for r in info_refs], axis=0)
    moe = jnp.concatenate([r[...] for r in moe_refs], axis=0)
    high = info[:, :experts]
    chosen = high >= 0
    prob = jnp.where(chosen, high.astype(f32) + info[:, experts:].astype(f32), 0.0)
    rank = dot_nn(earlier_same_block(tok * sp, tok), chosen.astype(bf16))
    pieces = []
    for b in range(sp):
        place = rank[b * tok : (b + 1) * tok, :]
        one = jnp.zeros((tok, experts), f32)
        for c in range(cap):
            row = terms_ref[pl.ds(c * sp + meta_ref[1 + b], 1), :]
            one = jnp.where(place == c, row, one)
        pieces.append(one)
    dgate = jnp.where(chosen, jnp.concatenate(pieces, axis=0), 0.0)
    dlogit = prob * (dgate - jnp.sum(prob * dgate, axis=-1, keepdims=True))
    a = dlogit.astype(bf16)
    rest = dlogit - a.astype(f32)
    b = rest.astype(bf16)
    c = (rest - b.astype(f32)).astype(bf16)
    wide = dot_tn(moe, jnp.concatenate([a, b, c], axis=1))
    total = wide[:, :experts] + wide[:, experts : 2 * experts] + wide[:, 2 * experts :]
    out_ref[...] = total.astype(bf16)


def router_grad(meta, packs, moe, terms, width, experts, cap, sp):
    half, packed = packs[0].shape
    share = width // sp
    info_at = packed // (2 * experts) - 1
    info_spec = pl.BlockSpec((half, 2 * experts), lambda i, m: (0, info_at))
    moe_specs = [whole((half, share))] * 2
    return pl.pallas_call(
        functools.partial(router_kernel, sp, cap),
        grid_spec=pltpu.PrefetchScalarGridSpec(
            num_scalar_prefetch=1,
            grid=(1,),
            in_specs=[info_spec] * 2 + moe_specs + [whole(terms.shape)],
            out_specs=whole((share, experts)),
            scratch_shapes=[pltpu.VMEM((cap * sp, experts), f32)],
        ),
        out_shape=jax.ShapeDtypeStruct((share, experts), bf16),
        compiler_params=pltpu.CompilerParams(vmem_limit_bytes=16 * mib),
        cost_estimate=takes(3),
        name="router_grad",
    )(meta, *packs, *moe, terms)


def flipped(x, axis, size, k):
    return lax.ppermute(x, axis, [(i, i ^ k) for i in range(size)])


def sent_over(axis, size, x):
    if size & (size - 1):
        return [lax.psum(x.astype(f32), axis)]
    return [x] + [flipped(x, axis, size, k) for k in range(1, size)]


def tree_sum(terms):
    terms = [x.astype(f32) for x in terms]
    while len(terms) > 1:
        terms = [a + b for a, b in zip(terms[0::2], terms[1::2])]
    return terms[0]


def together(*arrays):
    return lax.optimization_barrier(arrays)


def on_device(
    q_pre,
    attn_out,
    d_attn,
    k_pre,
    values,
    q_gain,
    k_gain,
    offsets,
    moe_in,
    router,
    expert_ids,
    d_moe,
    expert_out,
):
    dp = lax.axis_size("dp")
    sp = lax.axis_size("sp")
    me = lax.axis_index("sp").astype(jnp.int32)
    other = jnp.bitwise_xor(me, 1)
    chips = sp // 2
    swap = [(i, i ^ 1) for i in range(sp)]

    def exchange(x):
        return lax.ppermute(x, "sp", swap)

    def to_chip(x, k):
        return flipped(x, "sp", sp, 2 * k)

    def both(mine):
        mine = jnp.concatenate(mine, axis=0)
        return [mine, exchange(mine)]

    steps = 2 * jnp.arange(chips, dtype=jnp.int32)
    owners = jnp.concatenate([jnp.bitwise_xor(me, steps), jnp.bitwise_xor(other, steps)])
    qg, kg = q_gain[None, :], k_gain[None, :]
    kv_heads = k_pre.shape[2] // q_gain.shape[0]
    width = moe_in.shape[2]
    experts = router.shape[1]
    place = jnp.stack([me // 2, jnp.bitwise_and(me, 1)])

    experts_here, _, cap, _ = expert_out.shape[1:]
    eout = jnp.transpose(expert_out[0], (0, 2, 1, 3)).reshape(experts_here * cap * sp, width)
    slot_meta = jnp.concatenate([(me * experts_here)[None], owners])
    meta = jnp.concatenate([offsets + me * q_pre.shape[1], owners])

    kv = pack_keys(k_pre[0], values[0], kg)
    if chips == 4:
        far = to_chip(kv, 2)
        kv = [kv, to_chip(kv, 1), far, to_chip(far, 1)]
    else:
        kv = [kv] + [to_chip(kv, k) for k in range(1, chips)]
    pack, *shares = gates(place, moe_in[0], router, expert_ids[0], d_moe[0], chips)
    shares = [shares[0]] + [to_chip(shares[k], k) for k in range(1, chips)]
    kv, pack, shares = together(kv, pack, shares)

    packs = [pack] + [to_chip(pack, k) for k in range(1, chips)]
    share = width // sp
    mine = jnp.concatenate([x[:, :share] for x in shares], axis=0)
    theirs = exchange(jnp.concatenate([x[:, share:] for x in shares], axis=0))
    dq, own, keep, own_send, send = attend(
        meta, q_pre[0], attn_out[0], d_attn[0], qg, both(kv), sp, kv_heads
    )
    packs, mine, theirs, own, keep, own_send, send = together(
        packs, mine, theirs, own, keep, own_send, send
    )

    rows = k_pre.shape[1]
    arrived = exchange(send)
    first, rest = pair_sums(keep, arrived, rows, kv_heads)
    packs, first, rest, own_send = together(packs, first, rest, own_send)

    own_arrived = exchange(own_send)
    first = [to_chip(first[k - 1], k) for k in range(1, chips)]
    packs = both(packs)
    gated, terms = slot_terms(slot_meta, packs, eout, experts, cap, sp)
    terms = lax.all_to_all(terms, "sp", split_axis=0, concat_axis=0, tiled=True)
    batch = batch_grad(gated, packs, width)
    own_arrived, first, rest, batch = together(own_arrived, first, rest, batch)

    rest = [to_chip(rest[k - 1], k) for k in range(1, chips)]
    routed = router_grad(slot_meta, packs, (mine, theirs), terms, width, experts, cap, sp)
    routed = sent_over("dp", dp, routed)
    filled = finish_keys(k_pre[0], kg, [own, own_arrived], first, 0, [])
    dk, dv = finish_keys(k_pre[0], kg, [own, own_arrived], rest, 1, filled)
    batch = jnp.transpose(batch.reshape(experts_here, cap, sp, width), (0, 2, 1, 3))
    return (dq[None], dk[None], dv[None], batch[None], tree_sum(routed))


def solution(mesh):
    in_specs = (
        P("dp", "sp", None),
        P("dp", "sp", None),
        P("dp", "sp", None),
        P("dp", "sp", None),
        P("dp", "sp", None),
        P(),
        P(),
        P("dp"),
        P("dp", "sp", None),
        P(),
        P("dp", "sp", None),
        P("dp", "sp", None),
        P("dp", "sp", None, None, None),
    )
    out_specs = (
        P("dp", "sp", None),
        P("dp", "sp", None),
        P("dp", "sp", None),
        P("dp", "sp", None, None, None),
        P("sp", None),
    )
    return jax.shard_map(
        on_device, mesh=mesh, in_specs=in_specs, out_specs=out_specs, check_vma=False
    )
```
